32 devices in a mesh: cls: 8 (over z, y), dp: 4 (over x, core).
Axes of the slice: x: 2, y: 2, z: 4, core: 2. Of those that a mesh axis runs over, the one named last changes fastest.
Arguments:
- images: bfloat16 [4096, 4096], P(('cls', 'dp')), may hold values from -6 to 6
- defocus: bfloat16 [4096], P(('cls', 'dp')), may hold values from 0.5 to 2
- classes: int32 [4096, 1], P(('cls', 'dp')), may hold values from 0 to 7; in each aligned block of 128 rows (0 to 127, 128 to 255, ...) at most 32 rows name the same one
- rotations: int32 [4096], P(('cls', 'dp')), may hold values from 0 to 63
- references: bfloat16 [8, 64, 4096], P('cls'), may hold values from -6 to 6
Outputs:
- refined: bfloat16 [8, 64, 4096], P('cls', 'dp')
- misfit: float32 [4096], P(('cls', 'dp'))
The draws below stay inside these ranges and needn't reach their ends.
Inputs may be any that keep to these rules, and one draw needn't show every extreme that they name: `classes`: among the rows of one device no class is named by more than 32 particles, and in every draw some device has exactly 32 particles of one class.
All inputs are finite; a program needn't handle non-finite values.
Results may differ from the reference program's by a relative error of at most 0.008.
Values may be sent and summed in bfloat16 or wider, within the bound.
A program may use at most 64 MiB of HBM per device.

```python
import math
import jax
import jax.numpy as jnp
import numpy as np
from jax import lax

SIDE = 64
ROT = 64
PART_DEV = 128
CAP = 32
CLASSES = 8
PARTICLES = 4096
N_CLS = 8
N_DP = 4


def place_ends(values, own_key, low, top_value):
    shape = values.shape
    place = [jax.random.randint(jax.random.fold_in(own_key, axis), (), 0, shape[axis]) for axis in range(len(shape))]
    values = values.at[tuple(place)].set(low)
    longest = shape.index(max(shape))
    place[longest] = (place[longest] + 1) % shape[longest]
    return values.at[tuple(place)].set(top_value)


def levels(rng, extent, pieces, smallest, largest):
    factor_of = 1.0
    for dim, shards_of in pieces:
        draws = jax.random.uniform(jax.random.fold_in(jax.random.fold_in(rng, 6), dim), (shards_of,), jnp.float32, smallest / len(pieces), largest / len(pieces))
        factor_of = factor_of * jnp.repeat(jnp.exp(draws), extent[dim] // shards_of).reshape((-1,) + (1,) * (len(extent) - 1 - dim))
    return factor_of


def assign_block(own_key, own, number, rows, amount, top, most, slope):
    sequence = jax.random.permutation(own_key, amount)
    crowded, usual = portions_of(amount, rows * top, most, slope, True), portions_of(amount, rows * top, most, slope, False)
    places = jnp.arange(amount)

    def named(tallies, rotation):
        used = int((tallies > 0).sum())
        fixed = max(1, used // 4)
        moved = fixed + (places - fixed + rotation * (used - fixed)) % max(1, amount - fixed)
        return jnp.zeros((amount,), jnp.int32).at[sequence[jnp.where(places < fixed, places, moved)]].set(jnp.asarray(tallies, jnp.int32))

    tallies = jnp.where(number % 4 == 0, named(crowded, number // 4), named(usual, number - number // 4 - 1))
    mixed = jax.random.permutation(jax.random.fold_in(own, 3), amount)
    source_of, sink = mixed[0:amount // 2 * 2:2], mixed[1:amount // 2 * 2:2]
    slack = jnp.minimum(tallies[source_of] - 1, most - tallies[sink]) // 2
    slack = jnp.where((source_of == sequence[0]) | (sink == sequence[0]) | (tallies[sink] == 0), 0, jnp.maximum(slack, 0))
    moved = jax.random.randint(jax.random.fold_in(own, 4), (amount // 2,), 0, 1 << 20) % (slack + 1)
    tallies = tallies.at[source_of].add(-moved).at[sink].add(moved)
    items = jnp.searchsorted(jnp.cumsum(tallies), jnp.arange(rows * top), side="right").astype(jnp.int32)
    listing = items.reshape(top, rows).T
    listing = listing[jax.random.permutation(jax.random.fold_in(own, 1), rows)]
    rotation = jax.random.randint(jax.random.fold_in(own, 2), (rows, 1), 0, top)
    return jnp.take_along_axis(listing, (jnp.arange(top)[None, :] + rotation) % top, axis=1)


def portions_of(count, total, bound, skew, full):
    loads = [(1 << 20) // math.isqrt(rank ** skew) + 1 for rank in range(1, count + 1)]
    largest = bound if full else min(bound, max(-(-total // count), total * loads[0] // sum(loads)))
    least = 1 if total - largest >= count - 1 else 0
    given, spare = [largest] + [least] * (count - 1), total - largest - least * (count - 1)
    while spare > 0:
        candidates = [i for i in range(1, count) if given[i] < largest] or [i for i in range(1, count) if given[i] < bound]
        mass, remaining = sum([loads[i] for i in candidates]), spare
        for i in candidates:
            extra = min(bound - given[i], max(1, remaining * loads[i] // mass), spare)
            given[i] = given[i] + extra
            spare = spare - extra
    return np.array(given)


def scatter_about(stream_key, shape, deviation, bound, cuts=(), kind=jnp.bfloat16):
    result = jax.random.normal(stream_key, shape, jnp.float32) * deviation
    if len(cuts) > 0:
        result = levels(stream_key, shape, cuts, -0.22, 0.18) * result
    return jnp.clip(result, min=-bound, max=bound).astype(kind)


def setup_inputs(seed: int = 0) -> dict:
    streams_of = jax.random.split(jax.random.key(seed), 6)
    images = scatter_about(streams_of[0], (PARTICLES, SIDE * SIDE), 1.0, 6.0, ((0, 32),))
    defocus = jnp.clip(jnp.exp(math.log(2.0) - 1.3862944 * jax.random.uniform(streams_of[1], (PARTICLES,), jnp.float32) ** levels(streams_of[1], (PARTICLES,), ((0, 32),), -0.2, 0.2)), 0.5, 2.0).astype(jnp.bfloat16)
    classes_keys = jax.random.split(jax.random.fold_in(streams_of[2], 1), PARTICLES // PART_DEV)
    classes_turns = jax.random.permutation(jax.random.fold_in(streams_of[2], 3), PARTICLES // PART_DEV)
    classes = jax.vmap(lambda own, number: assign_block(jax.random.fold_in(streams_of[2], 2), own, number, PART_DEV, CLASSES, 1, CAP, 2))(classes_keys, classes_turns).reshape((PARTICLES, 1))
    rotations = place_ends(jax.random.randint(streams_of[3], (PARTICLES,), 0, ROT), jax.random.fold_in(streams_of[3], 1), 0, ROT - 1).astype(jnp.int32)
    references = scatter_about(streams_of[4], (CLASSES, ROT, SIDE * SIDE), 1.0, 6.0, ((0, 8),))
    return {"images": images, "defocus": defocus, "classes": classes, "rotations": rotations, "references": references}


def wave_table(side_count):
    pixel_index = jnp.arange(side_count * side_count, dtype=jnp.int32)
    half_side = side_count // 2
    row_freq = (pixel_index // side_count + half_side) % side_count - half_side
    col_freq = (pixel_index % side_count + half_side) % side_count - half_side
    return (row_freq * row_freq + col_freq * col_freq).astype(jnp.float32) / float(half_side * half_side)


def contrast(defocus_rows, radius):
    phase = 20.0 * defocus_rows.astype(jnp.float32)[:, None] * radius[None, :] + 0.1
    return -jnp.sin(phase) * jnp.exp(-0.5 * radius)[None, :]


def group_gradient(table, image_rows, flat_rows, defocus_rows, radius):
    tiles = table[flat_rows].astype(jnp.float32)
    contrast_rows = contrast(defocus_rows, radius)
    residual = contrast_rows * tiles - image_rows.astype(jnp.float32)
    misfit_rows = jnp.mean(residual * residual, axis=1)
    weighted = lax.optimization_barrier((contrast_rows * residual).astype(jnp.bfloat16))
    gradient = jnp.zeros(table.shape, jnp.float32).at[flat_rows].add(weighted.astype(jnp.float32))
    rounded = lax.optimization_barrier(gradient.astype(jnp.bfloat16))
    return rounded.astype(jnp.float32), misfit_rows


def refine_step(table, damping, image_groups, flat_groups, defocus_groups, radius):
    gradient = jnp.zeros(table.shape, jnp.float32)
    misfit_list = []
    for group in range(N_DP):
        group_grad, misfit_rows = group_gradient(table, image_groups[:, group].reshape(N_CLS * PART_DEV, SIDE * SIDE), flat_groups[:, group].reshape(N_CLS * PART_DEV), defocus_groups[:, group].reshape(N_CLS * PART_DEV), radius)
        gradient = gradient + group_grad
        misfit_list.append(misfit_rows.reshape(N_CLS, PART_DEV))
    fresh = (table.astype(jnp.float32) - gradient / damping[:, None]).astype(jnp.bfloat16)
    return fresh, jnp.stack(misfit_list, axis=1)


def reference(images, defocus, classes, rotations, references):
    radius = wave_table(SIDE)
    pixel_count = SIDE * SIDE
    table = references.reshape(CLASSES * ROT, pixel_count)
    flat_index = (classes[:, 0] * ROT + rotations).astype(jnp.int32)
    counts = jnp.zeros((CLASSES * ROT,), jnp.float32).at[flat_index].add(jnp.ones((PARTICLES,), jnp.float32))
    damping = 0.5 * counts + 1.0
    image_groups = images.reshape(N_CLS, N_DP, PART_DEV, pixel_count)
    flat_groups = flat_index.reshape(N_CLS, N_DP, PART_DEV)
    defocus_groups = defocus.reshape(N_CLS, N_DP, PART_DEV)
    table_first, unused_misfit = refine_step(table, damping, image_groups, flat_groups, defocus_groups, radius)
    table_second, misfit_grid = refine_step(table_first, damping, image_groups, flat_groups, defocus_groups, radius)
    return table_second.reshape(CLASSES, ROT, pixel_count), misfit_grid.reshape(PARTICLES)
```

```python
import functools
import jax
import jax.numpy as jnp
import numpy as np
from jax import lax
from jax.experimental import pallas as pl
from jax.experimental.pallas import tpu as pltpu
from jax.sharding import PartitionSpec as P

SIDE = 64
MESH = pl.DeviceIdType.MESH
CHUNKS = 8
LANES = 128


def wave_table(side_count):
    pixel_index = jnp.arange(side_count * side_count, dtype=jnp.int32)
    half_side = side_count // 2
    row_freq = (pixel_index // side_count + half_side) % side_count - half_side
    col_freq = (pixel_index % side_count + half_side) % side_count - half_side
    return (row_freq * row_freq + col_freq * col_freq).astype(jnp.float32) / float(
        half_side * half_side
    )


def contrast(defocus_rows, radius):
    phase = 20.0 * defocus_rows.astype(jnp.float32)[:, None] * radius[None, :] + 0.1
    return -jnp.sin(phase) * jnp.exp(-0.5 * radius)[None, :]


def sweep_rows(table, image_rows, rotation_rows, defocus_rows, radius):
    row_total = image_rows.shape[0]
    block_rows = min(64, row_total)
    block_count = row_total // block_rows
    rotation_count = table.shape[0]
    labels = jnp.arange(rotation_count, dtype=jnp.int32)

    def advance(gradient, block_index):
        row_start = block_index * block_rows
        image_block = lax.dynamic_slice_in_dim(image_rows, row_start, block_rows, 0)
        rotation_block = lax.dynamic_slice_in_dim(rotation_rows, row_start, block_rows, 0)
        defocus_block = lax.dynamic_slice_in_dim(defocus_rows, row_start, block_rows, 0)
        selector = (rotation_block[:, None] == labels[None, :]).astype(jnp.bfloat16)
        tiles = jnp.dot(selector, table, preferred_element_type=jnp.float32)
        contrast_rows = contrast(defocus_block, radius)
        residual = contrast_rows * tiles - image_block.astype(jnp.float32)
        misfit_rows = jnp.mean(residual * residual, axis=1)
        weighted = (contrast_rows * residual).astype(jnp.bfloat16)
        gradient = gradient + lax.dot_general(
            selector, weighted, (((0,), (0,)), ((), ())), preferred_element_type=jnp.float32
        )
        return (gradient, misfit_rows)

    start_grad = jnp.zeros((rotation_count, image_rows.shape[1]), jnp.float32)
    gradient, misfit_blocks = lax.scan(
        advance, start_grad, jnp.arange(block_count, dtype=jnp.int32)
    )
    return (gradient, misfit_blocks.reshape(row_total))


def build_slots(
    images, defocus, rotations, class_rows, class_rank, rank_first, slot_width, count_cls
):
    particle_ids = jnp.arange(images.shape[0], dtype=jnp.int32)
    inside = (class_rank >= rank_first) & (class_rank < rank_first + slot_width)
    slot_of = jnp.where(inside, class_rows * slot_width + class_rank - rank_first, -1)
    slot_ids = jnp.arange(count_cls * slot_width, dtype=jnp.int32)
    slot_match = slot_ids[:, None] == slot_of[None, :]
    slot_live = jnp.any(slot_match, axis=1)
    slot_source = jnp.sum(jnp.where(slot_match, particle_ids[None, :], 0), axis=1)
    send_images = jnp.where(
        slot_live[:, None], jnp.take(images, slot_source, axis=0), jnp.zeros((), jnp.bfloat16)
    )
    send_rotation = jnp.where(slot_live, jnp.take(rotations, slot_source), -1)
    send_defocus = jnp.where(
        slot_live, jnp.take(defocus, slot_source).astype(jnp.float32), 0.0
    ).astype(jnp.bfloat16)
    return (send_images, send_rotation, send_defocus)


def shards(images, defocus, classes, rotations, references):
    count_cls = lax.axis_size("cls")
    count_dp = lax.axis_size("dp")
    particle_count = images.shape[0]
    pixel_count = images.shape[1]
    rotation_count = references.shape[1]
    capacity = max(2, 2 * particle_count // count_cls)
    slot_count = count_cls * capacity
    radius = wave_table(SIDE)
    class_rows = classes[:, 0]
    particle_ids = jnp.arange(particle_count, dtype=jnp.int32)
    earlier_same = (class_rows[:, None] == class_rows[None, :]) & (
        particle_ids[None, :] < particle_ids[:, None]
    )
    class_rank = jnp.sum(earlier_same.astype(jnp.int32), axis=1)
    slot_of = class_rows * capacity + class_rank
    slot_ids = jnp.arange(slot_count, dtype=jnp.int32)
    slot_match = slot_ids[:, None] == slot_of[None, :]
    send_images, send_rotation, send_defocus = build_slots(
        images, defocus, rotations, class_rows, class_rank, 0, capacity, count_cls
    )
    recv_images, recv_rotation, recv_defocus = (
        lax.all_to_all(
            send_images.reshape(count_cls, capacity, pixel_count),
            "cls",
            split_axis=0,
            concat_axis=0,
            tiled=True,
        ),
        lax.all_to_all(
            send_rotation.astype(jnp.bfloat16).reshape(count_cls, capacity),
            "cls",
            split_axis=0,
            concat_axis=0,
            tiled=True,
        ),
        lax.all_to_all(
            send_defocus.reshape(count_cls, capacity),
            "cls",
            split_axis=0,
            concat_axis=0,
            tiled=True,
        ),
    )
    image_slots = recv_images.reshape(slot_count, pixel_count)
    rotation_slots = recv_rotation.reshape(slot_count).astype(jnp.int32)
    defocus_slots = recv_defocus.reshape(slot_count)
    labels = jnp.arange(rotation_count, dtype=jnp.int32)
    local_counts = jnp.sum((rotation_slots[:, None] == labels[None, :]).astype(jnp.float32), axis=0)
    counts = lax.psum(local_counts, "dp")
    damping = 0.5 * counts + 1.0
    table = references[0]
    grad_first, unused_first = sweep_rows(table, image_slots, rotation_slots, defocus_slots, radius)
    share_rows = rotation_count // count_dp
    share_start = lax.axis_index("dp") * share_rows
    damping_share = lax.dynamic_slice_in_dim(damping, share_start, share_rows, 0)
    grad_share = lax.psum_scatter(
        grad_first.astype(jnp.bfloat16), "dp", scatter_dimension=0, tiled=True
    ).astype(jnp.float32)
    anchor = lax.dynamic_slice_in_dim(table, share_start, share_rows, 0).astype(jnp.float32)
    fresh_share = (anchor - grad_share / damping_share[:, None]).astype(jnp.bfloat16)
    table_next = lax.all_gather(fresh_share, "dp", axis=0, tiled=True)
    grad_second, misfit_slots = sweep_rows(
        table_next, image_slots, rotation_slots, defocus_slots, radius
    )
    second_share = lax.psum_scatter(
        grad_second.astype(jnp.bfloat16), "dp", scatter_dimension=0, tiled=True
    ).astype(jnp.float32)
    anchor_next = lax.dynamic_slice_in_dim(table_next, share_start, share_rows, 0).astype(
        jnp.float32
    )
    refined = (anchor_next - second_share / damping_share[:, None]).astype(jnp.bfloat16)
    returned = lax.all_to_all(
        misfit_slots.reshape(count_cls, capacity), "cls", split_axis=0, concat_axis=0, tiled=True
    )
    returned_slots = returned.reshape(slot_count)
    misfit = jnp.sum(jnp.where(slot_match, returned_slots[:, None], 0.0), axis=0)
    return (refined.reshape(1, share_rows, pixel_count), misfit)


def radius_tables(side_count):
    half_side = side_count // 2
    freq = (np.arange(side_count) + half_side) % side_count - half_side
    square = (freq[:, None] ** 2 + freq[None, :] ** 2).reshape(-1)
    values, place = np.unique(square, return_inverse=True)
    width = -(-(len(values) + 1) // LANES) * LANES
    rows = np.zeros((8, width), np.float32)
    rows[0, : len(values)] = values.astype(np.float32) / np.float32(half_side * half_side)
    rows[1, : len(values)] = -np.exp(-0.5 * rows[0, : len(values)])
    rows[2, width - 1] = 1.0
    return rows, place.reshape(1, -1).astype(np.float32)


def bounded_sine(angle):
    turns = jnp.floor(angle * np.float32(1.0 / np.pi) + 0.5)
    rest = angle - turns * np.float32(3.140625)
    rest = rest - turns * np.float32(9.67502593994140625e-4)
    rest = rest - turns * np.float32(1.509957990978376432e-7)
    odd = turns - 2.0 * jnp.floor(turns * 0.5)
    sign = 1.0 - 2.0 * odd
    square = rest * rest
    poly = np.float32(-2.3889859e-08)
    poly = poly * square + np.float32(2.7525562e-06)
    poly = poly * square + np.float32(-1.9840874e-04)
    poly = poly * square + np.float32(8.3333310e-03)
    poly = poly * square + np.float32(-1.6666667e-01)
    return sign * (rest + rest * square * poly)


def refine_kernel(
    sizes,
    images,
    meta,
    tables,
    place,
    references,
    refined,
    misfit,
    img,
    metas,
    crad,
    sq,
    con,
    pick,
    hot,
    hot_t,
    work,
    b_own,
    b_send,
    y_got,
    z_own,
    z_send,
    z_got,
    table,
    s_own,
    s_send,
    sy_got,
    sz_own,
    sz_send,
    sz_got,
    s_sum,
    anchor,
    acc,
    mis,
    mis_got,
    send,
    recv,
    send_small,
    recv_small,
    local,
):
    chunks, width, share, side_y, side_z = sizes
    cls = lax.axis_index("cls")
    dp = lax.axis_index("dp")
    z = cls // side_y
    y = cls % side_y
    radii = crad.shape[2]
    half = side_z * share
    cells = side_y * half

    core_mate = (cls, dp + 1 - 2 * (dp % 2))
    x_mate = (cls, (dp + 2) % 4)
    far_mate = (cls, (dp + 2) % 4 + 1 - 2 * (dp % 2))
    y_mate = (z * side_y + 1 - y, dp)
    z_mates = [(((z + k) % side_z) * side_y + y, dp) for k in range(1, side_z)]

    barrier = pltpu.get_barrier_semaphore()
    everyone = [core_mate, x_mate, far_mate, y_mate] + z_mates
    for other in everyone:
        pl.semaphore_signal(barrier, inc=1, device_id=other, device_id_type=MESH)

    def remote(source, target, kind, index, device):
        return pltpu.make_async_remote_copy(
            src_ref=source,
            dst_ref=target,
            send_sem=send.at[kind, index],
            recv_sem=recv.at[kind, index],
            device_id=device,
            device_id_type=MESH,
        )

    def small(source, target, index, device):
        return pltpu.make_async_remote_copy(
            src_ref=source,
            dst_ref=target,
            send_sem=send_small.at[index],
            recv_sem=recv_small.at[index],
            device_id=device,
            device_id_type=MESH,
        )

    def columns(index):
        return pl.ds(pl.multiple_of(index * width, width), width)

    def own_copy(index):
        return pltpu.make_async_copy(
            images.at[:, columns(index)], img.at[0, index], local.at[index]
        )

    def core_copy(index):
        return remote(images.at[:, columns(index)], img.at[1, index], 0, index, core_mate)

    def x_copy(index):
        return remote(images.at[:, columns(index)], img.at[2, index], 1, index, x_mate)

    def forward_copy(index):
        return remote(img.at[2, index], img.at[3, index], 2, index, core_mate)

    def y_copy(index):
        return remote(b_send.at[index], y_got.at[index], 3, index, y_mate)

    def z_copy(index, k):
        return remote(
            z_send.at[index, k - 1], z_got.at[index, k - 1], 3 + k, index, z_mates[k - 1]
        )

    def table_z_copy(index, k):
        rows = pl.ds((side_z - k) * share, share)
        return remote(
            table.at[index, pl.ds(0, share)],
            table.at[index, rows],
            2 + side_z + k,
            index,
            z_mates[k - 1],
        )

    def table_y_copy(index):
        return remote(
            table.at[index, pl.ds(0, half)],
            table.at[index, pl.ds(half, half)],
            2 + 2 * side_z,
            index,
            y_mate,
        )

    def meta_copy(k):
        device = (core_mate, x_mate, far_mate)[k - 1]
        return small(meta, metas.at[k - 1], k - 1, device)

    def misfit_copy(k):
        device = (core_mate, x_mate, far_mate)[k - 1]
        return small(mis.at[k], mis_got.at[k - 1], 2 + k, device)

    s_y_copy = small(s_send, sy_got, 6, y_mate)

    def s_z_copy(k):
        return small(sz_send.at[k - 1], sz_got.at[k - 1], 6 + k, z_mates[k - 1])

    anchor_copy = pltpu.make_async_copy(
        references.at[0, pl.ds(pl.multiple_of(dp * share, share), share)],
        anchor,
        local.at[chunks],
    )
    anchor_copy.start()
    pl.loop(0, chunks)(lambda index: own_copy(index).start())
    pl.semaphore_wait(barrier, len(everyone))
    for k in range(1, 4):
        meta_copy(k).start()

    @pl.loop(0, chunks)
    def start_images(index):
        x_copy(index).start()
        core_copy(index).start()

    z_first = z.astype(jnp.float32)
    y_first = y.astype(jnp.float32)
    r_first = (dp * share).astype(jnp.float32)
    cell_rows = lax.broadcasted_iota(jnp.int32, (cells, LANES), 0).astype(jnp.float32)
    cell_lanes = lax.broadcasted_iota(jnp.int32, (LANES, cells), 1).astype(jnp.float32)
    owned = []
    for block in range(4):
        if block > 0:
            meta_copy(block).wait_recv()
            rows = metas[block - 1]
        else:
            rows = meta[...]
        class_row = rows[0:1]
        rel_r = rows[1:2] - r_first
        class_z = jnp.floor(class_row / float(side_y))
        rel_y = jnp.abs(class_row - float(side_y) * class_z - y_first)
        rel_z = class_z - z_first
        rel_z = jnp.where(rel_z < 0.0, rel_z + float(side_z), rel_z)
        mine = (rel_r >= 0.0) & (rel_r < float(share))
        cell = jnp.where(mine, rel_y * float(half) + rel_z * float(share) + rel_r, -1.0)
        owned.append(mine)
        hot[:, block * LANES : (block + 1) * LANES] = jnp.where(cell_rows == cell, 1.0, 0.0).astype(
            jnp.bfloat16
        )
        cell_t = jnp.transpose(jnp.broadcast_to(cell, (LANES, LANES)))
        hot_t[block] = jnp.where(cell_lanes == cell_t, 1.0, 0.0).astype(jnp.bfloat16)
        focus = jnp.transpose(jnp.broadcast_to(rows[2:3], (LANES, LANES)))
        for part in range(radii // LANES):
            lanes = slice(part * LANES, (part + 1) * LANES)
            phase = 20.0 * focus * tables[0:1, lanes] + 0.1
            wave = bounded_sine(phase) * tables[1:2, lanes]
            crad[block, :, lanes] = wave.astype(jnp.bfloat16)
            sq[block * LANES : (block + 1) * LANES, lanes] = (
                wave * wave + tables[2:3, lanes]
            ).astype(jnp.bfloat16)
    acc[...] = jnp.zeros_like(acc)
    partial = jnp.dot(hot[...], sq[...], preferred_element_type=jnp.float32)
    s_own[...] = partial[:half]
    s_send[...] = partial[half:].astype(jnp.bfloat16)
    s_y_copy.start()

    def tick(t, carry):
        @pl.when(t < chunks)
        def forward():
            x_copy(t).wait_recv()
            forward_copy(t).start()
            target = place[:, columns(t)]
            index_rows = lax.broadcasted_iota(jnp.int32, (radii, width), 0).astype(jnp.float32)
            pick[t] = jnp.where(index_rows == target, 1.0, 0.0).astype(jnp.bfloat16)
            for block in range(4):
                con[block, t] = jnp.dot(
                    crad[block], pick[t], preferred_element_type=jnp.float32
                ).astype(jnp.bfloat16)

        @pl.when(t == 0)
        def counts_out():
            s_y_copy.wait_recv()
            total = s_own[...] + sy_got[...].astype(jnp.float32)
            sz_own[...] = total[:share]
            for k in range(1, side_z):
                sz_send[k - 1] = total[k * share : (k + 1) * share].astype(jnp.bfloat16)
                s_z_copy(k).start()

        @pl.when((t >= 1) & (t < chunks + 1))
        def sum_y():
            index = t - 1
            y_copy(index).wait_recv()
            total = b_own[index] + y_got[index].astype(jnp.float32)
            z_own[index] = total[:share]
            for k in range(1, side_z):
                z_send[index, k - 1] = total[k * share : (k + 1) * share].astype(jnp.bfloat16)
                z_copy(index, k).start()

        @pl.when(t == 2)
        def counts_in():
            anchor_copy.wait()
            total = sz_own[...]
            for k in range(1, side_z):
                s_z_copy(k).wait_recv()
                total = total + sz_got[k - 1].astype(jnp.float32)
            s_sum[...] = total

        @pl.when((t >= 2) & (t < chunks + 2))
        def update():
            index = t - 2
            total = z_own[index]
            for k in range(1, side_z):
                z_copy(index, k).wait_recv()
                total = total + z_got[index, k - 1].astype(jnp.float32)
            squares = s_sum[...]
            coarse = squares.astype(jnp.bfloat16)
            fine = (squares - coarse.astype(jnp.float32)).astype(jnp.bfloat16)
            energy = jnp.dot(coarse, pick[index], preferred_element_type=jnp.float32)
            energy = energy + jnp.dot(fine, pick[index], preferred_element_type=jnp.float32)
            damping = 0.5 * squares[:, radii - 1 : radii] + 1.0
            scale = 1.0 / damping
            start = anchor[:, columns(index)].astype(jnp.float32)
            first = (start - (start * energy - total) * scale).astype(jnp.bfloat16)
            table[index, 0:share] = first
            for k in range(1, side_z):
                table_z_copy(index, k).start()
            again = first.astype(jnp.float32)
            refined[:, columns(index)] = (again - (again * energy - total) * scale).astype(
                jnp.bfloat16
            )

        @pl.when((t >= 3) & (t < chunks + 3))
        def spread():
            index = t - 3
            for k in range(1, side_z):
                table_z_copy(index, k).wait_recv()
            table_y_copy(index).start()

        @pl.when(t < chunks)
        def partial_sums():
            own_copy(t).wait()
            core_copy(t).wait_recv()
            forward_copy(t).wait_recv()
            for block in range(4):
                work[block * LANES : (block + 1) * LANES] = con[block, t] * img[block, t]
            total = jnp.dot(hot[...], work[...], preferred_element_type=jnp.float32)
            b_own[t] = total[:half]
            b_send[t] = total[half:].astype(jnp.bfloat16)
            y_copy(t).start()

        @pl.when(t >= 4)
        def residuals():
            index = t - 4
            table_y_copy(index).wait_recv()
            for block in range(4):
                tiles = jnp.dot(hot_t[block], table[index], preferred_element_type=jnp.float32)
                rest = con[block, index].astype(jnp.float32) * tiles - img[block, index].astype(
                    jnp.float32
                )
                rest = rest * rest
                total = acc[block]
                for part in range(width // LANES):
                    total = total + rest[:, part * LANES : (part + 1) * LANES]
                acc[block] = total

        return carry

    lax.fori_loop(0, chunks + 4, tick, 0)

    for block in (1, 2, 3, 0):
        row = jnp.sum(jnp.transpose(acc[block]), axis=0, keepdims=True)
        row = jnp.where(owned[block], row * (1.0 / float(chunks * width)), 0.0)
        mis[block] = jnp.broadcast_to(row, mis.shape[1:])
        if block > 0:
            misfit_copy(block).start()

    @pl.loop(0, chunks)
    def drain(index):
        core_copy(index).wait_send()
        x_copy(index).wait_send()
        forward_copy(index).wait_send()
        y_copy(index).wait_send()
        for k in range(1, side_z):
            z_copy(index, k).wait_send()
            table_z_copy(index, k).wait_send()
        table_y_copy(index).wait_send()

    s_y_copy.wait_send()
    for k in range(1, side_z):
        s_z_copy(k).wait_send()
    total = mis[0]
    for k in range(1, 4):
        meta_copy(k).wait_send()
        misfit_copy(k).wait()
        total = total + mis_got[k - 1]
    misfit[...] = total


def shards_close(side_y, side_z, images, defocus, classes, rotations, references):
    count_dp = lax.axis_size("dp")
    rows, pixels = images.shape
    share = references.shape[1] // count_dp
    chunks = CHUNKS
    width = pixels // chunks
    half = side_z * share
    cells = side_y * half
    tables, place = radius_tables(SIDE)
    radii = tables.shape[1]
    meta = jnp.concatenate(
        [
            classes.reshape(1, rows).astype(jnp.float32),
            rotations.reshape(1, rows).astype(jnp.float32),
            defocus.reshape(1, rows).astype(jnp.float32),
            jnp.zeros((5, rows), jnp.float32),
        ],
        axis=0,
    )
    bf16, f32 = jnp.bfloat16, jnp.float32
    kinds = 3 + 2 * side_z
    vmem = pl.BlockSpec(memory_space=pltpu.VMEM)
    anywhere = pl.BlockSpec(memory_space=pl.ANY)
    refined, misfit = pl.pallas_call(
        functools.partial(refine_kernel, (chunks, width, share, side_y, side_z)),
        out_shape=(
            jax.ShapeDtypeStruct((share, pixels), bf16),
            jax.ShapeDtypeStruct((8, rows), f32),
        ),
        in_specs=[anywhere, vmem, vmem, vmem, anywhere],
        out_specs=(vmem, vmem),
        scratch_shapes=[
            pltpu.VMEM((4, chunks, rows, width), bf16),
            pltpu.VMEM((3, 8, rows), f32),
            pltpu.VMEM((4, rows, radii), bf16),
            pltpu.VMEM((4 * rows, radii), bf16),
            pltpu.VMEM((4, chunks, rows, width), bf16),
            pltpu.VMEM((chunks, radii, width), bf16),
            pltpu.VMEM((cells, 4 * rows), bf16),
            pltpu.VMEM((4, rows, cells), bf16),
            pltpu.VMEM((4 * rows, width), bf16),
            pltpu.VMEM((chunks, half, width), f32),
            pltpu.VMEM((chunks, half, width), bf16),
            pltpu.VMEM((chunks, half, width), bf16),
            pltpu.VMEM((chunks, share, width), f32),
            pltpu.VMEM((chunks, side_z - 1, share, width), bf16),
            pltpu.VMEM((chunks, side_z - 1, share, width), bf16),
            pltpu.VMEM((chunks, cells, width), bf16),
            pltpu.VMEM((half, radii), f32),
            pltpu.VMEM((half, radii), bf16),
            pltpu.VMEM((half, radii), bf16),
            pltpu.VMEM((share, radii), f32),
            pltpu.VMEM((side_z - 1, share, radii), bf16),
            pltpu.VMEM((side_z - 1, share, radii), bf16),
            pltpu.VMEM((share, radii), f32),
            pltpu.VMEM((share, pixels), bf16),
            pltpu.VMEM((4, rows, LANES), f32),
            pltpu.VMEM((4, 8, rows), f32),
            pltpu.VMEM((3, 8, rows), f32),
            pltpu.SemaphoreType.DMA((kinds, chunks)),
            pltpu.SemaphoreType.DMA((kinds, chunks)),
            pltpu.SemaphoreType.DMA((6 + side_z,)),
            pltpu.SemaphoreType.DMA((6 + side_z,)),
            pltpu.SemaphoreType.DMA((chunks + 1,)),
        ],
        compiler_params=pltpu.CompilerParams(
            collective_id=0, has_side_effects=True, vmem_limit_bytes=48 * 1024 * 1024
        ),
    )(images, meta, jnp.asarray(tables), jnp.asarray(place), references)
    return refined.reshape(1, share, pixels), misfit[0]


def solution(mesh):
    in_specs = (
        P(("cls", "dp"), None),
        P(("cls", "dp")),
        P(("cls", "dp"), None),
        P(("cls", "dp")),
        P("cls", None, None),
    )
    out_specs = (P("cls", "dp", None), P(("cls", "dp")))
    per_device = shards
    if mesh.shape["cls"] == 8 and mesh.shape["dp"] == 4:
        per_device = functools.partial(shards_close, 2, 4)
    return jax.shard_map(
        per_device, mesh=mesh, in_specs=in_specs, out_specs=out_specs, check_vma=False
    )
```

```python
import functools
import jax
import jax.numpy as jnp
import numpy as np
from jax import lax
from jax.experimental import pallas as pl
from jax.experimental.pallas import tpu as pltpu
from jax.sharding import PartitionSpec as P

SIDE = 64
MESH = pl.DeviceIdType.MESH
CHUNKS = 8
WINDOW = 2
LANES = 128


def wave_table(side_count):
    pixel_index = jnp.arange(side_count * side_count, dtype=jnp.int32)
    half_side = side_count // 2
    row_freq = (pixel_index // side_count + half_side) % side_count - half_side
    col_freq = (pixel_index % side_count + half_side) % side_count - half_side
    return (row_freq * row_freq + col_freq * col_freq).astype(jnp.float32) / float(
        half_side * half_side
    )


def contrast(defocus_rows, radius):
    phase = 20.0 * defocus_rows.astype(jnp.float32)[:, None] * radius[None, :] + 0.1
    return -jnp.sin(phase) * jnp.exp(-0.5 * radius)[None, :]


def sweep_rows(table, image_rows, rotation_rows, defocus_rows, radius):
    row_total = image_rows.shape[0]
    block_rows = min(64, row_total)
    block_count = row_total // block_rows
    rotation_count = table.shape[0]
    labels = jnp.arange(rotation_count, dtype=jnp.int32)

    def advance(gradient, block_index):
        row_start = block_index * block_rows
        image_block = lax.dynamic_slice_in_dim(image_rows, row_start, block_rows, 0)
        rotation_block = lax.dynamic_slice_in_dim(rotation_rows, row_start, block_rows, 0)
        defocus_block = lax.dynamic_slice_in_dim(defocus_rows, row_start, block_rows, 0)
        selector = (rotation_block[:, None] == labels[None, :]).astype(jnp.bfloat16)
        tiles = jnp.dot(selector, table, preferred_element_type=jnp.float32)
        contrast_rows = contrast(defocus_block, radius)
        residual = contrast_rows * tiles - image_block.astype(jnp.float32)
        misfit_rows = jnp.mean(residual * residual, axis=1)
        weighted = (contrast_rows * residual).astype(jnp.bfloat16)
        gradient = gradient + lax.dot_general(
            selector, weighted, (((0,), (0,)), ((), ())), preferred_element_type=jnp.float32
        )
        return (gradient, misfit_rows)

    start_grad = jnp.zeros((rotation_count, image_rows.shape[1]), jnp.float32)
    gradient, misfit_blocks = lax.scan(
        advance, start_grad, jnp.arange(block_count, dtype=jnp.int32)
    )
    return (gradient, misfit_blocks.reshape(row_total))


def build_slots(
    images, defocus, rotations, class_rows, class_rank, rank_first, slot_width, count_cls
):
    particle_ids = jnp.arange(images.shape[0], dtype=jnp.int32)
    inside = (class_rank >= rank_first) & (class_rank < rank_first + slot_width)
    slot_of = jnp.where(inside, class_rows * slot_width + class_rank - rank_first, -1)
    slot_ids = jnp.arange(count_cls * slot_width, dtype=jnp.int32)
    slot_match = slot_ids[:, None] == slot_of[None, :]
    slot_live = jnp.any(slot_match, axis=1)
    slot_source = jnp.sum(jnp.where(slot_match, particle_ids[None, :], 0), axis=1)
    send_images = jnp.where(
        slot_live[:, None], jnp.take(images, slot_source, axis=0), jnp.zeros((), jnp.bfloat16)
    )
    send_rotation = jnp.where(slot_live, jnp.take(rotations, slot_source), -1)
    send_defocus = jnp.where(
        slot_live, jnp.take(defocus, slot_source).astype(jnp.float32), 0.0
    ).astype(jnp.bfloat16)
    return (send_images, send_rotation, send_defocus)


def shards(images, defocus, classes, rotations, references):
    count_cls = lax.axis_size("cls")
    count_dp = lax.axis_size("dp")
    particle_count = images.shape[0]
    pixel_count = images.shape[1]
    rotation_count = references.shape[1]
    capacity = max(2, 2 * particle_count // count_cls)
    slot_count = count_cls * capacity
    radius = wave_table(SIDE)
    class_rows = classes[:, 0]
    particle_ids = jnp.arange(particle_count, dtype=jnp.int32)
    earlier_same = (class_rows[:, None] == class_rows[None, :]) & (
        particle_ids[None, :] < particle_ids[:, None]
    )
    class_rank = jnp.sum(earlier_same.astype(jnp.int32), axis=1)
    slot_of = class_rows * capacity + class_rank
    slot_ids = jnp.arange(slot_count, dtype=jnp.int32)
    slot_match = slot_ids[:, None] == slot_of[None, :]
    send_images, send_rotation, send_defocus = build_slots(
        images, defocus, rotations, class_rows, class_rank, 0, capacity, count_cls
    )
    recv_images, recv_rotation, recv_defocus = (
        lax.all_to_all(
            send_images.reshape(count_cls, capacity, pixel_count),
            "cls",
            split_axis=0,
            concat_axis=0,
            tiled=True,
        ),
        lax.all_to_all(
            send_rotation.astype(jnp.bfloat16).reshape(count_cls, capacity),
            "cls",
            split_axis=0,
            concat_axis=0,
            tiled=True,
        ),
        lax.all_to_all(
            send_defocus.reshape(count_cls, capacity),
            "cls",
            split_axis=0,
            concat_axis=0,
            tiled=True,
        ),
    )
    image_slots = recv_images.reshape(slot_count, pixel_count)
    rotation_slots = recv_rotation.reshape(slot_count).astype(jnp.int32)
    defocus_slots = recv_defocus.reshape(slot_count)
    labels = jnp.arange(rotation_count, dtype=jnp.int32)
    local_counts = jnp.sum((rotation_slots[:, None] == labels[None, :]).astype(jnp.float32), axis=0)
    counts = lax.psum(local_counts, "dp")
    damping = 0.5 * counts + 1.0
    table = references[0]
    grad_first, unused_first = sweep_rows(table, image_slots, rotation_slots, defocus_slots, radius)
    share_rows = rotation_count // count_dp
    share_start = lax.axis_index("dp") * share_rows
    damping_share = lax.dynamic_slice_in_dim(damping, share_start, share_rows, 0)
    grad_share = lax.psum_scatter(
        grad_first.astype(jnp.bfloat16), "dp", scatter_dimension=0, tiled=True
    ).astype(jnp.float32)
    anchor = lax.dynamic_slice_in_dim(table, share_start, share_rows, 0).astype(jnp.float32)
    fresh_share = (anchor - grad_share / damping_share[:, None]).astype(jnp.bfloat16)
    table_next = lax.all_gather(fresh_share, "dp", axis=0, tiled=True)
    grad_second, misfit_slots = sweep_rows(
        table_next, image_slots, rotation_slots, defocus_slots, radius
    )
    second_share = lax.psum_scatter(
        grad_second.astype(jnp.bfloat16), "dp", scatter_dimension=0, tiled=True
    ).astype(jnp.float32)
    anchor_next = lax.dynamic_slice_in_dim(table_next, share_start, share_rows, 0).astype(
        jnp.float32
    )
    refined = (anchor_next - second_share / damping_share[:, None]).astype(jnp.bfloat16)
    returned = lax.all_to_all(
        misfit_slots.reshape(count_cls, capacity), "cls", split_axis=0, concat_axis=0, tiled=True
    )
    returned_slots = returned.reshape(slot_count)
    misfit = jnp.sum(jnp.where(slot_match, returned_slots[:, None], 0.0), axis=0)
    return (refined.reshape(1, share_rows, pixel_count), misfit)


def radius_tables(side_count):
    half_side = side_count // 2
    freq = (np.arange(side_count) + half_side) % side_count - half_side
    square = (freq[:, None] ** 2 + freq[None, :] ** 2).reshape(-1)
    values, place = np.unique(square, return_inverse=True)
    width = -(-(len(values) + 1) // LANES) * LANES
    rows = np.zeros((8, width), np.float32)
    rows[0, : len(values)] = values.astype(np.float32) / np.float32(half_side * half_side)
    rows[1, : len(values)] = -np.exp(-0.5 * rows[0, : len(values)])
    rows[2, width - 1] = 1.0
    return rows, place.reshape(1, -1).astype(np.float32)


def bounded_sine(angle):
    turns = jnp.floor(angle * np.float32(1.0 / np.pi) + 0.5)
    rest = angle - turns * np.float32(3.140625)
    rest = rest - turns * np.float32(9.67502593994140625e-4)
    rest = rest - turns * np.float32(1.509957990978376432e-7)
    odd = turns - 2.0 * jnp.floor(turns * 0.5)
    sign = 1.0 - 2.0 * odd
    square = rest * rest
    poly = np.float32(-2.3889859e-08)
    poly = poly * square + np.float32(2.7525562e-06)
    poly = poly * square + np.float32(-1.9840874e-04)
    poly = poly * square + np.float32(8.3333310e-03)
    poly = poly * square + np.float32(-1.6666667e-01)
    return sign * (rest + rest * square * poly)


def refine_kernel(
    sizes,
    images,
    class_in,
    rotation_in,
    defocus_in,
    tables,
    references,
    refined,
    misfit,
    img,
    meta,
    metas,
    crad,
    sq,
    con,
    pick,
    hot,
    hot_t,
    work,
    b_own,
    b_send,
    y_got,
    z_own,
    z_send,
    z_got,
    table,
    s_own,
    s_send,
    sy_got,
    sz_own,
    sz_send,
    sz_got,
    s_sum,
    anchor,
    acc,
    mis,
    mis_got,
    send,
    recv,
    send_small,
    recv_small,
    local,
):
    chunks, width, share, side_y, side_z = sizes
    cls = lax.axis_index("cls")
    dp = lax.axis_index("dp")
    z = cls // side_y
    y = cls % side_y
    radii = crad.shape[2]
    half = side_z * share
    cells = side_y * half

    core_mate = (cls, dp + 1 - 2 * (dp % 2))
    x_mate = (cls, (dp + 2) % 4)
    far_mate = (cls, (dp + 2) % 4 + 1 - 2 * (dp % 2))
    y_mate = (z * side_y + 1 - y, dp)
    z_mates = [(((z + k) % side_z) * side_y + y, dp) for k in range(1, side_z)]

    barrier = pltpu.get_barrier_semaphore()
    everyone = [core_mate, x_mate, far_mate, y_mate] + z_mates
    for other in everyone:
        pl.semaphore_signal(barrier, inc=1, device_id=other, device_id_type=MESH)

    def remote(source, target, kind, index, device):
        return pltpu.make_async_remote_copy(
            src_ref=source,
            dst_ref=target,
            send_sem=send.at[kind, index],
            recv_sem=recv.at[kind, index],
            device_id=device,
            device_id_type=MESH,
        )

    def small(source, target, index, device):
        return pltpu.make_async_remote_copy(
            src_ref=source,
            dst_ref=target,
            send_sem=send_small.at[index],
            recv_sem=recv_small.at[index],
            device_id=device,
            device_id_type=MESH,
        )

    def columns(index):
        return pl.ds(pl.multiple_of(index * width, width), width)

    def own_copy(index):
        return pltpu.make_async_copy(
            images.at[:, columns(index)], img.at[0, index], local.at[index]
        )

    def core_copy(index):
        return remote(images.at[:, columns(index)], img.at[1, index], 0, index, core_mate)

    def x_copy(index):
        return remote(images.at[:, columns(index)], img.at[2, index], 1, index, x_mate)

    def forward_copy(index):
        return remote(img.at[2, index], img.at[3, index], 2, index, core_mate)

    def y_copy(index):
        return remote(b_send.at[index], y_got.at[index], 3, index, y_mate)

    def z_copy(index, k):
        return remote(
            z_send.at[index, k - 1], z_got.at[index, k - 1], 3 + k, index, z_mates[k - 1]
        )

    def table_z_copy(index, k):
        rows = pl.ds((side_z - k) * share, share)
        return remote(
            table.at[index, pl.ds(0, share)],
            table.at[index, rows],
            2 + side_z + k,
            index,
            z_mates[k - 1],
        )

    def table_y_copy(index):
        return remote(
            table.at[index, pl.ds(0, half)],
            table.at[index, pl.ds(half, half)],
            2 + 2 * side_z,
            index,
            y_mate,
        )

    def meta_copy(k):
        device = (core_mate, x_mate, far_mate)[k - 1]
        return small(meta, metas.at[k - 1], k - 1, device)

    def misfit_copy(k):
        device = (core_mate, x_mate, far_mate)[k - 1]
        return small(mis.at[k], mis_got.at[k - 1], 2 + k, device)

    s_y_copy = small(s_send, sy_got, 6, y_mate)

    def s_z_copy(k):
        return small(sz_send.at[k - 1], sz_got.at[k - 1], 6 + k, z_mates[k - 1])

    anchor_copy = pltpu.make_async_copy(
        references.at[0, pl.ds(pl.multiple_of(dp * share, share), share)],
        anchor,
        local.at[chunks],
    )
    anchor_copy.start()
    pl.loop(0, chunks)(lambda index: own_copy(index).start())
    meta[0:1] = class_in[...].astype(jnp.float32)
    meta[1:2] = rotation_in[...].astype(jnp.float32)
    meta[2:3] = defocus_in[...].astype(jnp.float32)
    meta[3:8] = jnp.zeros((5, LANES), jnp.float32)
    pl.semaphore_wait(barrier, len(everyone))
    for k in range(1, 4):
        meta_copy(k).start()
    for index in range(WINDOW):
        x_copy(index).start()
        core_copy(index).start()

    @pl.loop(0, chunks)
    def pick_radii(index):
        target = tables[pl.ds(8 + index, 1), :width]
        index_rows = lax.broadcasted_iota(jnp.int32, (radii, width), 0).astype(jnp.float32)
        pick[index] = jnp.where(index_rows == target, 1.0, 0.0).astype(jnp.bfloat16)

    z_first = z.astype(jnp.float32)
    y_first = y.astype(jnp.float32)
    r_first = (dp * share).astype(jnp.float32)
    cell_rows = lax.broadcasted_iota(jnp.int32, (cells, LANES), 0).astype(jnp.float32)
    cell_lanes = lax.broadcasted_iota(jnp.int32, (LANES, cells), 1).astype(jnp.float32)
    owned = []
    for block in range(4):
        if block > 0:
            meta_copy(block).wait_recv()
            rows = metas[block - 1]
        else:
            rows = meta[...]
        class_row = rows[0:1]
        rel_r = rows[1:2] - r_first
        class_z = jnp.floor(class_row / float(side_y))
        rel_y = jnp.abs(class_row - float(side_y) * class_z - y_first)
        rel_z = class_z - z_first
        rel_z = jnp.where(rel_z < 0.0, rel_z + float(side_z), rel_z)
        mine = (rel_r >= 0.0) & (rel_r < float(share))
        cell = jnp.where(mine, rel_y * float(half) + rel_z * float(share) + rel_r, -1.0)
        owned.append(mine)
        hot[:, block * LANES : (block + 1) * LANES] = jnp.where(cell_rows == cell, 1.0, 0.0).astype(
            jnp.bfloat16
        )
        cell_t = jnp.transpose(jnp.broadcast_to(cell, (LANES, LANES)))
        hot_t[block] = jnp.where(cell_lanes == cell_t, 1.0, 0.0).astype(jnp.bfloat16)
        focus = jnp.transpose(jnp.broadcast_to(rows[2:3], (LANES, LANES)))
        for part in range(radii // LANES):
            lanes = slice(part * LANES, (part + 1) * LANES)
            phase = 20.0 * focus * tables[0:1, lanes] + 0.1
            wave = bounded_sine(phase) * tables[1:2, lanes]
            crad[block, :, lanes] = wave.astype(jnp.bfloat16)
            sq[block * LANES : (block + 1) * LANES, lanes] = (
                wave * wave + tables[2:3, lanes]
            ).astype(jnp.bfloat16)
    acc[...] = jnp.zeros_like(acc)
    partial = jnp.dot(hot[...], sq[...], preferred_element_type=jnp.float32)
    s_own[...] = partial[:half]
    s_send[...] = partial[half:].astype(jnp.bfloat16)
    s_y_copy.start()

    def tick(t, carry):
        @pl.when(t == 1)
        def counts_out():
            s_y_copy.wait_recv()
            total = s_own[...] + sy_got[...].astype(jnp.float32)
            sz_own[...] = total[:share]
            for k in range(1, side_z):
                sz_send[k - 1] = total[k * share : (k + 1) * share].astype(jnp.bfloat16)
                s_z_copy(k).start()

        @pl.when((t >= 3) & (t < chunks + 3))
        def sum_y():
            index = t - 3
            y_copy(index).wait_recv()
            total = b_own[index] + y_got[index].astype(jnp.float32)
            z_own[index] = total[:share]
            for k in range(1, side_z):
                z_send[index, k - 1] = total[k * share : (k + 1) * share].astype(jnp.bfloat16)
                z_copy(index, k).start()

        @pl.when(t == 5)
        def counts_in():
            anchor_copy.wait()
            total = sz_own[...]
            for k in range(1, side_z):
                s_z_copy(k).wait_recv()
                total = total + sz_got[k - 1].astype(jnp.float32)
            s_sum[...] = total

        @pl.when((t >= 5) & (t < chunks + 5))
        def update():
            index = t - 5
            total = z_own[index]
            for k in range(1, side_z):
                z_copy(index, k).wait_recv()
                total = total + z_got[index, k - 1].astype(jnp.float32)
            squares = s_sum[...]
            coarse = squares.astype(jnp.bfloat16)
            fine = (squares - coarse.astype(jnp.float32)).astype(jnp.bfloat16)
            energy = jnp.dot(coarse, pick[index], preferred_element_type=jnp.float32)
            energy = energy + jnp.dot(fine, pick[index], preferred_element_type=jnp.float32)
            damping = 0.5 * squares[:, radii - 1 : radii] + 1.0
            scale = 1.0 / damping
            start = anchor[:, columns(index)].astype(jnp.float32)
            first = (start - (start * energy - total) * scale).astype(jnp.bfloat16)
            table[index, 0:share] = first
            for k in range(1, side_z):
                table_z_copy(index, k).start()
            again = first.astype(jnp.float32)
            refined[:, columns(index)] = (again - (again * energy - total) * scale).astype(
                jnp.bfloat16
            )

        @pl.when((t >= 7) & (t < chunks + 7))
        def spread():
            index = t - 7
            for k in range(1, side_z):
                table_z_copy(index, k).wait_recv()
            table_y_copy(index).start()

        @pl.when(t < chunks)
        def contrasts():
            for block in range(4):
                con[block, t] = jnp.dot(
                    crad[block], pick[t], preferred_element_type=jnp.float32
                ).astype(jnp.bfloat16)

        @pl.when(t >= 9)
        def residuals():
            index = t - 9
            table_y_copy(index).wait_recv()
            for block in range(4):
                tiles = jnp.dot(hot_t[block], table[index], preferred_element_type=jnp.float32)
                rest = con[block, index].astype(jnp.float32) * tiles - img[block, index].astype(
                    jnp.float32
                )
                rest = rest * rest
                total = acc[block]
                for part in range(width // LANES):
                    total = total + rest[:, part * LANES : (part + 1) * LANES]
                acc[block] = total

        @pl.when(t < chunks)
        def forward():
            x_copy(t).wait_recv()
            forward_copy(t).start()

        @pl.when(t < chunks - WINDOW)
        def start_images():
            x_copy(t + WINDOW).start()
            core_copy(t + WINDOW).start()

        @pl.when((t >= 1) & (t < chunks + 1))
        def partial_sums():
            index = t - 1
            own_copy(index).wait()
            core_copy(index).wait_recv()
            forward_copy(index).wait_recv()
            for block in range(4):
                work[block * LANES : (block + 1) * LANES] = con[block, index] * img[block, index]
            total = jnp.dot(hot[...], work[...], preferred_element_type=jnp.float32)
            b_own[index] = total[:half]
            b_send[index] = total[half:].astype(jnp.bfloat16)
            y_copy(index).start()

        return carry

    lax.fori_loop(0, chunks + 9, tick, 0)

    for block in (1, 2, 3, 0):
        row = jnp.sum(jnp.transpose(acc[block]), axis=0, keepdims=True)
        row = jnp.where(owned[block], row * (1.0 / float(chunks * width)), 0.0)
        mis[block] = jnp.broadcast_to(row, mis.shape[1:])
        if block > 0:
            misfit_copy(block).start()

    @pl.loop(0, chunks)
    def drain(index):
        core_copy(index).wait_send()
        x_copy(index).wait_send()
        forward_copy(index).wait_send()
        y_copy(index).wait_send()
        for k in range(1, side_z):
            z_copy(index, k).wait_send()
            table_z_copy(index, k).wait_send()
        table_y_copy(index).wait_send()

    s_y_copy.wait_send()
    for k in range(1, side_z):
        s_z_copy(k).wait_send()
    total = mis[0]
    for k in range(1, 4):
        meta_copy(k).wait_send()
        misfit_copy(k).wait()
        total = total + mis_got[k - 1]
    misfit[...] = total[0:1]


def shards_close(side_y, side_z, images, defocus, classes, rotations, references):
    count_dp = lax.axis_size("dp")
    rows, pixels = images.shape
    share = references.shape[1] // count_dp
    chunks = CHUNKS
    width = pixels // chunks
    half = side_z * share
    cells = side_y * half
    tables, place = radius_tables(SIDE)
    radii = tables.shape[1]
    constants = np.zeros((8 + chunks, max(radii, width)), np.float32)
    constants[:8, :radii] = tables
    constants[8:, :width] = place.reshape(chunks, width)
    bf16, f32 = jnp.bfloat16, jnp.float32
    kinds = 3 + 2 * side_z
    vmem = pl.BlockSpec(memory_space=pltpu.VMEM)
    anywhere = pl.BlockSpec(memory_space=pltpu.HBM)
    refined, misfit = pl.pallas_call(
        functools.partial(refine_kernel, (chunks, width, share, side_y, side_z)),
        out_shape=(
            jax.ShapeDtypeStruct((share, pixels), bf16),
            jax.ShapeDtypeStruct((1, rows), f32),
        ),
        in_specs=[anywhere, vmem, vmem, vmem, vmem, anywhere],
        out_specs=(vmem, vmem),
        scratch_shapes=[
            pltpu.VMEM((4, chunks, rows, width), bf16),
            pltpu.VMEM((8, rows), f32),
            pltpu.VMEM((3, 8, rows), f32),
            pltpu.VMEM((4, rows, radii), bf16),
            pltpu.VMEM((4 * rows, radii), bf16),
            pltpu.VMEM((4, chunks, rows, width), bf16),
            pltpu.VMEM((chunks, radii, width), bf16),
            pltpu.VMEM((cells, 4 * rows), bf16),
            pltpu.VMEM((4, rows, cells), bf16),
            pltpu.VMEM((4 * rows, width), bf16),
            pltpu.VMEM((chunks, half, width), f32),
            pltpu.VMEM((chunks, half, width), bf16),
            pltpu.VMEM((chunks, half, width), bf16),
            pltpu.VMEM((chunks, share, width), f32),
            pltpu.VMEM((chunks, side_z - 1, share, width), bf16),
            pltpu.VMEM((chunks, side_z - 1, share, width), bf16),
            pltpu.VMEM((chunks, cells, width), bf16),
            pltpu.VMEM((half, radii), f32),
            pltpu.VMEM((half, radii), bf16),
            pltpu.VMEM((half, radii), bf16),
            pltpu.VMEM((share, radii), f32),
            pltpu.VMEM((side_z - 1, share, radii), bf16),
            pltpu.VMEM((side_z - 1, share, radii), bf16),
            pltpu.VMEM((share, radii), f32),
            pltpu.VMEM((share, pixels), bf16),
            pltpu.VMEM((4, rows, LANES), f32),
            pltpu.VMEM((4, 8, rows), f32),
            pltpu.VMEM((3, 8, rows), f32),
            pltpu.SemaphoreType.DMA((kinds, chunks)),
            pltpu.SemaphoreType.DMA((kinds, chunks)),
            pltpu.SemaphoreType.DMA((6 + side_z,)),
            pltpu.SemaphoreType.DMA((6 + side_z,)),
            pltpu.SemaphoreType.DMA((chunks + 1,)),
        ],
        compiler_params=pltpu.CompilerParams(
            collective_id=0, has_side_effects=True, vmem_limit_bytes=63 * 1024 * 1024
        ),
    )(
        images,
        classes.reshape(1, rows),
        rotations.reshape(1, rows),
        defocus.reshape(1, rows),
        jnp.asarray(constants),
        references,
    )
    return refined.reshape(1, share, pixels), misfit.reshape(rows)


def solution(mesh):
    in_specs = (
        P(("cls", "dp"), None),
        P(("cls", "dp")),
        P(("cls", "dp"), None),
        P(("cls", "dp")),
        P("cls", None, None),
    )
    out_specs = (P("cls", "dp", None), P(("cls", "dp")))
    per_device = shards
    if mesh.shape["cls"] == 8 and mesh.shape["dp"] == 4:
        per_device = functools.partial(shards_close, 2, 4)
    return jax.shard_map(
        per_device, mesh=mesh, in_specs=in_specs, out_specs=out_specs, check_vma=False
    )
```

```python
import functools
import jax
import jax.numpy as jnp
import numpy as np
from jax import lax
from jax.experimental import pallas as pl
from jax.experimental.pallas import tpu as pltpu
from jax.sharding import PartitionSpec as P

SIDE = 64
MESH = pl.DeviceIdType.MESH
CHUNKS = 8
WINDOW = 4
LANES = 128


def wave_table(side_count):
    pixel_index = jnp.arange(side_count * side_count, dtype=jnp.int32)
    half_side = side_count // 2
    row_freq = (pixel_index // side_count + half_side) % side_count - half_side
    col_freq = (pixel_index % side_count + half_side) % side_count - half_side
    return (row_freq * row_freq + col_freq * col_freq).astype(jnp.float32) / float(
        half_side * half_side
    )


def contrast(defocus_rows, radius):
    phase = 20.0 * defocus_rows.astype(jnp.float32)[:, None] * radius[None, :] + 0.1
    return -jnp.sin(phase) * jnp.exp(-0.5 * radius)[None, :]


def sweep_rows(table, image_rows, rotation_rows, defocus_rows, radius):
    row_total = image_rows.shape[0]
    block_rows = min(64, row_total)
    block_count = row_total // block_rows
    rotation_count = table.shape[0]
    labels = jnp.arange(rotation_count, dtype=jnp.int32)

    def advance(gradient, block_index):
        row_start = block_index * block_rows
        image_block = lax.dynamic_slice_in_dim(image_rows, row_start, block_rows, 0)
        rotation_block = lax.dynamic_slice_in_dim(rotation_rows, row_start, block_rows, 0)
        defocus_block = lax.dynamic_slice_in_dim(defocus_rows, row_start, block_rows, 0)
        selector = (rotation_block[:, None] == labels[None, :]).astype(jnp.bfloat16)
        tiles = jnp.dot(selector, table, preferred_element_type=jnp.float32)
        contrast_rows = contrast(defocus_block, radius)
        residual = contrast_rows * tiles - image_block.astype(jnp.float32)
        misfit_rows = jnp.mean(residual * residual, axis=1)
        weighted = (contrast_rows * residual).astype(jnp.bfloat16)
        gradient = gradient + lax.dot_general(
            selector, weighted, (((0,), (0,)), ((), ())), preferred_element_type=jnp.float32
        )
        return (gradient, misfit_rows)

    start_grad = jnp.zeros((rotation_count, image_rows.shape[1]), jnp.float32)
    gradient, misfit_blocks = lax.scan(
        advance, start_grad, jnp.arange(block_count, dtype=jnp.int32)
    )
    return (gradient, misfit_blocks.reshape(row_total))


def build_slots(
    images, defocus, rotations, class_rows, class_rank, rank_first, slot_width, count_cls
):
    particle_ids = jnp.arange(images.shape[0], dtype=jnp.int32)
    inside = (class_rank >= rank_first) & (class_rank < rank_first + slot_width)
    slot_of = jnp.where(inside, class_rows * slot_width + class_rank - rank_first, -1)
    slot_ids = jnp.arange(count_cls * slot_width, dtype=jnp.int32)
    slot_match = slot_ids[:, None] == slot_of[None, :]
    slot_live = jnp.any(slot_match, axis=1)
    slot_source = jnp.sum(jnp.where(slot_match, particle_ids[None, :], 0), axis=1)
    send_images = jnp.where(
        slot_live[:, None], jnp.take(images, slot_source, axis=0), jnp.zeros((), jnp.bfloat16)
    )
    send_rotation = jnp.where(slot_live, jnp.take(rotations, slot_source), -1)
    send_defocus = jnp.where(
        slot_live, jnp.take(defocus, slot_source).astype(jnp.float32), 0.0
    ).astype(jnp.bfloat16)
    return (send_images, send_rotation, send_defocus)


def shards(images, defocus, classes, rotations, references):
    count_cls = lax.axis_size("cls")
    count_dp = lax.axis_size("dp")
    particle_count = images.shape[0]
    pixel_count = images.shape[1]
    rotation_count = references.shape[1]
    capacity = max(2, 2 * particle_count // count_cls)
    slot_count = count_cls * capacity
    radius = wave_table(SIDE)
    class_rows = classes[:, 0]
    particle_ids = jnp.arange(particle_count, dtype=jnp.int32)
    earlier_same = (class_rows[:, None] == class_rows[None, :]) & (
        particle_ids[None, :] < particle_ids[:, None]
    )
    class_rank = jnp.sum(earlier_same.astype(jnp.int32), axis=1)
    slot_of = class_rows * capacity + class_rank
    slot_ids = jnp.arange(slot_count, dtype=jnp.int32)
    slot_match = slot_ids[:, None] == slot_of[None, :]
    send_images, send_rotation, send_defocus = build_slots(
        images, defocus, rotations, class_rows, class_rank, 0, capacity, count_cls
    )
    recv_images, recv_rotation, recv_defocus = (
        lax.all_to_all(
            send_images.reshape(count_cls, capacity, pixel_count),
            "cls",
            split_axis=0,
            concat_axis=0,
            tiled=True,
        ),
        lax.all_to_all(
            send_rotation.astype(jnp.bfloat16).reshape(count_cls, capacity),
            "cls",
            split_axis=0,
            concat_axis=0,
            tiled=True,
        ),
        lax.all_to_all(
            send_defocus.reshape(count_cls, capacity),
            "cls",
            split_axis=0,
            concat_axis=0,
            tiled=True,
        ),
    )
    image_slots = recv_images.reshape(slot_count, pixel_count)
    rotation_slots = recv_rotation.reshape(slot_count).astype(jnp.int32)
    defocus_slots = recv_defocus.reshape(slot_count)
    labels = jnp.arange(rotation_count, dtype=jnp.int32)
    local_counts = jnp.sum((rotation_slots[:, None] == labels[None, :]).astype(jnp.float32), axis=0)
    counts = lax.psum(local_counts, "dp")
    damping = 0.5 * counts + 1.0
    table = references[0]
    grad_first, unused_first = sweep_rows(table, image_slots, rotation_slots, defocus_slots, radius)
    share_rows = rotation_count // count_dp
    share_start = lax.axis_index("dp") * share_rows
    damping_share = lax.dynamic_slice_in_dim(damping, share_start, share_rows, 0)
    grad_share = lax.psum_scatter(
        grad_first.astype(jnp.bfloat16), "dp", scatter_dimension=0, tiled=True
    ).astype(jnp.float32)
    anchor = lax.dynamic_slice_in_dim(table, share_start, share_rows, 0).astype(jnp.float32)
    fresh_share = (anchor - grad_share / damping_share[:, None]).astype(jnp.bfloat16)
    table_next = lax.all_gather(fresh_share, "dp", axis=0, tiled=True)
    grad_second, misfit_slots = sweep_rows(
        table_next, image_slots, rotation_slots, defocus_slots, radius
    )
    second_share = lax.psum_scatter(
        grad_second.astype(jnp.bfloat16), "dp", scatter_dimension=0, tiled=True
    ).astype(jnp.float32)
    anchor_next = lax.dynamic_slice_in_dim(table_next, share_start, share_rows, 0).astype(
        jnp.float32
    )
    refined = (anchor_next - second_share / damping_share[:, None]).astype(jnp.bfloat16)
    returned = lax.all_to_all(
        misfit_slots.reshape(count_cls, capacity), "cls", split_axis=0, concat_axis=0, tiled=True
    )
    returned_slots = returned.reshape(slot_count)
    misfit = jnp.sum(jnp.where(slot_match, returned_slots[:, None], 0.0), axis=0)
    return (refined.reshape(1, share_rows, pixel_count), misfit)


def radius_tables(side_count):
    half_side = side_count // 2
    freq = (np.arange(side_count) + half_side) % side_count - half_side
    square = (freq[:, None] ** 2 + freq[None, :] ** 2).reshape(-1)
    values, place = np.unique(square, return_inverse=True)
    width = -(-(len(values) + 1) // LANES) * LANES
    rows = np.zeros((8, width), np.float32)
    rows[0, : len(values)] = values.astype(np.float32) / np.float32(half_side * half_side)
    rows[1, : len(values)] = -np.exp(-0.5 * rows[0, : len(values)])
    rows[2, width - 1] = 1.0
    return rows, place.reshape(1, -1).astype(np.float32)


def bounded_sine(angle):
    turns = jnp.floor(angle * np.float32(1.0 / np.pi) + 0.5)
    rest = angle - turns * np.float32(3.140625)
    rest = rest - turns * np.float32(9.67502593994140625e-4)
    rest = rest - turns * np.float32(1.509957990978376432e-7)
    odd = turns - 2.0 * jnp.floor(turns * 0.5)
    sign = 1.0 - 2.0 * odd
    square = rest * rest
    poly = np.float32(-2.3889859e-08)
    poly = poly * square + np.float32(2.7525562e-06)
    poly = poly * square + np.float32(-1.9840874e-04)
    poly = poly * square + np.float32(8.3333310e-03)
    poly = poly * square + np.float32(-1.6666667e-01)
    return sign * (rest + rest * square * poly)


def refine_kernel(
    sizes,
    images,
    class_in,
    rotation_in,
    defocus_in,
    tables,
    references,
    refined,
    misfit,
    img,
    meta,
    metas,
    crad,
    sq,
    con,
    pick,
    hot,
    hot_t,
    b_own,
    b_send,
    y_got,
    z_own,
    z_send,
    z_got,
    table,
    s_own,
    s_send,
    sy_got,
    sz_own,
    sz_send,
    sz_got,
    s_sum,
    anchor,
    acc,
    mis,
    mis_got,
    send,
    recv,
    send_small,
    recv_small,
    local,
):
    chunks, width, share, side_y, side_z = sizes
    cls = lax.axis_index("cls")
    dp = lax.axis_index("dp")
    z = cls // side_y
    y = cls % side_y
    radii = crad.shape[2]
    half = side_z * share
    cells = side_y * half

    core = dp % 2
    x = dp // 2
    other_core = dp + 1 - 2 * core
    other_x = dp + 2 - 4 * x
    other_y = cls + 1 - 2 * y
    core_mate = (cls, other_core)
    x_mate = (cls, other_x)
    y_mate = (other_y, dp)
    mates = (
        core_mate,
        x_mate,
        (cls, other_x + 1 - 2 * core),
        y_mate,
        (other_y, other_core),
    )
    z_mates = [(((z + k) % side_z) * side_y + y, dp) for k in range(1, side_z)]

    barrier = pltpu.get_barrier_semaphore()
    everyone = list(mates) + z_mates
    for other in everyone:
        pl.semaphore_signal(barrier, inc=1, device_id=other, device_id_type=MESH)

    def remote(source, target, kind, index, device):
        return pltpu.make_async_remote_copy(
            src_ref=source,
            dst_ref=target,
            send_sem=send.at[kind, index],
            recv_sem=recv.at[kind, index],
            device_id=device,
            device_id_type=MESH,
        )

    def small(source, target, index, device):
        return pltpu.make_async_remote_copy(
            src_ref=source,
            dst_ref=target,
            send_sem=send_small.at[index],
            recv_sem=recv_small.at[index],
            device_id=device,
            device_id_type=MESH,
        )

    def share_mate(index):
        family = index % 2
        return (cls + family * (1 - 2 * y), dp + (1 - family) * (2 - 4 * x))

    def sum_mate(index):
        family = index % 2
        return (cls + (1 - family) * (1 - 2 * y), dp + family * (2 - 4 * x))

    def block_rows(block):
        return pl.ds(block * LANES, LANES)

    def columns(index):
        return pl.ds(pl.multiple_of(index * width, width), width)

    def own_copy(index):
        return pltpu.make_async_copy(
            images.at[:, columns(index)], img.at[index, block_rows(0)], local.at[index]
        )

    def core_copy(index):
        return remote(
            images.at[:, columns(index)], img.at[index, block_rows(1)], 0, index, core_mate
        )

    def share_copy(index):
        return remote(
            images.at[:, columns(index)],
            img.at[index, block_rows(2)],
            1,
            index,
            share_mate(index),
        )

    def forward_copy(index):
        return remote(
            img.at[index, block_rows(2)], img.at[index, block_rows(3)], 2, index, core_mate
        )

    def y_copy(index):
        return remote(b_send.at[index], y_got.at[index], 3, index, sum_mate(index))

    def z_copy(index, k):
        return remote(
            z_send.at[index, k - 1], z_got.at[index, k - 1], 3 + k, index, z_mates[k - 1]
        )

    def table_z_copy(index, k):
        rows = pl.ds((side_z - k) * share, share)
        return remote(
            table.at[index, pl.ds(0, share)],
            table.at[index, rows],
            2 + side_z + k,
            index,
            z_mates[k - 1],
        )

    def table_y_copy(index):
        return remote(
            table.at[index, pl.ds(0, half)],
            table.at[index, pl.ds(half, half)],
            2 + 2 * side_z,
            index,
            sum_mate(index),
        )

    def meta_copy(k):
        return small(meta, metas.at[k], k, mates[k])

    def misfit_copy(k):
        return small(mis.at[k], mis_got.at[k], 5 + k, mates[k])

    s_y_copy = small(s_send, sy_got, 10, y_mate)

    def s_z_copy(k):
        return small(sz_send.at[k - 1], sz_got.at[k - 1], 10 + k, z_mates[k - 1])

    anchor_copy = pltpu.make_async_copy(
        references.at[0, pl.ds(pl.multiple_of(dp * share, share), share)],
        anchor,
        local.at[chunks],
    )
    anchor_copy.start()
    pl.loop(0, chunks)(lambda index: own_copy(index).start())
    meta[0:1] = class_in[...].astype(jnp.float32)
    meta[1:2] = rotation_in[...].astype(jnp.float32)
    meta[2:3] = defocus_in[...].astype(jnp.float32)
    meta[3:8] = jnp.zeros((5, LANES), jnp.float32)
    pl.semaphore_wait(barrier, len(everyone))
    for k in range(5):
        meta_copy(k).start()
    for index in range(WINDOW):
        share_copy(index).start()
        core_copy(index).start()

    @pl.loop(0, chunks)
    def pick_radii(index):
        target = tables[pl.ds(8 + index, 1), :width]
        index_rows = lax.broadcasted_iota(jnp.int32, (radii, width), 0).astype(jnp.float32)
        pick[index] = jnp.where(index_rows == target, 1.0, 0.0).astype(jnp.bfloat16)

    z_first = z.astype(jnp.float32)
    y_first = y.astype(jnp.float32)
    x_first = x.astype(jnp.float32)
    core_first = core.astype(jnp.float32)
    cell_rows = lax.broadcasted_iota(jnp.int32, (cells, LANES), 0).astype(jnp.float32)
    cell_lanes = lax.broadcasted_iota(jnp.int32, (LANES, cells), 1).astype(jnp.float32)
    owned = {}
    for source, places in enumerate((((0, 0), (1, 0)), ((0, 1), (1, 1)), ((0, 2),), ((0, 3),), ((1, 2),), ((1, 3),))):
        if source > 0:
            meta_copy(source - 1).wait_recv()
            rows = metas[source - 1]
        else:
            rows = meta[...]
        class_z = jnp.floor(rows[0:1] / float(side_y))
        class_y = rows[0:1] - float(side_y) * class_z
        turn_dp = jnp.floor(rows[1:2] / float(share))
        turn_r = rows[1:2] - float(share) * turn_dp
        turn_x = jnp.floor(turn_dp * 0.5)
        rel_z = class_z - z_first
        rel_z = jnp.where(rel_z < 0.0, rel_z + float(side_z), rel_z)
        off_x = jnp.abs(turn_x - x_first)
        off_y = jnp.abs(class_y - y_first)
        off_core = jnp.abs(turn_dp - 2.0 * turn_x - core_first)
        focus = jnp.transpose(jnp.broadcast_to(rows[2:3], (LANES, LANES)))
        for family, block in places:
            off_share, off_sum = (off_x, off_y) if family == 0 else (off_y, off_x)
            mine = (off_share + off_core) < 0.5
            cell = jnp.where(mine, off_sum * float(half) + rel_z * float(share) + turn_r, -1.0)
            owned[family, block] = mine
            span = slice(block * LANES, (block + 1) * LANES)
            hot[family, :, span] = jnp.where(cell_rows == cell, 1.0, 0.0).astype(jnp.bfloat16)
            cell_t = jnp.transpose(jnp.broadcast_to(cell, (LANES, LANES)))
            hot_t[family, span] = jnp.where(cell_lanes == cell_t, 1.0, 0.0).astype(jnp.bfloat16)
        for part in range(radii // LANES):
            lanes = slice(part * LANES, (part + 1) * LANES)
            phase = 20.0 * focus * tables[0:1, lanes] + 0.1
            wave = bounded_sine(phase) * tables[1:2, lanes]
            for family, block in places:
                span = slice(block * LANES, (block + 1) * LANES)
                crad[family, span, lanes] = wave.astype(jnp.bfloat16)
                if family == 0:
                    sq[span, lanes] = (wave * wave + tables[2:3, lanes]).astype(jnp.bfloat16)
    acc[...] = jnp.zeros_like(acc)
    partial = jnp.dot(hot[0], sq[...], preferred_element_type=jnp.float32)
    s_own[...] = partial[:half]
    s_send[...] = partial[half:].astype(jnp.bfloat16)
    s_y_copy.start()

    def tick(t, carry):
        @pl.when(t == 1)
        def counts_out():
            s_y_copy.wait_recv()
            total = s_own[...] + sy_got[...].astype(jnp.float32)
            sz_own[...] = total[:share]
            for k in range(1, side_z):
                sz_send[k - 1] = total[k * share : (k + 1) * share].astype(jnp.bfloat16)
                s_z_copy(k).start()

        @pl.when((t >= 3) & (t < chunks + 3))
        def sum_y():
            index = t - 3
            y_copy(index).wait_recv()
            total = b_own[index] + y_got[index].astype(jnp.float32)
            z_own[index] = total[:share]
            for k in range(1, side_z):
                z_send[index, k - 1] = total[k * share : (k + 1) * share].astype(jnp.bfloat16)
                z_copy(index, k).start()

        @pl.when(t == 5)
        def counts_in():
            anchor_copy.wait()
            total = sz_own[...]
            for k in range(1, side_z):
                s_z_copy(k).wait_recv()
                total = total + sz_got[k - 1].astype(jnp.float32)
            s_sum[...] = total

        @pl.when((t >= 5) & (t < chunks + 5))
        def update():
            index = t - 5
            total = z_own[index]
            for k in range(1, side_z):
                z_copy(index, k).wait_recv()
                total = total + z_got[index, k - 1].astype(jnp.float32)
            squares = s_sum[...]
            coarse = squares.astype(jnp.bfloat16)
            fine = (squares - coarse.astype(jnp.float32)).astype(jnp.bfloat16)
            pair = jnp.dot(
                jnp.concatenate([coarse, fine], axis=0),
                pick[index],
                preferred_element_type=jnp.float32,
            )
            energy = pair[:share] + pair[share:]
            damping = 0.5 * squares[:, radii - 1 : radii] + 1.0
            scale = 1.0 / damping
            start = anchor[:, columns(index)].astype(jnp.float32)
            first = (start - (start * energy - total) * scale).astype(jnp.bfloat16)
            table[index, 0:share] = first
            for k in range(1, side_z):
                table_z_copy(index, k).start()
            again = first.astype(jnp.float32)
            refined[:, columns(index)] = (again - (again * energy - total) * scale).astype(
                jnp.bfloat16
            )

        @pl.when((t >= 7) & (t < chunks + 7))
        def spread():
            index = t - 7
            for k in range(1, side_z):
                table_z_copy(index, k).wait_recv()
            table_y_copy(index).start()

        @pl.when(t < chunks)
        def contrasts():
            con[t] = jnp.dot(
                crad[t % 2], pick[t], preferred_element_type=jnp.float32
            ).astype(jnp.bfloat16)

        @pl.when(t >= 9)
        def residuals():
            index = t - 9
            table_y_copy(index).wait_recv()
            tiles = jnp.dot(hot_t[index % 2], table[index], preferred_element_type=jnp.float32)
            rest = con[index].astype(jnp.float32) * tiles - img[index].astype(jnp.float32)
            rest = rest * rest
            total = acc[index % 2]
            for part in range(width // LANES):
                total = total + rest[:, part * LANES : (part + 1) * LANES]
            acc[index % 2] = total

        @pl.when(t < chunks)
        def forward():
            share_copy(t).wait_recv()
            forward_copy(t).start()

        @pl.when(t < chunks - WINDOW)
        def start_images():
            share_copy(t + WINDOW).start()
            core_copy(t + WINDOW).start()

        @pl.when((t >= 1) & (t < chunks + 1))
        def partial_sums():
            index = t - 1
            own_copy(index).wait()
            core_copy(index).wait_recv()
            forward_copy(index).wait_recv()
            total = jnp.dot(
                hot[index % 2], con[index] * img[index], preferred_element_type=jnp.float32
            )
            b_own[index] = total[:half]
            b_send[index] = total[half:].astype(jnp.bfloat16)
            y_copy(index).start()

        return carry

    lax.fori_loop(0, chunks + 9, tick, 0)

    def row_of(family, block):
        part = acc[family, block * LANES : (block + 1) * LANES]
        row = jnp.sum(jnp.transpose(part), axis=0, keepdims=True)
        return jnp.where(owned[family, block], row * (1.0 / float(chunks * width)), 0.0)

    for k, row in enumerate(
        (
            row_of(0, 1) + row_of(1, 1),
            row_of(0, 2),
            row_of(0, 3),
            row_of(1, 2),
            row_of(1, 3),
        )
    ):
        mis[k] = jnp.broadcast_to(row, mis.shape[1:])
        misfit_copy(k).start()

    @pl.loop(0, chunks)
    def drain(index):
        core_copy(index).wait_send()
        share_copy(index).wait_send()
        forward_copy(index).wait_send()
        y_copy(index).wait_send()
        for k in range(1, side_z):
            z_copy(index, k).wait_send()
            table_z_copy(index, k).wait_send()
        table_y_copy(index).wait_send()

    s_y_copy.wait_send()
    for k in range(1, side_z):
        s_z_copy(k).wait_send()
    total = row_of(0, 0) + row_of(1, 0)
    for k in range(5):
        meta_copy(k).wait_send()
        misfit_copy(k).wait()
        total = total + mis_got[k, 0:1]
    misfit[...] = total


def shards_close(side_y, side_z, images, defocus, classes, rotations, references):
    count_dp = lax.axis_size("dp")
    rows, pixels = images.shape
    share = references.shape[1] // count_dp
    chunks = CHUNKS
    width = pixels // chunks
    half = side_z * share
    cells = side_y * half
    tables, place = radius_tables(SIDE)
    radii = tables.shape[1]
    constants = np.zeros((8 + chunks, max(radii, width)), np.float32)
    constants[:8, :radii] = tables
    constants[8:, :width] = place.reshape(chunks, width)
    bf16, f32 = jnp.bfloat16, jnp.float32
    kinds = 3 + 2 * side_z
    vmem = pl.BlockSpec(memory_space=pltpu.VMEM)
    anywhere = pl.BlockSpec(memory_space=pltpu.HBM)
    refined, misfit = pl.pallas_call(
        functools.partial(refine_kernel, (chunks, width, share, side_y, side_z)),
        out_shape=(
            jax.ShapeDtypeStruct((share, pixels), bf16),
            jax.ShapeDtypeStruct((1, rows), f32),
        ),
        in_specs=[anywhere, vmem, vmem, vmem, vmem, anywhere],
        out_specs=(vmem, vmem),
        scratch_shapes=[
            pltpu.VMEM((chunks, 4 * rows, width), bf16),
            pltpu.VMEM((8, rows), f32),
            pltpu.VMEM((5, 8, rows), f32),
            pltpu.VMEM((2, 4 * rows, radii), bf16),
            pltpu.VMEM((4 * rows, radii), bf16),
            pltpu.VMEM((chunks, 4 * rows, width), bf16),
            pltpu.VMEM((chunks, radii, width), bf16),
            pltpu.VMEM((2, cells, 4 * rows), bf16),
            pltpu.VMEM((2, 4 * rows, cells), bf16),
            pltpu.VMEM((chunks, half, width), f32),
            pltpu.VMEM((chunks, half, width), bf16),
            pltpu.VMEM((chunks, half, width), bf16),
            pltpu.VMEM((chunks, share, width), f32),
            pltpu.VMEM((chunks, side_z - 1, share, width), bf16),
            pltpu.VMEM((chunks, side_z - 1, share, width), bf16),
            pltpu.VMEM((chunks, cells, width), bf16),
            pltpu.VMEM((half, radii), f32),
            pltpu.VMEM((half, radii), bf16),
            pltpu.VMEM((half, radii), bf16),
            pltpu.VMEM((share, radii), f32),
            pltpu.VMEM((side_z - 1, share, radii), bf16),
            pltpu.VMEM((side_z - 1, share, radii), bf16),
            pltpu.VMEM((share, radii), f32),
            pltpu.VMEM((share, pixels), bf16),
            pltpu.VMEM((2, 4 * rows, LANES), f32),
            pltpu.VMEM((5, 8, rows), f32),
            pltpu.VMEM((5, 8, rows), f32),
            pltpu.SemaphoreType.DMA((kinds, chunks)),
            pltpu.SemaphoreType.DMA((kinds, chunks)),
            pltpu.SemaphoreType.DMA((10 + side_z,)),
            pltpu.SemaphoreType.DMA((10 + side_z,)),
            pltpu.SemaphoreType.DMA((chunks + 1,)),
        ],
        compiler_params=pltpu.CompilerParams(
            collective_id=0, has_side_effects=True, vmem_limit_bytes=63 * 1024 * 1024
        ),
    )(
        images,
        classes.reshape(1, rows),
        rotations.reshape(1, rows),
        defocus.reshape(1, rows),
        jnp.asarray(constants),
        references,
    )
    return refined.reshape(1, share, pixels), misfit.reshape(rows)


def solution(mesh):
    in_specs = (
        P(("cls", "dp"), None),
        P(("cls", "dp")),
        P(("cls", "dp"), None),
        P(("cls", "dp")),
        P("cls", None, None),
    )
    out_specs = (P("cls", "dp", None), P(("cls", "dp")))
    per_device = shards
    if mesh.shape["cls"] == 8 and mesh.shape["dp"] == 4:
        per_device = functools.partial(shards_close, 2, 4)
    return jax.shard_map(
        per_device, mesh=mesh, in_specs=in_specs, out_specs=out_specs, check_vma=False
    )
```

```python
import functools
import jax
import jax.numpy as jnp
import numpy as np
from jax import lax
from jax.experimental import pallas as pl
from jax.experimental.pallas import tpu as pltpu
from jax.sharding import PartitionSpec as P

SIDE = 64
MESH = pl.DeviceIdType.MESH
CHUNKS = 4
WINDOW = 4
LANES = 128


def wave_table(side_count):
    pixel_index = jnp.arange(side_count * side_count, dtype=jnp.int32)
    half_side = side_count // 2
    row_freq = (pixel_index // side_count + half_side) % side_count - half_side
    col_freq = (pixel_index % side_count + half_side) % side_count - half_side
    return (row_freq * row_freq + col_freq * col_freq).astype(jnp.float32) / float(
        half_side * half_side
    )


def contrast(defocus_rows, radius):
    phase = 20.0 * defocus_rows.astype(jnp.float32)[:, None] * radius[None, :] + 0.1
    return -jnp.sin(phase) * jnp.exp(-0.5 * radius)[None, :]


def sweep_rows(table, image_rows, rotation_rows, defocus_rows, radius):
    row_total = image_rows.shape[0]
    block_rows = min(64, row_total)
    block_count = row_total // block_rows
    rotation_count = table.shape[0]
    labels = jnp.arange(rotation_count, dtype=jnp.int32)

    def advance(gradient, block_index):
        row_start = block_index * block_rows
        image_block = lax.dynamic_slice_in_dim(image_rows, row_start, block_rows, 0)
        rotation_block = lax.dynamic_slice_in_dim(rotation_rows, row_start, block_rows, 0)
        defocus_block = lax.dynamic_slice_in_dim(defocus_rows, row_start, block_rows, 0)
        selector = (rotation_block[:, None] == labels[None, :]).astype(jnp.bfloat16)
        tiles = jnp.dot(selector, table, preferred_element_type=jnp.float32)
        contrast_rows = contrast(defocus_block, radius)
        residual = contrast_rows * tiles - image_block.astype(jnp.float32)
        misfit_rows = jnp.mean(residual * residual, axis=1)
        weighted = (contrast_rows * residual).astype(jnp.bfloat16)
        gradient = gradient + lax.dot_general(
            selector, weighted, (((0,), (0,)), ((), ())), preferred_element_type=jnp.float32
        )
        return (gradient, misfit_rows)

    start_grad = jnp.zeros((rotation_count, image_rows.shape[1]), jnp.float32)
    gradient, misfit_blocks = lax.scan(
        advance, start_grad, jnp.arange(block_count, dtype=jnp.int32)
    )
    return (gradient, misfit_blocks.reshape(row_total))


def build_slots(
    images, defocus, rotations, class_rows, class_rank, rank_first, slot_width, count_cls
):
    particle_ids = jnp.arange(images.shape[0], dtype=jnp.int32)
    inside = (class_rank >= rank_first) & (class_rank < rank_first + slot_width)
    slot_of = jnp.where(inside, class_rows * slot_width + class_rank - rank_first, -1)
    slot_ids = jnp.arange(count_cls * slot_width, dtype=jnp.int32)
    slot_match = slot_ids[:, None] == slot_of[None, :]
    slot_live = jnp.any(slot_match, axis=1)
    slot_source = jnp.sum(jnp.where(slot_match, particle_ids[None, :], 0), axis=1)
    send_images = jnp.where(
        slot_live[:, None], jnp.take(images, slot_source, axis=0), jnp.zeros((), jnp.bfloat16)
    )
    send_rotation = jnp.where(slot_live, jnp.take(rotations, slot_source), -1)
    send_defocus = jnp.where(
        slot_live, jnp.take(defocus, slot_source).astype(jnp.float32), 0.0
    ).astype(jnp.bfloat16)
    return (send_images, send_rotation, send_defocus)


def shards(images, defocus, classes, rotations, references):
    count_cls = lax.axis_size("cls")
    count_dp = lax.axis_size("dp")
    particle_count = images.shape[0]
    pixel_count = images.shape[1]
    rotation_count = references.shape[1]
    capacity = max(2, 2 * particle_count // count_cls)
    slot_count = count_cls * capacity
    radius = wave_table(SIDE)
    class_rows = classes[:, 0]
    particle_ids = jnp.arange(particle_count, dtype=jnp.int32)
    earlier_same = (class_rows[:, None] == class_rows[None, :]) & (
        particle_ids[None, :] < particle_ids[:, None]
    )
    class_rank = jnp.sum(earlier_same.astype(jnp.int32), axis=1)
    slot_of = class_rows * capacity + class_rank
    slot_ids = jnp.arange(slot_count, dtype=jnp.int32)
    slot_match = slot_ids[:, None] == slot_of[None, :]
    send_images, send_rotation, send_defocus = build_slots(
        images, defocus, rotations, class_rows, class_rank, 0, capacity, count_cls
    )
    recv_images, recv_rotation, recv_defocus = (
        lax.all_to_all(
            send_images.reshape(count_cls, capacity, pixel_count),
            "cls",
            split_axis=0,
            concat_axis=0,
            tiled=True,
        ),
        lax.all_to_all(
            send_rotation.astype(jnp.bfloat16).reshape(count_cls, capacity),
            "cls",
            split_axis=0,
            concat_axis=0,
            tiled=True,
        ),
        lax.all_to_all(
            send_defocus.reshape(count_cls, capacity),
            "cls",
            split_axis=0,
            concat_axis=0,
            tiled=True,
        ),
    )
    image_slots = recv_images.reshape(slot_count, pixel_count)
    rotation_slots = recv_rotation.reshape(slot_count).astype(jnp.int32)
    defocus_slots = recv_defocus.reshape(slot_count)
    labels = jnp.arange(rotation_count, dtype=jnp.int32)
    local_counts = jnp.sum((rotation_slots[:, None] == labels[None, :]).astype(jnp.float32), axis=0)
    counts = lax.psum(local_counts, "dp")
    damping = 0.5 * counts + 1.0
    table = references[0]
    grad_first, unused_first = sweep_rows(table, image_slots, rotation_slots, defocus_slots, radius)
    share_rows = rotation_count // count_dp
    share_start = lax.axis_index("dp") * share_rows
    damping_share = lax.dynamic_slice_in_dim(damping, share_start, share_rows, 0)
    grad_share = lax.psum_scatter(
        grad_first.astype(jnp.bfloat16), "dp", scatter_dimension=0, tiled=True
    ).astype(jnp.float32)
    anchor = lax.dynamic_slice_in_dim(table, share_start, share_rows, 0).astype(jnp.float32)
    fresh_share = (anchor - grad_share / damping_share[:, None]).astype(jnp.bfloat16)
    table_next = lax.all_gather(fresh_share, "dp", axis=0, tiled=True)
    grad_second, misfit_slots = sweep_rows(
        table_next, image_slots, rotation_slots, defocus_slots, radius
    )
    second_share = lax.psum_scatter(
        grad_second.astype(jnp.bfloat16), "dp", scatter_dimension=0, tiled=True
    ).astype(jnp.float32)
    anchor_next = lax.dynamic_slice_in_dim(table_next, share_start, share_rows, 0).astype(
        jnp.float32
    )
    refined = (anchor_next - second_share / damping_share[:, None]).astype(jnp.bfloat16)
    returned = lax.all_to_all(
        misfit_slots.reshape(count_cls, capacity), "cls", split_axis=0, concat_axis=0, tiled=True
    )
    returned_slots = returned.reshape(slot_count)
    misfit = jnp.sum(jnp.where(slot_match, returned_slots[:, None], 0.0), axis=0)
    return (refined.reshape(1, share_rows, pixel_count), misfit)


def radius_tables(side_count):
    half_side = side_count // 2
    freq = (np.arange(side_count) + half_side) % side_count - half_side
    square = (freq[:, None] ** 2 + freq[None, :] ** 2).reshape(-1)
    values, place = np.unique(square, return_inverse=True)
    width = -(-(len(values) + 1) // LANES) * LANES
    rows = np.zeros((8, width), np.float32)
    rows[0, : len(values)] = values.astype(np.float32) / np.float32(half_side * half_side)
    rows[1, : len(values)] = -np.exp(-0.5 * rows[0, : len(values)])
    rows[2, width - 1] = 1.0
    return rows, place.reshape(1, -1).astype(np.float32)


def bounded_sine(angle):
    turns = jnp.floor(angle * np.float32(1.0 / np.pi) + 0.5)
    rest = angle - turns * np.float32(3.140625)
    rest = rest - turns * np.float32(9.67502593994140625e-4)
    rest = rest - turns * np.float32(1.509957990978376432e-7)
    odd = turns - 2.0 * jnp.floor(turns * 0.5)
    sign = 1.0 - 2.0 * odd
    square = rest * rest
    poly = np.float32(-2.3889859e-08)
    poly = poly * square + np.float32(2.7525562e-06)
    poly = poly * square + np.float32(-1.9840874e-04)
    poly = poly * square + np.float32(8.3333310e-03)
    poly = poly * square + np.float32(-1.6666667e-01)
    return sign * (rest + rest * square * poly)


def refine_kernel(
    sizes,
    images,
    class_in,
    rotation_in,
    defocus_in,
    tables,
    references,
    refined,
    misfit,
    img,
    meta,
    metas,
    crad,
    sq,
    con,
    pick,
    hot,
    hot_t,
    b_own,
    b_send,
    y_got,
    z_own,
    z_send,
    z_got,
    table,
    s_own,
    s_send,
    sy_got,
    sz_own,
    sz_send,
    sz_got,
    s_sum,
    anchor,
    acc,
    mis,
    mis_got,
    send,
    recv,
    send_small,
    recv_small,
    local,
):
    chunks, width, share, side_y, side_z = sizes
    cls = lax.axis_index("cls")
    dp = lax.axis_index("dp")
    z = cls // side_y
    y = cls % side_y
    radii = crad.shape[2]
    half = side_z * share
    cells = side_y * half

    core = dp % 2
    x = dp // 2
    other_core = dp + 1 - 2 * core
    other_x = dp + 2 - 4 * x
    other_y = cls + 1 - 2 * y
    core_mate = (cls, other_core)
    x_mate = (cls, other_x)
    y_mate = (other_y, dp)
    mates = (
        core_mate,
        x_mate,
        (cls, other_x + 1 - 2 * core),
        y_mate,
        (other_y, other_core),
    )
    z_mates = [(((z + k) % side_z) * side_y + y, dp) for k in range(1, side_z)]

    barrier = pltpu.get_barrier_semaphore()
    everyone = list(mates) + z_mates
    for other in everyone:
        pl.semaphore_signal(barrier, inc=1, device_id=other, device_id_type=MESH)

    def remote(source, target, kind, index, device):
        return pltpu.make_async_remote_copy(
            src_ref=source,
            dst_ref=target,
            send_sem=send.at[kind, index],
            recv_sem=recv.at[kind, index],
            device_id=device,
            device_id_type=MESH,
        )

    def small(source, target, index, device):
        return pltpu.make_async_remote_copy(
            src_ref=source,
            dst_ref=target,
            send_sem=send_small.at[index],
            recv_sem=recv_small.at[index],
            device_id=device,
            device_id_type=MESH,
        )

    def share_mate(index):
        family = index % 2
        return (cls + family * (1 - 2 * y), dp + (1 - family) * (2 - 4 * x))

    def sum_mate(index):
        family = index % 2
        return (cls + (1 - family) * (1 - 2 * y), dp + family * (2 - 4 * x))

    def block_rows(block):
        return pl.ds(block * LANES, LANES)

    def columns(index):
        return pl.ds(pl.multiple_of(index * width, width), width)

    def own_copy(index):
        return pltpu.make_async_copy(
            images.at[:, columns(index)], img.at[index, block_rows(0)], local.at[index]
        )

    def core_copy(index):
        return remote(
            images.at[:, columns(index)], img.at[index, block_rows(1)], 0, index, core_mate
        )

    def share_copy(index):
        return remote(
            images.at[:, columns(index)],
            img.at[index, block_rows(2)],
            1,
            index,
            share_mate(index),
        )

    def forward_copy(index):
        return remote(
            img.at[index, block_rows(2)], img.at[index, block_rows(3)], 2, index, core_mate
        )

    def y_copy(index):
        return remote(b_send.at[index], y_got.at[index], 3, index, sum_mate(index))

    def z_copy(index, k):
        return remote(
            z_send.at[index, k - 1], z_got.at[index, k - 1], 3 + k, index, z_mates[k - 1]
        )

    def table_z_copy(index, k):
        rows = pl.ds((side_z - k) * share, share)
        return remote(
            table.at[index, pl.ds(0, share)],
            table.at[index, rows],
            2 + side_z + k,
            index,
            z_mates[k - 1],
        )

    def table_y_copy(index):
        return remote(
            table.at[index, pl.ds(0, half)],
            table.at[index, pl.ds(half, half)],
            2 + 2 * side_z,
            index,
            sum_mate(index),
        )

    def meta_copy(k):
        return small(meta, metas.at[k], k, mates[k])

    def misfit_copy(k):
        return small(mis.at[k], mis_got.at[k], 5 + k, mates[k])

    s_y_copy = small(s_send, sy_got, 10, y_mate)

    def s_z_copy(k):
        return small(sz_send.at[k - 1], sz_got.at[k - 1], 10 + k, z_mates[k - 1])

    anchor_copy = pltpu.make_async_copy(
        references.at[0, pl.ds(pl.multiple_of(dp * share, share), share)],
        anchor,
        local.at[chunks],
    )
    anchor_copy.start()
    pl.loop(0, chunks)(lambda index: own_copy(index).start())
    meta[0:1] = class_in[...].astype(jnp.float32)
    meta[1:2] = rotation_in[...].astype(jnp.float32)
    meta[2:3] = defocus_in[...].astype(jnp.float32)
    meta[3:8] = jnp.zeros((5, LANES), jnp.float32)
    pl.semaphore_wait(barrier, len(everyone))
    for k in range(5):
        meta_copy(k).start()
    for index in range(WINDOW):
        share_copy(index).start()
        core_copy(index).start()

    @pl.loop(0, chunks)
    def pick_radii(index):
        target = tables[pl.ds(8 + index, 1), :width]
        index_rows = lax.broadcasted_iota(jnp.int32, (radii, width), 0).astype(jnp.float32)
        pick[index] = jnp.where(index_rows == target, 1.0, 0.0).astype(jnp.bfloat16)

    z_first = z.astype(jnp.float32)
    y_first = y.astype(jnp.float32)
    x_first = x.astype(jnp.float32)
    core_first = core.astype(jnp.float32)
    cell_rows = lax.broadcasted_iota(jnp.int32, (cells, LANES), 0).astype(jnp.float32)
    cell_lanes = lax.broadcasted_iota(jnp.int32, (LANES, cells), 1).astype(jnp.float32)
    owned = {}
    for source, places in enumerate((((0, 0), (1, 0)), ((0, 1), (1, 1)), ((0, 2),), ((0, 3),), ((1, 2),), ((1, 3),))):
        if source > 0:
            meta_copy(source - 1).wait_recv()
            rows = metas[source - 1]
        else:
            rows = meta[...]
        class_z = jnp.floor(rows[0:1] / float(side_y))
        class_y = rows[0:1] - float(side_y) * class_z
        turn_dp = jnp.floor(rows[1:2] / float(share))
        turn_r = rows[1:2] - float(share) * turn_dp
        turn_x = jnp.floor(turn_dp * 0.5)
        rel_z = class_z - z_first
        rel_z = jnp.where(rel_z < 0.0, rel_z + float(side_z), rel_z)
        off_x = jnp.abs(turn_x - x_first)
        off_y = jnp.abs(class_y - y_first)
        off_core = jnp.abs(turn_dp - 2.0 * turn_x - core_first)
        focus = jnp.transpose(jnp.broadcast_to(rows[2:3], (LANES, LANES)))
        for family, block in places:
            off_share, off_sum = (off_x, off_y) if family == 0 else (off_y, off_x)
            mine = (off_share + off_core) < 0.5
            cell = jnp.where(mine, off_sum * float(half) + rel_z * float(share) + turn_r, -1.0)
            owned[family, block] = mine
            span = slice(block * LANES, (block + 1) * LANES)
            hot[family, :, span] = jnp.where(cell_rows == cell, 1.0, 0.0).astype(jnp.bfloat16)
            cell_t = jnp.transpose(jnp.broadcast_to(cell, (LANES, LANES)))
            hot_t[family, span] = jnp.where(cell_lanes == cell_t, 1.0, 0.0).astype(jnp.bfloat16)
        for part in range(radii // LANES):
            lanes = slice(part * LANES, (part + 1) * LANES)
            phase = 20.0 * focus * tables[0:1, lanes] + 0.1
            wave = bounded_sine(phase) * tables[1:2, lanes]
            for family, block in places:
                span = slice(block * LANES, (block + 1) * LANES)
                crad[family, span, lanes] = wave.astype(jnp.bfloat16)
                if family == 0:
                    sq[span, lanes] = (wave * wave + tables[2:3, lanes]).astype(jnp.bfloat16)
    acc[...] = jnp.zeros_like(acc)
    partial = jnp.dot(hot[0], sq[...], preferred_element_type=jnp.float32)
    s_own[...] = partial[:half]
    s_send[...] = partial[half:].astype(jnp.bfloat16)
    s_y_copy.start()

    def tick(t, carry):
        @pl.when(t == 1)
        def counts_out():
            s_y_copy.wait_recv()
            total = s_own[...] + sy_got[...].astype(jnp.float32)
            sz_own[...] = total[:share]
            for k in range(1, side_z):
                sz_send[k - 1] = total[k * share : (k + 1) * share].astype(jnp.bfloat16)
                s_z_copy(k).start()

        @pl.when((t >= 3) & (t < chunks + 3))
        def sum_y():
            index = t - 3
            y_copy(index).wait_recv()
            total = b_own[index] + y_got[index].astype(jnp.float32)
            z_own[index] = total[:share]
            for k in range(1, side_z):
                z_send[index, k - 1] = total[k * share : (k + 1) * share].astype(jnp.bfloat16)
                z_copy(index, k).start()

        @pl.when(t == 5)
        def counts_in():
            anchor_copy.wait()
            total = sz_own[...]
            for k in range(1, side_z):
                s_z_copy(k).wait_recv()
                total = total + sz_got[k - 1].astype(jnp.float32)
            s_sum[...] = total

        @pl.when((t >= 5) & (t < chunks + 5))
        def update():
            index = t - 5
            total = z_own[index]
            for k in range(1, side_z):
                z_copy(index, k).wait_recv()
                total = total + z_got[index, k - 1].astype(jnp.float32)
            squares = s_sum[...]
            coarse = squares.astype(jnp.bfloat16)
            fine = (squares - coarse.astype(jnp.float32)).astype(jnp.bfloat16)
            pair = jnp.dot(
                jnp.concatenate([coarse, fine], axis=0),
                pick[index],
                preferred_element_type=jnp.float32,
            )
            energy = pair[:share] + pair[share:]
            damping = 0.5 * squares[:, radii - 1 : radii] + 1.0
            scale = 1.0 / damping
            start = anchor[:, columns(index)].astype(jnp.float32)
            first = (start - (start * energy - total) * scale).astype(jnp.bfloat16)
            table[index, 0:share] = first
            for k in range(1, side_z):
                table_z_copy(index, k).start()
            again = first.astype(jnp.float32)
            refined[:, columns(index)] = (again - (again * energy - total) * scale).astype(
                jnp.bfloat16
            )

        @pl.when((t >= 7) & (t < chunks + 7))
        def spread():
            index = t - 7
            for k in range(1, side_z):
                table_z_copy(index, k).wait_recv()
            table_y_copy(index).start()

        @pl.when(t < chunks)
        def contrasts():
            con[t] = jnp.dot(
                crad[t % 2], pick[t], preferred_element_type=jnp.float32
            ).astype(jnp.bfloat16)

        @pl.when(t >= 9)
        def residuals():
            index = t - 9
            table_y_copy(index).wait_recv()
            tiles = jnp.dot(hot_t[index % 2], table[index], preferred_element_type=jnp.float32)
            rest = con[index].astype(jnp.float32) * tiles - img[index].astype(jnp.float32)
            rest = rest * rest
            total = acc[index % 2]
            for part in range(width // LANES):
                total = total + rest[:, part * LANES : (part + 1) * LANES]
            acc[index % 2] = total

        @pl.when(t < chunks)
        def forward():
            share_copy(t).wait_recv()
            forward_copy(t).start()

        @pl.when(t < chunks - WINDOW)
        def start_images():
            share_copy(t + WINDOW).start()
            core_copy(t + WINDOW).start()

        @pl.when((t >= 1) & (t < chunks + 1))
        def partial_sums():
            index = t - 1
            own_copy(index).wait()
            core_copy(index).wait_recv()
            forward_copy(index).wait_recv()
            total = jnp.dot(
                hot[index % 2], con[index] * img[index], preferred_element_type=jnp.float32
            )
            b_own[index] = total[:half]
            b_send[index] = total[half:].astype(jnp.bfloat16)
            y_copy(index).start()

        return carry

    lax.fori_loop(0, chunks + 9, tick, 0)

    def row_of(family, block):
        part = acc[family, block * LANES : (block + 1) * LANES]
        row = jnp.sum(jnp.transpose(part), axis=0, keepdims=True)
        return jnp.where(owned[family, block], row * (1.0 / float(chunks * width)), 0.0)

    for k, row in enumerate(
        (
            row_of(0, 1) + row_of(1, 1),
            row_of(0, 2),
            row_of(0, 3),
            row_of(1, 2),
            row_of(1, 3),
        )
    ):
        mis[k] = jnp.broadcast_to(row, mis.shape[1:])
        misfit_copy(k).start()

    @pl.loop(0, chunks)
    def drain(index):
        core_copy(index).wait_send()
        share_copy(index).wait_send()
        forward_copy(index).wait_send()
        y_copy(index).wait_send()
        for k in range(1, side_z):
            z_copy(index, k).wait_send()
            table_z_copy(index, k).wait_send()
        table_y_copy(index).wait_send()

    s_y_copy.wait_send()
    for k in range(1, side_z):
        s_z_copy(k).wait_send()
    total = row_of(0, 0) + row_of(1, 0)
    for k in range(5):
        meta_copy(k).wait_send()
        misfit_copy(k).wait()
        total = total + mis_got[k, 0:1]
    misfit[...] = total


def shards_close(side_y, side_z, images, defocus, classes, rotations, references):
    count_dp = lax.axis_size("dp")
    rows, pixels = images.shape
    share = references.shape[1] // count_dp
    chunks = CHUNKS
    width = pixels // chunks
    half = side_z * share
    cells = side_y * half
    tables, place = radius_tables(SIDE)
    radii = tables.shape[1]
    constants = np.zeros((8 + chunks, max(radii, width)), np.float32)
    constants[:8, :radii] = tables
    constants[8:, :width] = place.reshape(chunks, width)
    bf16, f32 = jnp.bfloat16, jnp.float32
    kinds = 3 + 2 * side_z
    vmem = pl.BlockSpec(memory_space=pltpu.VMEM)
    anywhere = pl.BlockSpec(memory_space=pltpu.HBM)
    refined, misfit = pl.pallas_call(
        functools.partial(refine_kernel, (chunks, width, share, side_y, side_z)),
        out_shape=(
            jax.ShapeDtypeStruct((share, pixels), bf16),
            jax.ShapeDtypeStruct((1, rows), f32),
        ),
        in_specs=[anywhere, vmem, vmem, vmem, vmem, anywhere],
        out_specs=(vmem, vmem),
        scratch_shapes=[
            pltpu.VMEM((chunks, 4 * rows, width), bf16),
            pltpu.VMEM((8, rows), f32),
            pltpu.VMEM((5, 8, rows), f32),
            pltpu.VMEM((2, 4 * rows, radii), bf16),
            pltpu.VMEM((4 * rows, radii), bf16),
            pltpu.VMEM((chunks, 4 * rows, width), bf16),
            pltpu.VMEM((chunks, radii, width), bf16),
            pltpu.VMEM((2, cells, 4 * rows), bf16),
            pltpu.VMEM((2, 4 * rows, cells), bf16),
            pltpu.VMEM((chunks, half, width), f32),
            pltpu.VMEM((chunks, half, width), bf16),
            pltpu.VMEM((chunks, half, width), bf16),
            pltpu.VMEM((chunks, share, width), f32),
            pltpu.VMEM((chunks, side_z - 1, share, width), bf16),
            pltpu.VMEM((chunks, side_z - 1, share, width), bf16),
            pltpu.VMEM((chunks, cells, width), bf16),
            pltpu.VMEM((half, radii), f32),
            pltpu.VMEM((half, radii), bf16),
            pltpu.VMEM((half, radii), bf16),
            pltpu.VMEM((share, radii), f32),
            pltpu.VMEM((side_z - 1, share, radii), bf16),
            pltpu.VMEM((side_z - 1, share, radii), bf16),
            pltpu.VMEM((share, radii), f32),
            pltpu.VMEM((share, pixels), bf16),
            pltpu.VMEM((2, 4 * rows, LANES), f32),
            pltpu.VMEM((5, 8, rows), f32),
            pltpu.VMEM((5, 8, rows), f32),
            pltpu.SemaphoreType.DMA((kinds, chunks)),
            pltpu.SemaphoreType.DMA((kinds, chunks)),
            pltpu.SemaphoreType.DMA((10 + side_z,)),
            pltpu.SemaphoreType.DMA((10 + side_z,)),
            pltpu.SemaphoreType.DMA((chunks + 1,)),
        ],
        compiler_params=pltpu.CompilerParams(
            collective_id=0, has_side_effects=True, vmem_limit_bytes=63 * 1024 * 1024
        ),
    )(
        images,
        classes.reshape(1, rows),
        rotations.reshape(1, rows),
        defocus.reshape(1, rows),
        jnp.asarray(constants),
        references,
    )
    return refined.reshape(1, share, pixels), misfit.reshape(rows)


def solution(mesh):
    in_specs = (
        P(("cls", "dp"), None),
        P(("cls", "dp")),
        P(("cls", "dp"), None),
        P(("cls", "dp")),
        P("cls", None, None),
    )
    out_specs = (P("cls", "dp", None), P(("cls", "dp")))
    per_device = shards
    if mesh.shape["cls"] == 8 and mesh.shape["dp"] == 4:
        per_device = functools.partial(shards_close, 2, 4)
    return jax.shard_map(
        per_device, mesh=mesh, in_specs=in_specs, out_specs=out_specs, check_vma=False
    )
```

```python
import functools
import jax
import jax.numpy as jnp
import numpy as np
from jax import lax
from jax.experimental import pallas as pl
from jax.experimental.pallas import tpu as pltpu
from jax.sharding import PartitionSpec as P

SIDE = 64
MESH = pl.DeviceIdType.MESH
CHUNKS = 8
WINDOW = 4
LANES = 128


def wave_table(side_count):
    pixel_index = jnp.arange(side_count * side_count, dtype=jnp.int32)
    half_side = side_count // 2
    row_freq = (pixel_index // side_count + half_side) % side_count - half_side
    col_freq = (pixel_index % side_count + half_side) % side_count - half_side
    return (row_freq * row_freq + col_freq * col_freq).astype(jnp.float32) / float(
        half_side * half_side
    )


def contrast(defocus_rows, radius):
    phase = 20.0 * defocus_rows.astype(jnp.float32)[:, None] * radius[None, :] + 0.1
    return -jnp.sin(phase) * jnp.exp(-0.5 * radius)[None, :]


def sweep_rows(table, image_rows, rotation_rows, defocus_rows, radius):
    row_total = image_rows.shape[0]
    block_rows = min(64, row_total)
    block_count = row_total // block_rows
    rotation_count = table.shape[0]
    labels = jnp.arange(rotation_count, dtype=jnp.int32)

    def advance(gradient, block_index):
        row_start = block_index * block_rows
        image_block = lax.dynamic_slice_in_dim(image_rows, row_start, block_rows, 0)
        rotation_block = lax.dynamic_slice_in_dim(rotation_rows, row_start, block_rows, 0)
        defocus_block = lax.dynamic_slice_in_dim(defocus_rows, row_start, block_rows, 0)
        selector = (rotation_block[:, None] == labels[None, :]).astype(jnp.bfloat16)
        tiles = jnp.dot(selector, table, preferred_element_type=jnp.float32)
        contrast_rows = contrast(defocus_block, radius)
        residual = contrast_rows * tiles - image_block.astype(jnp.float32)
        misfit_rows = jnp.mean(residual * residual, axis=1)
        weighted = (contrast_rows * residual).astype(jnp.bfloat16)
        gradient = gradient + lax.dot_general(
            selector, weighted, (((0,), (0,)), ((), ())), preferred_element_type=jnp.float32
        )
        return (gradient, misfit_rows)

    start_grad = jnp.zeros((rotation_count, image_rows.shape[1]), jnp.float32)
    gradient, misfit_blocks = lax.scan(
        advance, start_grad, jnp.arange(block_count, dtype=jnp.int32)
    )
    return (gradient, misfit_blocks.reshape(row_total))


def build_slots(
    images, defocus, rotations, class_rows, class_rank, rank_first, slot_width, count_cls
):
    particle_ids = jnp.arange(images.shape[0], dtype=jnp.int32)
    inside = (class_rank >= rank_first) & (class_rank < rank_first + slot_width)
    slot_of = jnp.where(inside, class_rows * slot_width + class_rank - rank_first, -1)
    slot_ids = jnp.arange(count_cls * slot_width, dtype=jnp.int32)
    slot_match = slot_ids[:, None] == slot_of[None, :]
    slot_live = jnp.any(slot_match, axis=1)
    slot_source = jnp.sum(jnp.where(slot_match, particle_ids[None, :], 0), axis=1)
    send_images = jnp.where(
        slot_live[:, None], jnp.take(images, slot_source, axis=0), jnp.zeros((), jnp.bfloat16)
    )
    send_rotation = jnp.where(slot_live, jnp.take(rotations, slot_source), -1)
    send_defocus = jnp.where(
        slot_live, jnp.take(defocus, slot_source).astype(jnp.float32), 0.0
    ).astype(jnp.bfloat16)
    return (send_images, send_rotation, send_defocus)


def shards(images, defocus, classes, rotations, references):
    count_cls = lax.axis_size("cls")
    count_dp = lax.axis_size("dp")
    particle_count = images.shape[0]
    pixel_count = images.shape[1]
    rotation_count = references.shape[1]
    capacity = max(2, 2 * particle_count // count_cls)
    slot_count = count_cls * capacity
    radius = wave_table(SIDE)
    class_rows = classes[:, 0]
    particle_ids = jnp.arange(particle_count, dtype=jnp.int32)
    earlier_same = (class_rows[:, None] == class_rows[None, :]) & (
        particle_ids[None, :] < particle_ids[:, None]
    )
    class_rank = jnp.sum(earlier_same.astype(jnp.int32), axis=1)
    slot_of = class_rows * capacity + class_rank
    slot_ids = jnp.arange(slot_count, dtype=jnp.int32)
    slot_match = slot_ids[:, None] == slot_of[None, :]
    send_images, send_rotation, send_defocus = build_slots(
        images, defocus, rotations, class_rows, class_rank, 0, capacity, count_cls
    )
    recv_images, recv_rotation, recv_defocus = (
        lax.all_to_all(
            send_images.reshape(count_cls, capacity, pixel_count),
            "cls",
            split_axis=0,
            concat_axis=0,
            tiled=True,
        ),
        lax.all_to_all(
            send_rotation.astype(jnp.bfloat16).reshape(count_cls, capacity),
            "cls",
            split_axis=0,
            concat_axis=0,
            tiled=True,
        ),
        lax.all_to_all(
            send_defocus.reshape(count_cls, capacity),
            "cls",
            split_axis=0,
            concat_axis=0,
            tiled=True,
        ),
    )
    image_slots = recv_images.reshape(slot_count, pixel_count)
    rotation_slots = recv_rotation.reshape(slot_count).astype(jnp.int32)
    defocus_slots = recv_defocus.reshape(slot_count)
    labels = jnp.arange(rotation_count, dtype=jnp.int32)
    local_counts = jnp.sum((rotation_slots[:, None] == labels[None, :]).astype(jnp.float32), axis=0)
    counts = lax.psum(local_counts, "dp")
    damping = 0.5 * counts + 1.0
    table = references[0]
    grad_first, unused_first = sweep_rows(table, image_slots, rotation_slots, defocus_slots, radius)
    share_rows = rotation_count // count_dp
    share_start = lax.axis_index("dp") * share_rows
    damping_share = lax.dynamic_slice_in_dim(damping, share_start, share_rows, 0)
    grad_share = lax.psum_scatter(
        grad_first.astype(jnp.bfloat16), "dp", scatter_dimension=0, tiled=True
    ).astype(jnp.float32)
    anchor = lax.dynamic_slice_in_dim(table, share_start, share_rows, 0).astype(jnp.float32)
    fresh_share = (anchor - grad_share / damping_share[:, None]).astype(jnp.bfloat16)
    table_next = lax.all_gather(fresh_share, "dp", axis=0, tiled=True)
    grad_second, misfit_slots = sweep_rows(
        table_next, image_slots, rotation_slots, defocus_slots, radius
    )
    second_share = lax.psum_scatter(
        grad_second.astype(jnp.bfloat16), "dp", scatter_dimension=0, tiled=True
    ).astype(jnp.float32)
    anchor_next = lax.dynamic_slice_in_dim(table_next, share_start, share_rows, 0).astype(
        jnp.float32
    )
    refined = (anchor_next - second_share / damping_share[:, None]).astype(jnp.bfloat16)
    returned = lax.all_to_all(
        misfit_slots.reshape(count_cls, capacity), "cls", split_axis=0, concat_axis=0, tiled=True
    )
    returned_slots = returned.reshape(slot_count)
    misfit = jnp.sum(jnp.where(slot_match, returned_slots[:, None], 0.0), axis=0)
    return (refined.reshape(1, share_rows, pixel_count), misfit)


def radius_tables(side_count):
    half_side = side_count // 2
    freq = (np.arange(side_count) + half_side) % side_count - half_side
    square = (freq[:, None] ** 2 + freq[None, :] ** 2).reshape(-1)
    values, place = np.unique(square, return_inverse=True)
    width = -(-(len(values) + 1) // LANES) * LANES
    rows = np.zeros((8, width), np.float32)
    rows[0, : len(values)] = values.astype(np.float32) / np.float32(half_side * half_side)
    rows[1, : len(values)] = -np.exp(-0.5 * rows[0, : len(values)])
    rows[2, width - 1] = 1.0
    return rows, place.reshape(1, -1).astype(np.float32)


def bounded_sine(angle):
    turns = jnp.floor(angle * np.float32(1.0 / np.pi) + 0.5)
    rest = angle - turns * np.float32(3.140625)
    rest = rest - turns * np.float32(9.67502593994140625e-4)
    rest = rest - turns * np.float32(1.509957990978376432e-7)
    odd = turns - 2.0 * jnp.floor(turns * 0.5)
    sign = 1.0 - 2.0 * odd
    square = rest * rest
    poly = np.float32(-2.3889859e-08)
    poly = poly * square + np.float32(2.7525562e-06)
    poly = poly * square + np.float32(-1.9840874e-04)
    poly = poly * square + np.float32(8.3333310e-03)
    poly = poly * square + np.float32(-1.6666667e-01)
    return sign * (rest + rest * square * poly)


def refine_kernel(
    sizes,
    images,
    class_in,
    rotation_in,
    defocus_in,
    tables,
    references,
    refined,
    misfit,
    img,
    meta,
    metas,
    crad,
    sq,
    con,
    pick,
    hot,
    hot_t,
    b_own,
    b_send,
    y_got,
    z_own,
    z_send,
    z_got,
    table,
    s_own,
    s_send,
    sy_got,
    sz_own,
    sz_send,
    sz_got,
    s_sum,
    anchor,
    acc,
    mis,
    mis_got,
    send,
    recv,
    send_small,
    recv_small,
    local,
):
    chunks, width, share, side_y, side_z = sizes
    cls = lax.axis_index("cls")
    dp = lax.axis_index("dp")
    z = cls // side_y
    y = cls % side_y
    radii = crad.shape[2]
    half = side_z * share
    cells = side_y * half

    core = dp % 2
    x = dp // 2
    other_core = dp + 1 - 2 * core
    other_x = dp + 2 - 4 * x
    other_y = cls + 1 - 2 * y
    core_mate = (cls, other_core)
    x_mate = (cls, other_x)
    y_mate = (other_y, dp)
    mates = (
        core_mate,
        x_mate,
        (cls, other_x + 1 - 2 * core),
        y_mate,
        (other_y, other_core),
    )
    z_mates = [(((z + k) % side_z) * side_y + y, dp) for k in range(1, side_z)]

    barrier = pltpu.get_barrier_semaphore()
    everyone = list(mates) + z_mates
    for other in everyone:
        pl.semaphore_signal(barrier, inc=1, device_id=other, device_id_type=MESH)

    def remote(source, target, kind, index, device):
        return pltpu.make_async_remote_copy(
            src_ref=source,
            dst_ref=target,
            send_sem=send.at[kind, index],
            recv_sem=recv.at[kind, index],
            device_id=device,
            device_id_type=MESH,
        )

    def small(source, target, index, device):
        return pltpu.make_async_remote_copy(
            src_ref=source,
            dst_ref=target,
            send_sem=send_small.at[index],
            recv_sem=recv_small.at[index],
            device_id=device,
            device_id_type=MESH,
        )

    def share_mate(index):
        family = index % 2
        return (cls + family * (1 - 2 * y), dp + (1 - family) * (2 - 4 * x))

    def sum_mate(index):
        family = index % 2
        return (cls + (1 - family) * (1 - 2 * y), dp + family * (2 - 4 * x))

    def block_rows(block):
        return pl.ds(block * LANES, LANES)

    def columns(index):
        return pl.ds(pl.multiple_of(index * width, width), width)

    def own_copy(index):
        return pltpu.make_async_copy(
            images.at[:, columns(index)], img.at[index, block_rows(0)], local.at[index]
        )

    def core_copy(index):
        return remote(
            images.at[:, columns(index)], img.at[index, block_rows(1)], 0, index, core_mate
        )

    def share_copy(index):
        return remote(
            images.at[:, columns(index)],
            img.at[index, block_rows(2)],
            1,
            index,
            share_mate(index),
        )

    def forward_copy(index):
        return remote(
            img.at[index, block_rows(2)], img.at[index, block_rows(3)], 2, index, core_mate
        )

    def y_copy(index):
        return remote(b_send.at[index], y_got.at[index], 3, index, sum_mate(index))

    def z_copy(index, k):
        return remote(
            z_send.at[index, k - 1], z_got.at[index, k - 1], 3 + k, index, z_mates[k - 1]
        )

    def table_z_copy(index, k):
        rows = pl.ds((side_z - k) * share, share)
        return remote(
            table.at[index, pl.ds(0, share)],
            table.at[index, rows],
            2 + side_z + k,
            index,
            z_mates[k - 1],
        )

    def table_y_copy(index):
        return remote(
            table.at[index, pl.ds(0, half)],
            table.at[index, pl.ds(half, half)],
            2 + 2 * side_z,
            index,
            sum_mate(index),
        )

    def meta_copy(k):
        return small(meta, metas.at[k], k, mates[k])

    def misfit_copy(k):
        return small(mis.at[k], mis_got.at[k], 5 + k, mates[k])

    s_y_copy = small(s_send, sy_got, 10, y_mate)

    def s_z_copy(k):
        return small(sz_send.at[k - 1], sz_got.at[k - 1], 10 + k, z_mates[k - 1])

    anchor_copy = pltpu.make_async_copy(
        references.at[0, pl.ds(pl.multiple_of(dp * share, share), share)],
        anchor,
        local.at[chunks],
    )
    anchor_copy.start()

    @pl.loop(0, chunks)
    def start_local(index):
        own_copy(index).start()

    meta[0:1] = class_in[...].astype(jnp.float32)
    meta[1:2] = rotation_in[...].astype(jnp.float32)
    meta[2:3] = defocus_in[...].astype(jnp.float32)
    meta[3:8] = jnp.zeros((5, LANES), jnp.float32)
    pl.semaphore_wait(barrier, len(everyone))
    for k in range(5):
        meta_copy(k).start()
    for index in range(WINDOW):
        share_copy(index).start()
        core_copy(index).start()

    index_rows = lax.broadcasted_iota(jnp.int32, (LANES, LANES), 0).astype(jnp.float32)

    @pl.loop(0, chunks)
    def pick_radii(index):
        row = tables[pl.ds(8 + index, 1), :width]
        for part in range(width // LANES):
            lanes = slice(part * LANES, (part + 1) * LANES)
            target = jnp.broadcast_to(row[:, lanes], (LANES, LANES))
            for block in range(radii // LANES):
                match = index_rows == target - float(block * LANES)
                pick[index, block * LANES : (block + 1) * LANES, lanes] = jnp.where(
                    match, 1.0, 0.0
                ).astype(jnp.bfloat16)

    z_first = z.astype(jnp.float32)
    y_first = y.astype(jnp.float32)
    x_first = x.astype(jnp.float32)
    core_first = core.astype(jnp.float32)
    cell_rows = lax.broadcasted_iota(jnp.int32, (cells, LANES), 0).astype(jnp.float32)
    cell_lanes = lax.broadcasted_iota(jnp.int32, (LANES, cells), 1).astype(jnp.float32)
    owned = {}
    for source, places in enumerate((((0, 0), (1, 0)), ((0, 1), (1, 1)), ((0, 2),), ((0, 3),), ((1, 2),), ((1, 3),))):
        if source > 0:
            meta_copy(source - 1).wait_recv()
            rows = metas[source - 1]
        else:
            rows = meta[...]
        class_z = jnp.floor(rows[0:1] / float(side_y))
        class_y = rows[0:1] - float(side_y) * class_z
        turn_dp = jnp.floor(rows[1:2] / float(share))
        turn_r = rows[1:2] - float(share) * turn_dp
        turn_x = jnp.floor(turn_dp * 0.5)
        rel_z = class_z - z_first
        rel_z = jnp.where(rel_z < 0.0, rel_z + float(side_z), rel_z)
        off_x = jnp.abs(turn_x - x_first)
        off_y = jnp.abs(class_y - y_first)
        off_core = jnp.abs(turn_dp - 2.0 * turn_x - core_first)
        focus = jnp.transpose(jnp.broadcast_to(rows[2:3], (LANES, LANES)))
        for family, block in places:
            off_share, off_sum = (off_x, off_y) if family == 0 else (off_y, off_x)
            mine = (off_share + off_core) < 0.5
            cell = jnp.where(mine, off_sum * float(half) + rel_z * float(share) + turn_r, -1.0)
            owned[family, block] = mine
            span = slice(block * LANES, (block + 1) * LANES)
            hot[family, :, span] = jnp.where(cell_rows == cell, 1.0, 0.0).astype(jnp.bfloat16)
            cell_t = jnp.transpose(jnp.broadcast_to(cell, (LANES, LANES)))
            hot_t[family, span] = jnp.where(cell_lanes == cell_t, 1.0, 0.0).astype(jnp.bfloat16)
        for part in range(radii // LANES):
            lanes = slice(part * LANES, (part + 1) * LANES)
            phase = 20.0 * focus * tables[0:1, lanes] + 0.1
            wave = bounded_sine(phase) * tables[1:2, lanes]
            for family, block in places:
                span = slice(block * LANES, (block + 1) * LANES)
                crad[family, span, lanes] = wave.astype(jnp.bfloat16)
                if family == 0:
                    sq[span, lanes] = (wave * wave + tables[2:3, lanes]).astype(jnp.bfloat16)
    acc[...] = jnp.zeros_like(acc)
    partial = jnp.dot(hot[0], sq[...], preferred_element_type=jnp.float32)
    s_own[...] = partial[:half]
    s_send[...] = partial[half:].astype(jnp.bfloat16)
    s_y_copy.start()

    def tick(t, carry):
        @pl.when(t == 1)
        def counts_out():
            s_y_copy.wait_recv()
            total = s_own[...] + sy_got[...].astype(jnp.float32)
            sz_own[...] = total[:share]
            for k in range(1, side_z):
                sz_send[k - 1] = total[k * share : (k + 1) * share].astype(jnp.bfloat16)
                s_z_copy(k).start()

        @pl.when((t >= 3) & (t < chunks + 3))
        def sum_y():
            index = t - 3
            y_copy(index).wait_recv()
            total = b_own[index] + y_got[index].astype(jnp.float32)
            z_own[index] = total[:share]
            for k in range(1, side_z):
                z_send[index, k - 1] = total[k * share : (k + 1) * share].astype(jnp.bfloat16)
                z_copy(index, k).start()

        @pl.when(t == 5)
        def counts_in():
            anchor_copy.wait()
            total = sz_own[...]
            for k in range(1, side_z):
                s_z_copy(k).wait_recv()
                total = total + sz_got[k - 1].astype(jnp.float32)
            s_sum[...] = total

        @pl.when((t >= 5) & (t < chunks + 5))
        def update():
            index = t - 5
            total = z_own[index]
            for k in range(1, side_z):
                z_copy(index, k).wait_recv()
                total = total + z_got[index, k - 1].astype(jnp.float32)
            squares = s_sum[...]
            coarse = squares.astype(jnp.bfloat16)
            fine = (squares - coarse.astype(jnp.float32)).astype(jnp.bfloat16)
            pair = jnp.dot(
                jnp.concatenate([coarse, fine], axis=0),
                pick[index],
                preferred_element_type=jnp.float32,
            )
            energy = pair[:share] + pair[share:]
            damping = 0.5 * squares[:, radii - 1 : radii] + 1.0
            scale = 1.0 / damping
            start = anchor[:, columns(index)].astype(jnp.float32)
            first = (start - (start * energy - total) * scale).astype(jnp.bfloat16)
            table[index, 0:share] = first
            for k in range(1, side_z):
                table_z_copy(index, k).start()
            again = first.astype(jnp.float32)
            refined[:, columns(index)] = again - (again * energy - total) * scale

        @pl.when((t >= 7) & (t < chunks + 7))
        def spread():
            index = t - 7
            for k in range(1, side_z):
                table_z_copy(index, k).wait_recv()
            table_y_copy(index).start()

        @pl.when(t < chunks)
        def contrasts():
            for block in range(2):
                span = pl.ds(2 * block * LANES, 2 * LANES)
                con[t, span] = jnp.dot(
                    crad[t % 2, span], pick[t], preferred_element_type=jnp.float32
                ).astype(jnp.bfloat16)

        @pl.when(t >= 9)
        def residuals():
            index = t - 9
            table_y_copy(index).wait_recv()
            for block in range(4):
                span = block_rows(block)
                tiles = jnp.dot(
                    hot_t[index % 2, span], table[index], preferred_element_type=jnp.float32
                )
                total = acc[index % 2, span]
                for part in range(width // LANES):
                    lanes = slice(part * LANES, (part + 1) * LANES)
                    rest = con[index, span, lanes].astype(jnp.float32) * tiles[:, lanes]
                    rest = rest - img[index, span, lanes].astype(jnp.float32)
                    total = total + rest * rest
                acc[index % 2, span] = total

        @pl.when(t < chunks)
        def forward():
            share_copy(t).wait_recv()
            forward_copy(t).start()

        @pl.when(t < chunks - WINDOW)
        def start_images():
            share_copy(t + WINDOW).start()
            core_copy(t + WINDOW).start()

        @pl.when((t >= 1) & (t < chunks + 1))
        def partial_sums():
            index = t - 1
            own_copy(index).wait()
            core_copy(index).wait_recv()
            forward_copy(index).wait_recv()
            total = jnp.dot(
                hot[index % 2], con[index] * img[index], preferred_element_type=jnp.float32
            )
            b_own[index] = total[:half]
            b_send[index] = total[half:].astype(jnp.bfloat16)
            y_copy(index).start()

        return carry

    lax.fori_loop(0, chunks + 9, tick, 0)

    def row_of(family, block):
        part = acc[family, block * LANES : (block + 1) * LANES]
        row = jnp.sum(jnp.transpose(part), axis=0, keepdims=True)
        return jnp.where(owned[family, block], row * (1.0 / float(chunks * width)), 0.0)

    for k, row in enumerate(
        (
            row_of(0, 1) + row_of(1, 1),
            row_of(0, 2),
            row_of(0, 3),
            row_of(1, 2),
            row_of(1, 3),
        )
    ):
        mis[k] = jnp.broadcast_to(row, mis.shape[1:])
        misfit_copy(k).start()

    @pl.loop(0, chunks)
    def drain(index):
        core_copy(index).wait_send()
        share_copy(index).wait_send()
        forward_copy(index).wait_send()
        y_copy(index).wait_send()
        for k in range(1, side_z):
            z_copy(index, k).wait_send()
            table_z_copy(index, k).wait_send()
        table_y_copy(index).wait_send()

    s_y_copy.wait_send()
    for k in range(1, side_z):
        s_z_copy(k).wait_send()
    total = row_of(0, 0) + row_of(1, 0)
    for k in range(5):
        meta_copy(k).wait_send()
        misfit_copy(k).wait()
        total = total + mis_got[k, 0:1]
    misfit[...] = total


def shards_close(side_y, side_z, images, defocus, classes, rotations, references):
    count_dp = lax.axis_size("dp")
    rows, pixels = images.shape
    share = references.shape[1] // count_dp
    chunks = CHUNKS
    width = pixels // chunks
    half = side_z * share
    cells = side_y * half
    tables, place = radius_tables(SIDE)
    radii = tables.shape[1]
    constants = np.zeros((8 + chunks, max(radii, width)), np.float32)
    constants[:8, :radii] = tables
    constants[8:, :width] = place.reshape(chunks, width)
    bf16, f32 = jnp.bfloat16, jnp.float32
    kinds = 3 + 2 * side_z
    vmem = pl.BlockSpec(memory_space=pltpu.VMEM)
    anywhere = pl.BlockSpec(memory_space=pltpu.HBM)
    refined, misfit = pl.pallas_call(
        functools.partial(refine_kernel, (chunks, width, share, side_y, side_z)),
        out_shape=(
            jax.ShapeDtypeStruct((share, pixels), f32),
            jax.ShapeDtypeStruct((1, rows), f32),
        ),
        in_specs=[anywhere, vmem, vmem, vmem, vmem, anywhere],
        out_specs=(vmem, vmem),
        scratch_shapes=[
            pltpu.VMEM((chunks, 4 * rows, width), bf16),
            pltpu.VMEM((8, rows), f32),
            pltpu.VMEM((5, 8, rows), f32),
            pltpu.VMEM((2, 4 * rows, radii), bf16),
            pltpu.VMEM((4 * rows, radii), bf16),
            pltpu.VMEM((chunks, 4 * rows, width), bf16),
            pltpu.VMEM((chunks, radii, width), bf16),
            pltpu.VMEM((2, cells, 4 * rows), bf16),
            pltpu.VMEM((2, 4 * rows, cells), bf16),
            pltpu.VMEM((chunks, half, width), f32),
            pltpu.VMEM((chunks, half, width), bf16),
            pltpu.VMEM((chunks, half, width), bf16),
            pltpu.VMEM((chunks, share, width), f32),
            pltpu.VMEM((chunks, side_z - 1, share, width), bf16),
            pltpu.VMEM((chunks, side_z - 1, share, width), bf16),
            pltpu.VMEM((chunks, cells, width), bf16),
            pltpu.VMEM((half, radii), f32),
            pltpu.VMEM((half, radii), bf16),
            pltpu.VMEM((half, radii), bf16),
            pltpu.VMEM((share, radii), f32),
            pltpu.VMEM((side_z - 1, share, radii), bf16),
            pltpu.VMEM((side_z - 1, share, radii), bf16),
            pltpu.VMEM((share, radii), f32),
            pltpu.VMEM((share, pixels), bf16),
            pltpu.VMEM((2, 4 * rows, LANES), f32),
            pltpu.VMEM((5, 8, rows), f32),
            pltpu.VMEM((5, 8, rows), f32),
            pltpu.SemaphoreType.DMA((kinds, chunks)),
            pltpu.SemaphoreType.DMA((kinds, chunks)),
            pltpu.SemaphoreType.DMA((10 + side_z,)),
            pltpu.SemaphoreType.DMA((10 + side_z,)),
            pltpu.SemaphoreType.DMA((chunks + 1,)),
        ],
        compiler_params=pltpu.CompilerParams(
            collective_id=0, has_side_effects=True, vmem_limit_bytes=63 * 1024 * 1024
        ),
    )(
        images,
        classes.reshape(1, rows),
        rotations.reshape(1, rows),
        defocus.reshape(1, rows),
        jnp.asarray(constants),
        references,
    )
    return refined.astype(bf16).reshape(1, share, pixels), misfit.reshape(rows)


def solution(mesh):
    in_specs = (
        P(("cls", "dp"), None),
        P(("cls", "dp")),
        P(("cls", "dp"), None),
        P(("cls", "dp")),
        P("cls", None, None),
    )
    out_specs = (P("cls", "dp", None), P(("cls", "dp")))
    per_device = shards
    if mesh.shape["cls"] == 8 and mesh.shape["dp"] == 4:
        per_device = functools.partial(shards_close, 2, 4)
    return jax.shard_map(
        per_device, mesh=mesh, in_specs=in_specs, out_specs=out_specs, check_vma=False
    )
```

```python
import functools
import jax
import jax.numpy as jnp
import numpy as np
from jax import lax
from jax.experimental import pallas as pl
from jax.experimental.pallas import tpu as pltpu
from jax.sharding import PartitionSpec as P

SIDE = 64
MESH = pl.DeviceIdType.MESH
CHUNKS = 8
WINDOW = 4
FAMILIES = 1
SINE = (
    6.283182792843448,
    -41.341419333015786,
    81.59613740878902,
    -76.57967400034848,
    41.203682075135006,
    -12.268761447374176,
)
LANES = 128


def wave_table(side_count):
    pixel_index = jnp.arange(side_count * side_count, dtype=jnp.int32)
    half_side = side_count // 2
    row_freq = (pixel_index // side_count + half_side) % side_count - half_side
    col_freq = (pixel_index % side_count + half_side) % side_count - half_side
    return (row_freq * row_freq + col_freq * col_freq).astype(jnp.float32) / float(
        half_side * half_side
    )


def contrast(defocus_rows, radius):
    phase = 20.0 * defocus_rows.astype(jnp.float32)[:, None] * radius[None, :] + 0.1
    return -jnp.sin(phase) * jnp.exp(-0.5 * radius)[None, :]


def sweep_rows(table, image_rows, rotation_rows, defocus_rows, radius):
    row_total = image_rows.shape[0]
    block_rows = min(64, row_total)
    block_count = row_total // block_rows
    rotation_count = table.shape[0]
    labels = jnp.arange(rotation_count, dtype=jnp.int32)

    def advance(gradient, block_index):
        row_start = block_index * block_rows
        image_block = lax.dynamic_slice_in_dim(image_rows, row_start, block_rows, 0)
        rotation_block = lax.dynamic_slice_in_dim(rotation_rows, row_start, block_rows, 0)
        defocus_block = lax.dynamic_slice_in_dim(defocus_rows, row_start, block_rows, 0)
        selector = (rotation_block[:, None] == labels[None, :]).astype(jnp.bfloat16)
        tiles = jnp.dot(selector, table, preferred_element_type=jnp.float32)
        contrast_rows = contrast(defocus_block, radius)
        residual = contrast_rows * tiles - image_block.astype(jnp.float32)
        misfit_rows = jnp.mean(residual * residual, axis=1)
        weighted = (contrast_rows * residual).astype(jnp.bfloat16)
        gradient = gradient + lax.dot_general(
            selector, weighted, (((0,), (0,)), ((), ())), preferred_element_type=jnp.float32
        )
        return (gradient, misfit_rows)

    start_grad = jnp.zeros((rotation_count, image_rows.shape[1]), jnp.float32)
    gradient, misfit_blocks = lax.scan(
        advance, start_grad, jnp.arange(block_count, dtype=jnp.int32)
    )
    return (gradient, misfit_blocks.reshape(row_total))


def build_slots(
    images, defocus, rotations, class_rows, class_rank, rank_first, slot_width, count_cls
):
    particle_ids = jnp.arange(images.shape[0], dtype=jnp.int32)
    inside = (class_rank >= rank_first) & (class_rank < rank_first + slot_width)
    slot_of = jnp.where(inside, class_rows * slot_width + class_rank - rank_first, -1)
    slot_ids = jnp.arange(count_cls * slot_width, dtype=jnp.int32)
    slot_match = slot_ids[:, None] == slot_of[None, :]
    slot_live = jnp.any(slot_match, axis=1)
    slot_source = jnp.sum(jnp.where(slot_match, particle_ids[None, :], 0), axis=1)
    send_images = jnp.where(
        slot_live[:, None], jnp.take(images, slot_source, axis=0), jnp.zeros((), jnp.bfloat16)
    )
    send_rotation = jnp.where(slot_live, jnp.take(rotations, slot_source), -1)
    send_defocus = jnp.where(
        slot_live, jnp.take(defocus, slot_source).astype(jnp.float32), 0.0
    ).astype(jnp.bfloat16)
    return (send_images, send_rotation, send_defocus)


def shards(images, defocus, classes, rotations, references):
    count_cls = lax.axis_size("cls")
    count_dp = lax.axis_size("dp")
    particle_count = images.shape[0]
    pixel_count = images.shape[1]
    rotation_count = references.shape[1]
    capacity = max(2, 2 * particle_count // count_cls)
    slot_count = count_cls * capacity
    radius = wave_table(SIDE)
    class_rows = classes[:, 0]
    particle_ids = jnp.arange(particle_count, dtype=jnp.int32)
    earlier_same = (class_rows[:, None] == class_rows[None, :]) & (
        particle_ids[None, :] < particle_ids[:, None]
    )
    class_rank = jnp.sum(earlier_same.astype(jnp.int32), axis=1)
    slot_of = class_rows * capacity + class_rank
    slot_ids = jnp.arange(slot_count, dtype=jnp.int32)
    slot_match = slot_ids[:, None] == slot_of[None, :]
    send_images, send_rotation, send_defocus = build_slots(
        images, defocus, rotations, class_rows, class_rank, 0, capacity, count_cls
    )
    recv_images, recv_rotation, recv_defocus = (
        lax.all_to_all(
            send_images.reshape(count_cls, capacity, pixel_count),
            "cls",
            split_axis=0,
            concat_axis=0,
            tiled=True,
        ),
        lax.all_to_all(
            send_rotation.astype(jnp.bfloat16).reshape(count_cls, capacity),
            "cls",
            split_axis=0,
            concat_axis=0,
            tiled=True,
        ),
        lax.all_to_all(
            send_defocus.reshape(count_cls, capacity),
            "cls",
            split_axis=0,
            concat_axis=0,
            tiled=True,
        ),
    )
    image_slots = recv_images.reshape(slot_count, pixel_count)
    rotation_slots = recv_rotation.reshape(slot_count).astype(jnp.int32)
    defocus_slots = recv_defocus.reshape(slot_count)
    labels = jnp.arange(rotation_count, dtype=jnp.int32)
    local_counts = jnp.sum((rotation_slots[:, None] == labels[None, :]).astype(jnp.float32), axis=0)
    counts = lax.psum(local_counts, "dp")
    damping = 0.5 * counts + 1.0
    table = references[0]
    grad_first, unused_first = sweep_rows(table, image_slots, rotation_slots, defocus_slots, radius)
    share_rows = rotation_count // count_dp
    share_start = lax.axis_index("dp") * share_rows
    damping_share = lax.dynamic_slice_in_dim(damping, share_start, share_rows, 0)
    grad_share = lax.psum_scatter(
        grad_first.astype(jnp.bfloat16), "dp", scatter_dimension=0, tiled=True
    ).astype(jnp.float32)
    anchor = lax.dynamic_slice_in_dim(table, share_start, share_rows, 0).astype(jnp.float32)
    fresh_share = (anchor - grad_share / damping_share[:, None]).astype(jnp.bfloat16)
    table_next = lax.all_gather(fresh_share, "dp", axis=0, tiled=True)
    grad_second, misfit_slots = sweep_rows(
        table_next, image_slots, rotation_slots, defocus_slots, radius
    )
    second_share = lax.psum_scatter(
        grad_second.astype(jnp.bfloat16), "dp", scatter_dimension=0, tiled=True
    ).astype(jnp.float32)
    anchor_next = lax.dynamic_slice_in_dim(table_next, share_start, share_rows, 0).astype(
        jnp.float32
    )
    refined = (anchor_next - second_share / damping_share[:, None]).astype(jnp.bfloat16)
    returned = lax.all_to_all(
        misfit_slots.reshape(count_cls, capacity), "cls", split_axis=0, concat_axis=0, tiled=True
    )
    returned_slots = returned.reshape(slot_count)
    misfit = jnp.sum(jnp.where(slot_match, returned_slots[:, None], 0.0), axis=0)
    return (refined.reshape(1, share_rows, pixel_count), misfit)


def radius_tables(side_count):
    half_side = side_count // 2
    freq = (np.arange(side_count) + half_side) % side_count - half_side
    square = (freq[:, None] ** 2 + freq[None, :] ** 2).reshape(-1)
    values, place = np.unique(square, return_inverse=True)
    width = -(-(len(values) + 1) // LANES) * LANES
    rows = np.zeros((8, width), np.float32)
    rows[0, : len(values)] = values.astype(np.float32) / np.float32(half_side * half_side)
    rows[1, : len(values)] = -np.exp(-0.5 * rows[0, : len(values)])
    rows[0] = (rows[0].astype(np.float64) * (10.0 / np.pi)).astype(np.float32)
    rows[2, width - 1] = 1.0
    return rows, place.reshape(1, -1).astype(np.float32)


def sine_of_turns(turns):
    rest = turns - jnp.floor(turns + 0.5)
    square = rest * rest
    poly = np.float32(SINE[-1])
    for term in SINE[-2::-1]:
        poly = poly * square + np.float32(term)
    return rest * poly


def refine_kernel(
    sizes,
    images,
    class_in,
    rotation_in,
    defocus_in,
    tables,
    references,
    refined,
    misfit,
    img,
    meta,
    metas,
    crad,
    sq,
    con,
    pick,
    hot,
    hot_t,
    b_own,
    b_send,
    y_got,
    z_own,
    z_send,
    z_got,
    table,
    s_own,
    s_send,
    sy_got,
    sz_own,
    sz_send,
    sz_got,
    s_sum,
    anchor,
    acc,
    mis,
    mis_got,
    send,
    recv,
    send_small,
    recv_small,
    local,
):
    chunks, width, share, side_y, side_z = sizes
    cls = lax.axis_index("cls")
    dp = lax.axis_index("dp")
    z = cls // side_y
    y = cls % side_y
    radii = crad.shape[2]
    half = side_z * share
    cells = side_y * half

    core = dp % 2
    x = dp // 2
    other_core = dp + 1 - 2 * core
    other_x = dp + 2 - 4 * x
    other_y = cls + 1 - 2 * y
    core_mate = (cls, other_core)
    x_mate = (cls, other_x)
    y_mate = (other_y, dp)
    mates = (
        core_mate,
        x_mate,
        (cls, other_x + 1 - 2 * core),
        y_mate,
        (other_y, other_core),
    )
    z_mates = [(((z + k) % side_z) * side_y + y, dp) for k in range(1, side_z)]

    barrier = pltpu.get_barrier_semaphore()
    friends = 1 + 2 * FAMILIES
    everyone = list(mates[:friends]) + z_mates
    if FAMILIES == 1:
        everyone.append(y_mate)
    for other in everyone:
        pl.semaphore_signal(barrier, inc=1, device_id=other, device_id_type=MESH)

    def remote(source, target, kind, index, device):
        return pltpu.make_async_remote_copy(
            src_ref=source,
            dst_ref=target,
            send_sem=send.at[kind, index],
            recv_sem=recv.at[kind, index],
            device_id=device,
            device_id_type=MESH,
        )

    def small(source, target, index, device):
        return pltpu.make_async_remote_copy(
            src_ref=source,
            dst_ref=target,
            send_sem=send_small.at[index],
            recv_sem=recv_small.at[index],
            device_id=device,
            device_id_type=MESH,
        )

    def share_mate(index):
        family = index % FAMILIES
        return (cls + family * (1 - 2 * y), dp + (1 - family) * (2 - 4 * x))

    def sum_mate(index):
        family = index % FAMILIES
        return (cls + (1 - family) * (1 - 2 * y), dp + family * (2 - 4 * x))

    def block_rows(block):
        return pl.ds(block * LANES, LANES)

    def columns(index):
        return pl.ds(pl.multiple_of(index * width, width), width)

    def own_copy(index):
        return pltpu.make_async_copy(
            images.at[:, columns(index)], img.at[index, block_rows(0)], local.at[index]
        )

    def core_copy(index):
        return remote(
            images.at[:, columns(index)], img.at[index, block_rows(1)], 0, index, core_mate
        )

    def share_copy(index):
        return remote(
            images.at[:, columns(index)],
            img.at[index, block_rows(2)],
            1,
            index,
            share_mate(index),
        )

    def forward_copy(index):
        return remote(
            img.at[index, block_rows(2)], img.at[index, block_rows(3)], 2, index, core_mate
        )

    def y_copy(index):
        return remote(b_send.at[index], y_got.at[index], 3, index, sum_mate(index))

    def z_copy(index, k):
        return remote(
            z_send.at[index, k - 1], z_got.at[index, k - 1], 3 + k, index, z_mates[k - 1]
        )

    def table_z_copy(index, k):
        rows = pl.ds((side_z - k) * share, share)
        return remote(
            table.at[index, pl.ds(0, share)],
            table.at[index, rows],
            2 + side_z + k,
            index,
            z_mates[k - 1],
        )

    def table_y_copy(index):
        return remote(
            table.at[index, pl.ds(0, half)],
            table.at[index, pl.ds(half, half)],
            2 + 2 * side_z,
            index,
            sum_mate(index),
        )

    def meta_copy(k):
        return small(meta, metas.at[k], k, mates[k])

    def misfit_copy(k):
        return small(mis.at[k], mis_got.at[k], 5 + k, mates[k])

    s_y_copy = small(s_send, sy_got, 10, y_mate)

    def s_z_copy(k):
        return small(sz_send.at[k - 1], sz_got.at[k - 1], 10 + k, z_mates[k - 1])

    anchor_copy = pltpu.make_async_copy(
        references.at[0, pl.ds(pl.multiple_of(dp * share, share), share)],
        anchor,
        local.at[chunks],
    )
    anchor_copy.start()

    @pl.loop(0, chunks)
    def start_local(index):
        own_copy(index).start()

    meta[0:1] = class_in[...].astype(jnp.float32)
    meta[1:2] = rotation_in[...].astype(jnp.float32)
    meta[2:3] = defocus_in[...].astype(jnp.float32)
    meta[3:8] = jnp.zeros((5, LANES), jnp.float32)
    pl.semaphore_wait(barrier, len(everyone))
    for k in range(friends):
        meta_copy(k).start()
    for index in range(WINDOW):
        share_copy(index).start()
        core_copy(index).start()

    index_rows = lax.broadcasted_iota(jnp.int32, (LANES, LANES), 0).astype(jnp.float32)

    @pl.loop(0, chunks)
    def pick_radii(index):
        row = tables[pl.ds(8 + index, 1), :width]
        for part in range(width // LANES):
            lanes = slice(part * LANES, (part + 1) * LANES)
            target = jnp.broadcast_to(row[:, lanes], (LANES, LANES))
            for block in range(radii // LANES):
                match = index_rows == target - float(block * LANES)
                pick[index, block * LANES : (block + 1) * LANES, lanes] = jnp.where(
                    match, 1.0, 0.0
                ).astype(jnp.bfloat16)

    z_first = z.astype(jnp.float32)
    y_first = y.astype(jnp.float32)
    x_first = x.astype(jnp.float32)
    core_first = core.astype(jnp.float32)
    cell_rows = lax.broadcasted_iota(jnp.int32, (cells, LANES), 0).astype(jnp.float32)
    cell_lanes = lax.broadcasted_iota(jnp.int32, (LANES, cells), 1).astype(jnp.float32)
    owned = {}
    groups = (((0, 0), (1, 0)), ((0, 1), (1, 1)), ((0, 2),), ((0, 3),), ((1, 2),), ((1, 3),))
    for source in range(friends + 1):
        places = [place for place in groups[source] if place[0] < FAMILIES]
        if source > 0:
            meta_copy(source - 1).wait_recv()
            rows = metas[source - 1]
        else:
            rows = meta[...]
        class_z = jnp.floor(rows[0:1] / float(side_y))
        class_y = rows[0:1] - float(side_y) * class_z
        turn_dp = jnp.floor(rows[1:2] / float(share))
        turn_r = rows[1:2] - float(share) * turn_dp
        turn_x = jnp.floor(turn_dp * 0.5)
        rel_z = class_z - z_first
        rel_z = jnp.where(rel_z < 0.0, rel_z + float(side_z), rel_z)
        off_x = jnp.abs(turn_x - x_first)
        off_y = jnp.abs(class_y - y_first)
        off_core = jnp.abs(turn_dp - 2.0 * turn_x - core_first)
        focus = jnp.transpose(jnp.broadcast_to(rows[2:3], (LANES, LANES)))
        for family, block in places:
            off_share, off_sum = (off_x, off_y) if family == 0 else (off_y, off_x)
            mine = (off_share + off_core) < 0.5
            cell = jnp.where(mine, off_sum * float(half) + rel_z * float(share) + turn_r, -1.0)
            owned[family, block] = mine
            span = slice(block * LANES, (block + 1) * LANES)
            hot[family, :, span] = jnp.where(cell_rows == cell, 1.0, 0.0).astype(jnp.bfloat16)
            cell_t = jnp.transpose(jnp.broadcast_to(cell, (LANES, LANES)))
            hot_t[family, span] = jnp.where(cell_lanes == cell_t, 1.0, 0.0).astype(jnp.bfloat16)
        for part in range(radii // LANES):
            lanes = slice(part * LANES, (part + 1) * LANES)
            turns = focus * tables[0:1, lanes] + np.float32(0.1 / (2.0 * np.pi))
            wave = sine_of_turns(turns) * tables[1:2, lanes]
            for family, block in places:
                span = slice(block * LANES, (block + 1) * LANES)
                crad[family, span, lanes] = wave.astype(jnp.bfloat16)
                if family == 0:
                    sq[span, lanes] = (wave * wave + tables[2:3, lanes]).astype(jnp.bfloat16)
    acc[...] = jnp.zeros_like(acc)

    def tick(t, carry):
        @pl.when(t == 3)
        def counts_out():
            s_y_copy.wait_recv()
            total = s_own[...] + sy_got[...].astype(jnp.float32)
            sz_own[...] = total[:share]
            for k in range(1, side_z):
                sz_send[k - 1] = total[k * share : (k + 1) * share].astype(jnp.bfloat16)
                s_z_copy(k).start()

        @pl.when((t >= 3) & (t < chunks + 3))
        def sum_y():
            index = t - 3
            y_copy(index).wait_recv()
            total = b_own[index] + y_got[index].astype(jnp.float32)
            z_own[index] = total[:share]
            for k in range(1, side_z):
                z_send[index, k - 1] = total[k * share : (k + 1) * share].astype(jnp.bfloat16)
                z_copy(index, k).start()

        @pl.when(t == 5)
        def counts_in():
            anchor_copy.wait()
            total = sz_own[...]
            for k in range(1, side_z):
                s_z_copy(k).wait_recv()
                total = total + sz_got[k - 1].astype(jnp.float32)
            s_sum[...] = total

        @pl.when((t >= 5) & (t < chunks + 5))
        def update():
            index = t - 5
            total = z_own[index]
            for k in range(1, side_z):
                z_copy(index, k).wait_recv()
                total = total + z_got[index, k - 1].astype(jnp.float32)
            squares = s_sum[...]
            coarse = squares.astype(jnp.bfloat16)
            fine = (squares - coarse.astype(jnp.float32)).astype(jnp.bfloat16)
            pair = jnp.dot(
                jnp.concatenate([coarse, fine], axis=0),
                pick[index],
                preferred_element_type=jnp.float32,
            )
            energy = pair[:share] + pair[share:]
            damping = 0.5 * squares[:, radii - 1 : radii] + 1.0
            scale = 1.0 / damping
            start = anchor[:, columns(index)].astype(jnp.float32)
            first = (start - (start * energy - total) * scale).astype(jnp.bfloat16)
            table[index, 0:share] = first
            for k in range(1, side_z):
                table_z_copy(index, k).start()
            again = first.astype(jnp.float32)
            refined[:, columns(index)] = (again - (again * energy - total) * scale).astype(
                jnp.bfloat16
            )

        @pl.when((t >= 7) & (t < chunks + 7))
        def spread():
            index = t - 7
            for k in range(1, side_z):
                table_z_copy(index, k).wait_recv()
            table_y_copy(index).start()

        @pl.when(t < chunks)
        def contrasts():
            for block in range(2):
                span = pl.ds(2 * block * LANES, 2 * LANES)
                con[t, span] = jnp.dot(
                    crad[t % FAMILIES, span], pick[t], preferred_element_type=jnp.float32
                ).astype(jnp.bfloat16)

        @pl.when(t >= 9)
        def residuals():
            index = t - 9
            table_y_copy(index).wait_recv()
            for block in range(4):
                span = block_rows(block)
                tiles = jnp.dot(
                    hot_t[index % FAMILIES, span], table[index], preferred_element_type=jnp.float32
                )
                total = acc[index % FAMILIES, span]
                for part in range(width // LANES):
                    lanes = slice(part * LANES, (part + 1) * LANES)
                    rest = con[index, span, lanes].astype(jnp.float32) * tiles[:, lanes]
                    rest = rest - img[index, span, lanes].astype(jnp.float32)
                    total = total + rest * rest
                acc[index % FAMILIES, span] = total

        @pl.when(t < chunks)
        def forward():
            share_copy(t).wait_recv()
            forward_copy(t).start()

        @pl.when(t < chunks - WINDOW)
        def start_images():
            share_copy(t + WINDOW).start()
            core_copy(t + WINDOW).start()

        @pl.when((t >= 1) & (t < chunks + 1))
        def partial_sums():
            index = t - 1
            own_copy(index).wait()
            core_copy(index).wait_recv()
            forward_copy(index).wait_recv()
            total = jnp.dot(
                hot[index % FAMILIES], con[index] * img[index], preferred_element_type=jnp.float32
            )
            b_own[index] = total[:half]
            b_send[index] = total[half:].astype(jnp.bfloat16)
            y_copy(index).start()

        @pl.when(t == 1)
        def counts_start():
            partial = jnp.dot(hot[0], sq[...], preferred_element_type=jnp.float32)
            s_own[...] = partial[:half]
            s_send[...] = partial[half:].astype(jnp.bfloat16)
            s_y_copy.start()

        return carry

    lax.fori_loop(0, chunks + 9, tick, 0)

    def row_of(family, block):
        part = acc[family, block * LANES : (block + 1) * LANES]
        row = jnp.sum(jnp.transpose(part), axis=0, keepdims=True)
        return jnp.where(owned[family, block], row * (1.0 / float(chunks * width)), 0.0)

    rows_out = [row_of(0, 1), row_of(0, 2), row_of(0, 3)]
    if FAMILIES == 2:
        rows_out[0] = rows_out[0] + row_of(1, 1)
        rows_out = rows_out + [row_of(1, 2), row_of(1, 3)]
    for k, row in enumerate(rows_out):
        mis[k] = jnp.broadcast_to(row, mis.shape[1:])
        misfit_copy(k).start()

    @pl.loop(0, chunks)
    def drain(index):
        core_copy(index).wait_send()
        share_copy(index).wait_send()
        forward_copy(index).wait_send()
        y_copy(index).wait_send()
        for k in range(1, side_z):
            z_copy(index, k).wait_send()
            table_z_copy(index, k).wait_send()
        table_y_copy(index).wait_send()

    s_y_copy.wait_send()
    for k in range(1, side_z):
        s_z_copy(k).wait_send()
    total = row_of(0, 0)
    if FAMILIES == 2:
        total = total + row_of(1, 0)
    for k in range(friends):
        meta_copy(k).wait_send()
        misfit_copy(k).wait()
        total = total + mis_got[k, 0:1]
    misfit[...] = total


def shards_close(side_y, side_z, images, defocus, classes, rotations, references):
    count_dp = lax.axis_size("dp")
    rows, pixels = images.shape
    share = references.shape[1] // count_dp
    chunks = CHUNKS
    width = pixels // chunks
    half = side_z * share
    cells = side_y * half
    tables, place = radius_tables(SIDE)
    radii = tables.shape[1]
    constants = np.zeros((8 + chunks, max(radii, width)), np.float32)
    constants[:8, :radii] = tables
    constants[8:, :width] = place.reshape(chunks, width)
    bf16, f32 = jnp.bfloat16, jnp.float32
    kinds = 3 + 2 * side_z
    vmem = pl.BlockSpec(memory_space=pltpu.VMEM)
    anywhere = pl.BlockSpec(memory_space=pltpu.HBM)
    refined, misfit = pl.pallas_call(
        functools.partial(refine_kernel, (chunks, width, share, side_y, side_z)),
        out_shape=(
            jax.ShapeDtypeStruct((share, pixels), bf16),
            jax.ShapeDtypeStruct((1, rows), f32),
        ),
        in_specs=[anywhere, vmem, vmem, vmem, vmem, anywhere],
        out_specs=(vmem, vmem),
        scratch_shapes=[
            pltpu.VMEM((chunks, 4 * rows, width), bf16),
            pltpu.VMEM((8, rows), f32),
            pltpu.VMEM((1 + 2 * FAMILIES, 8, rows), f32),
            pltpu.VMEM((FAMILIES, 4 * rows, radii), bf16),
            pltpu.VMEM((4 * rows, radii), bf16),
            pltpu.VMEM((chunks, 4 * rows, width), bf16),
            pltpu.VMEM((chunks, radii, width), bf16),
            pltpu.VMEM((FAMILIES, cells, 4 * rows), bf16),
            pltpu.VMEM((FAMILIES, 4 * rows, cells), bf16),
            pltpu.VMEM((chunks, half, width), f32),
            pltpu.VMEM((chunks, half, width), bf16),
            pltpu.VMEM((chunks, half, width), bf16),
            pltpu.VMEM((chunks, share, width), f32),
            pltpu.VMEM((chunks, side_z - 1, share, width), bf16),
            pltpu.VMEM((chunks, side_z - 1, share, width), bf16),
            pltpu.VMEM((chunks, cells, width), bf16),
            pltpu.VMEM((half, radii), f32),
            pltpu.VMEM((half, radii), bf16),
            pltpu.VMEM((half, radii), bf16),
            pltpu.VMEM((share, radii), f32),
            pltpu.VMEM((side_z - 1, share, radii), bf16),
            pltpu.VMEM((side_z - 1, share, radii), bf16),
            pltpu.VMEM((share, radii), f32),
            pltpu.VMEM((share, pixels), bf16),
            pltpu.VMEM((FAMILIES, 4 * rows, LANES), f32),
            pltpu.VMEM((1 + 2 * FAMILIES, 8, rows), f32),
            pltpu.VMEM((1 + 2 * FAMILIES, 8, rows), f32),
            pltpu.SemaphoreType.DMA((kinds, chunks)),
            pltpu.SemaphoreType.DMA((kinds, chunks)),
            pltpu.SemaphoreType.DMA((10 + side_z,)),
            pltpu.SemaphoreType.DMA((10 + side_z,)),
            pltpu.SemaphoreType.DMA((chunks + 1,)),
        ],
        compiler_params=pltpu.CompilerParams(
            collective_id=0, has_side_effects=True, vmem_limit_bytes=63 * 1024 * 1024
        ),
    )(
        images,
        classes.reshape(1, rows),
        rotations.reshape(1, rows),
        defocus.reshape(1, rows),
        jnp.asarray(constants),
        references,
    )
    return refined.reshape(1, share, pixels), misfit.reshape(rows)


def solution(mesh):
    in_specs = (
        P(("cls", "dp"), None),
        P(("cls", "dp")),
        P(("cls", "dp"), None),
        P(("cls", "dp")),
        P("cls", None, None),
    )
    out_specs = (P("cls", "dp", None), P(("cls", "dp")))
    per_device = shards
    if mesh.shape["cls"] == 8 and mesh.shape["dp"] == 4:
        per_device = functools.partial(shards_close, 2, 4)
    return jax.shard_map(
        per_device, mesh=mesh, in_specs=in_specs, out_specs=out_specs, check_vma=False
    )
```

```python
import functools
import jax
import jax.numpy as jnp
import numpy as np
from jax import lax
from jax.experimental import pallas as pl
from jax.experimental.pallas import tpu as pltpu
from jax.sharding import PartitionSpec as P

SIDE = 64
MESH = pl.DeviceIdType.MESH
CHUNKS = 8
WINDOW = 2
FAMILIES = 1
SINE = (
    6.283182792843448,
    -41.341419333015786,
    81.59613740878902,
    -76.57967400034848,
    41.203682075135006,
    -12.268761447374176,
)
LANES = 128


def wave_table(side_count):
    pixel_index = jnp.arange(side_count * side_count, dtype=jnp.int32)
    half_side = side_count // 2
    row_freq = (pixel_index // side_count + half_side) % side_count - half_side
    col_freq = (pixel_index % side_count + half_side) % side_count - half_side
    return (row_freq * row_freq + col_freq * col_freq).astype(jnp.float32) / float(
        half_side * half_side
    )


def contrast(defocus_rows, radius):
    phase = 20.0 * defocus_rows.astype(jnp.float32)[:, None] * radius[None, :] + 0.1
    return -jnp.sin(phase) * jnp.exp(-0.5 * radius)[None, :]


def sweep_rows(table, image_rows, rotation_rows, defocus_rows, radius):
    row_total = image_rows.shape[0]
    block_rows = min(64, row_total)
    block_count = row_total // block_rows
    rotation_count = table.shape[0]
    labels = jnp.arange(rotation_count, dtype=jnp.int32)

    def advance(gradient, block_index):
        row_start = block_index * block_rows
        image_block = lax.dynamic_slice_in_dim(image_rows, row_start, block_rows, 0)
        rotation_block = lax.dynamic_slice_in_dim(rotation_rows, row_start, block_rows, 0)
        defocus_block = lax.dynamic_slice_in_dim(defocus_rows, row_start, block_rows, 0)
        selector = (rotation_block[:, None] == labels[None, :]).astype(jnp.bfloat16)
        tiles = jnp.dot(selector, table, preferred_element_type=jnp.float32)
        contrast_rows = contrast(defocus_block, radius)
        residual = contrast_rows * tiles - image_block.astype(jnp.float32)
        misfit_rows = jnp.mean(residual * residual, axis=1)
        weighted = (contrast_rows * residual).astype(jnp.bfloat16)
        gradient = gradient + lax.dot_general(
            selector, weighted, (((0,), (0,)), ((), ())), preferred_element_type=jnp.float32
        )
        return (gradient, misfit_rows)

    start_grad = jnp.zeros((rotation_count, image_rows.shape[1]), jnp.float32)
    gradient, misfit_blocks = lax.scan(
        advance, start_grad, jnp.arange(block_count, dtype=jnp.int32)
    )
    return (gradient, misfit_blocks.reshape(row_total))


def build_slots(
    images, defocus, rotations, class_rows, class_rank, rank_first, slot_width, count_cls
):
    particle_ids = jnp.arange(images.shape[0], dtype=jnp.int32)
    inside = (class_rank >= rank_first) & (class_rank < rank_first + slot_width)
    slot_of = jnp.where(inside, class_rows * slot_width + class_rank - rank_first, -1)
    slot_ids = jnp.arange(count_cls * slot_width, dtype=jnp.int32)
    slot_match = slot_ids[:, None] == slot_of[None, :]
    slot_live = jnp.any(slot_match, axis=1)
    slot_source = jnp.sum(jnp.where(slot_match, particle_ids[None, :], 0), axis=1)
    send_images = jnp.where(
        slot_live[:, None], jnp.take(images, slot_source, axis=0), jnp.zeros((), jnp.bfloat16)
    )
    send_rotation = jnp.where(slot_live, jnp.take(rotations, slot_source), -1)
    send_defocus = jnp.where(
        slot_live, jnp.take(defocus, slot_source).astype(jnp.float32), 0.0
    ).astype(jnp.bfloat16)
    return (send_images, send_rotation, send_defocus)


def shards(images, defocus, classes, rotations, references):
    count_cls = lax.axis_size("cls")
    count_dp = lax.axis_size("dp")
    particle_count = images.shape[0]
    pixel_count = images.shape[1]
    rotation_count = references.shape[1]
    capacity = max(2, 2 * particle_count // count_cls)
    slot_count = count_cls * capacity
    radius = wave_table(SIDE)
    class_rows = classes[:, 0]
    particle_ids = jnp.arange(particle_count, dtype=jnp.int32)
    earlier_same = (class_rows[:, None] == class_rows[None, :]) & (
        particle_ids[None, :] < particle_ids[:, None]
    )
    class_rank = jnp.sum(earlier_same.astype(jnp.int32), axis=1)
    slot_of = class_rows * capacity + class_rank
    slot_ids = jnp.arange(slot_count, dtype=jnp.int32)
    slot_match = slot_ids[:, None] == slot_of[None, :]
    send_images, send_rotation, send_defocus = build_slots(
        images, defocus, rotations, class_rows, class_rank, 0, capacity, count_cls
    )
    recv_images, recv_rotation, recv_defocus = (
        lax.all_to_all(
            send_images.reshape(count_cls, capacity, pixel_count),
            "cls",
            split_axis=0,
            concat_axis=0,
            tiled=True,
        ),
        lax.all_to_all(
            send_rotation.astype(jnp.bfloat16).reshape(count_cls, capacity),
            "cls",
            split_axis=0,
            concat_axis=0,
            tiled=True,
        ),
        lax.all_to_all(
            send_defocus.reshape(count_cls, capacity),
            "cls",
            split_axis=0,
            concat_axis=0,
            tiled=True,
        ),
    )
    image_slots = recv_images.reshape(slot_count, pixel_count)
    rotation_slots = recv_rotation.reshape(slot_count).astype(jnp.int32)
    defocus_slots = recv_defocus.reshape(slot_count)
    labels = jnp.arange(rotation_count, dtype=jnp.int32)
    local_counts = jnp.sum((rotation_slots[:, None] == labels[None, :]).astype(jnp.float32), axis=0)
    counts = lax.psum(local_counts, "dp")
    damping = 0.5 * counts + 1.0
    table = references[0]
    grad_first, unused_first = sweep_rows(table, image_slots, rotation_slots, defocus_slots, radius)
    share_rows = rotation_count // count_dp
    share_start = lax.axis_index("dp") * share_rows
    damping_share = lax.dynamic_slice_in_dim(damping, share_start, share_rows, 0)
    grad_share = lax.psum_scatter(
        grad_first.astype(jnp.bfloat16), "dp", scatter_dimension=0, tiled=True
    ).astype(jnp.float32)
    anchor = lax.dynamic_slice_in_dim(table, share_start, share_rows, 0).astype(jnp.float32)
    fresh_share = (anchor - grad_share / damping_share[:, None]).astype(jnp.bfloat16)
    table_next = lax.all_gather(fresh_share, "dp", axis=0, tiled=True)
    grad_second, misfit_slots = sweep_rows(
        table_next, image_slots, rotation_slots, defocus_slots, radius
    )
    second_share = lax.psum_scatter(
        grad_second.astype(jnp.bfloat16), "dp", scatter_dimension=0, tiled=True
    ).astype(jnp.float32)
    anchor_next = lax.dynamic_slice_in_dim(table_next, share_start, share_rows, 0).astype(
        jnp.float32
    )
    refined = (anchor_next - second_share / damping_share[:, None]).astype(jnp.bfloat16)
    returned = lax.all_to_all(
        misfit_slots.reshape(count_cls, capacity), "cls", split_axis=0, concat_axis=0, tiled=True
    )
    returned_slots = returned.reshape(slot_count)
    misfit = jnp.sum(jnp.where(slot_match, returned_slots[:, None], 0.0), axis=0)
    return (refined.reshape(1, share_rows, pixel_count), misfit)


def radius_tables(side_count):
    half_side = side_count // 2
    freq = (np.arange(side_count) + half_side) % side_count - half_side
    square = (freq[:, None] ** 2 + freq[None, :] ** 2).reshape(-1)
    values, place = np.unique(square, return_inverse=True)
    width = -(-(len(values) + 1) // LANES) * LANES
    rows = np.zeros((8, width), np.float32)
    rows[0, : len(values)] = values.astype(np.float32) / np.float32(half_side * half_side)
    rows[1, : len(values)] = -np.exp(-0.5 * rows[0, : len(values)])
    rows[0] = (rows[0].astype(np.float64) * (10.0 / np.pi)).astype(np.float32)
    rows[2, width - 1] = 1.0
    return rows, place.reshape(1, -1).astype(np.float32)


def sine_of_turns(turns):
    rest = turns - jnp.floor(turns + 0.5)
    square = rest * rest
    poly = np.float32(SINE[-1])
    for term in SINE[-2::-1]:
        poly = poly * square + np.float32(term)
    return rest * poly


def refine_kernel(
    sizes,
    images,
    class_in,
    rotation_in,
    defocus_in,
    tables,
    references,
    refined,
    misfit,
    img,
    meta,
    metas,
    crad,
    sq,
    con,
    pick,
    hot,
    hot_t,
    b_own,
    b_send,
    y_got,
    z_own,
    z_send,
    z_got,
    table,
    s_own,
    s_send,
    sy_got,
    sz_own,
    sz_send,
    sz_got,
    s_sum,
    anchor,
    acc,
    mis,
    mis_got,
    send,
    recv,
    send_small,
    recv_small,
    local,
):
    chunks, width, share, side_y, side_z = sizes
    cls = lax.axis_index("cls")
    dp = lax.axis_index("dp")
    z = cls // side_y
    y = cls % side_y
    radii = crad.shape[2]
    half = side_z * share
    cells = side_y * half

    core = dp % 2
    x = dp // 2
    other_core = dp + 1 - 2 * core
    other_x = dp + 2 - 4 * x
    other_y = cls + 1 - 2 * y
    core_mate = (cls, other_core)
    x_mate = (cls, other_x)
    y_mate = (other_y, dp)
    mates = (
        core_mate,
        x_mate,
        (cls, other_x + 1 - 2 * core),
        y_mate,
        (other_y, other_core),
    )
    z_mates = [(((z + k) % side_z) * side_y + y, dp) for k in range(1, side_z)]

    barrier = pltpu.get_barrier_semaphore()
    friends = 1 + 2 * FAMILIES
    everyone = list(mates[:friends]) + z_mates
    if FAMILIES == 1:
        everyone.append(y_mate)
    for other in everyone:
        pl.semaphore_signal(barrier, inc=1, device_id=other, device_id_type=MESH)

    def remote(source, target, kind, index, device):
        return pltpu.make_async_remote_copy(
            src_ref=source,
            dst_ref=target,
            send_sem=send.at[kind, index],
            recv_sem=recv.at[kind, index],
            device_id=device,
            device_id_type=MESH,
        )

    def small(source, target, index, device):
        return pltpu.make_async_remote_copy(
            src_ref=source,
            dst_ref=target,
            send_sem=send_small.at[index],
            recv_sem=recv_small.at[index],
            device_id=device,
            device_id_type=MESH,
        )

    def share_mate(index):
        family = index % FAMILIES
        return (cls + family * (1 - 2 * y), dp + (1 - family) * (2 - 4 * x))

    def sum_mate(index):
        family = index % FAMILIES
        return (cls + (1 - family) * (1 - 2 * y), dp + family * (2 - 4 * x))

    def block_rows(block):
        return pl.ds(block * LANES, LANES)

    def columns(index):
        return pl.ds(pl.multiple_of(index * width, width), width)

    def own_copy(index):
        return pltpu.make_async_copy(
            images.at[:, columns(index)], img.at[index, block_rows(0)], local.at[index]
        )

    def core_copy(index):
        return remote(
            images.at[:, columns(index)], img.at[index, block_rows(1)], 0, index, core_mate
        )

    def share_copy(index):
        return remote(
            images.at[:, columns(index)],
            img.at[index, block_rows(2)],
            1,
            index,
            share_mate(index),
        )

    def forward_copy(index):
        return remote(
            img.at[index, block_rows(2)], img.at[index, block_rows(3)], 2, index, core_mate
        )

    def y_copy(index):
        return remote(b_send.at[index], y_got.at[index], 3, index, sum_mate(index))

    def z_copy(index, k):
        return remote(
            z_send.at[index, k - 1], z_got.at[index, k - 1], 3 + k, index, z_mates[k - 1]
        )

    def table_z_copy(index, k):
        rows = pl.ds((side_z - k) * share, share)
        return remote(
            table.at[index, pl.ds(0, share)],
            table.at[index, rows],
            2 + side_z + k,
            index,
            z_mates[k - 1],
        )

    def table_y_copy(index):
        return remote(
            table.at[index, pl.ds(0, half)],
            table.at[index, pl.ds(half, half)],
            2 + 2 * side_z,
            index,
            sum_mate(index),
        )

    def meta_copy(k):
        return small(meta, metas.at[k], k, mates[k])

    def misfit_copy(k):
        return small(mis.at[k], mis_got.at[k], 5 + k, mates[k])

    s_y_copy = small(s_send, sy_got, 10, y_mate)

    def s_z_copy(k):
        return small(sz_send.at[k - 1], sz_got.at[k - 1], 10 + k, z_mates[k - 1])

    anchor_copy = pltpu.make_async_copy(
        references.at[0, pl.ds(pl.multiple_of(dp * share, share), share)],
        anchor,
        local.at[chunks],
    )
    anchor_copy.start()

    @pl.loop(0, chunks)
    def start_local(index):
        own_copy(index).start()

    meta[0:1] = class_in[...].astype(jnp.float32)
    meta[1:2] = rotation_in[...].astype(jnp.float32)
    meta[2:3] = defocus_in[...].astype(jnp.float32)
    meta[3:8] = jnp.zeros((5, LANES), jnp.float32)
    pl.semaphore_wait(barrier, len(everyone))
    for k in range(friends):
        meta_copy(k).start()
    for index in range(WINDOW):
        share_copy(index).start()
        core_copy(index).start()

    index_rows = lax.broadcasted_iota(jnp.int32, (LANES, LANES), 0).astype(jnp.float32)

    @pl.loop(0, chunks)
    def pick_radii(index):
        row = tables[pl.ds(8 + index, 1), :width]
        for part in range(width // LANES):
            lanes = slice(part * LANES, (part + 1) * LANES)
            target = jnp.broadcast_to(row[:, lanes], (LANES, LANES))
            for block in range(radii // LANES):
                match = index_rows == target - float(block * LANES)
                pick[index, block * LANES : (block + 1) * LANES, lanes] = jnp.where(
                    match, 1.0, 0.0
                ).astype(jnp.bfloat16)

    z_first = z.astype(jnp.float32)
    y_first = y.astype(jnp.float32)
    x_first = x.astype(jnp.float32)
    core_first = core.astype(jnp.float32)
    cell_rows = lax.broadcasted_iota(jnp.int32, (cells, LANES), 0).astype(jnp.float32)
    cell_lanes = lax.broadcasted_iota(jnp.int32, (LANES, cells), 1).astype(jnp.float32)
    owned = {}
    groups = (((0, 0), (1, 0)), ((0, 1), (1, 1)), ((0, 2),), ((0, 3),), ((1, 2),), ((1, 3),))
    for source in range(friends + 1):
        places = [place for place in groups[source] if place[0] < FAMILIES]
        if source > 0:
            meta_copy(source - 1).wait_recv()
            rows = metas[source - 1]
        else:
            rows = meta[...]
        class_z = jnp.floor(rows[0:1] / float(side_y))
        class_y = rows[0:1] - float(side_y) * class_z
        turn_dp = jnp.floor(rows[1:2] / float(share))
        turn_r = rows[1:2] - float(share) * turn_dp
        turn_x = jnp.floor(turn_dp * 0.5)
        rel_z = class_z - z_first
        rel_z = jnp.where(rel_z < 0.0, rel_z + float(side_z), rel_z)
        off_x = jnp.abs(turn_x - x_first)
        off_y = jnp.abs(class_y - y_first)
        off_core = jnp.abs(turn_dp - 2.0 * turn_x - core_first)
        focus = jnp.transpose(jnp.broadcast_to(rows[2:3], (LANES, LANES)))
        for family, block in places:
            off_share, off_sum = (off_x, off_y) if family == 0 else (off_y, off_x)
            mine = (off_share + off_core) < 0.5
            cell = jnp.where(mine, off_sum * float(half) + rel_z * float(share) + turn_r, -1.0)
            owned[family, block] = mine
            span = slice(block * LANES, (block + 1) * LANES)
            hot[family, :, span] = jnp.where(cell_rows == cell, 1.0, 0.0).astype(jnp.bfloat16)
            cell_t = jnp.transpose(jnp.broadcast_to(cell, (LANES, LANES)))
            hot_t[family, span] = jnp.where(cell_lanes == cell_t, 1.0, 0.0).astype(jnp.bfloat16)
        for part in range(radii // LANES):
            lanes = slice(part * LANES, (part + 1) * LANES)
            turns = focus * tables[0:1, lanes] + np.float32(0.1 / (2.0 * np.pi))
            wave = sine_of_turns(turns) * tables[1:2, lanes]
            for family, block in places:
                span = slice(block * LANES, (block + 1) * LANES)
                crad[family, span, lanes] = wave.astype(jnp.bfloat16)
                if family == 0:
                    sq[span, lanes] = (wave * wave + tables[2:3, lanes]).astype(jnp.bfloat16)
    acc[...] = jnp.zeros_like(acc)

    def tick(t, carry):
        @pl.when(t == 3)
        def counts_out():
            s_y_copy.wait_recv()
            total = s_own[...] + sy_got[...].astype(jnp.float32)
            sz_own[...] = total[:share]
            for k in range(1, side_z):
                sz_send[k - 1] = total[k * share : (k + 1) * share].astype(jnp.bfloat16)
                s_z_copy(k).start()

        @pl.when((t >= 3) & (t < chunks + 3))
        def sum_y():
            index = t - 3
            y_copy(index).wait_recv()
            total = b_own[index] + y_got[index].astype(jnp.float32)
            z_own[index] = total[:share]
            for k in range(1, side_z):
                z_send[index, k - 1] = total[k * share : (k + 1) * share].astype(jnp.bfloat16)
                z_copy(index, k).start()

        @pl.when(t == 5)
        def counts_in():
            anchor_copy.wait()
            total = sz_own[...]
            for k in range(1, side_z):
                s_z_copy(k).wait_recv()
                total = total + sz_got[k - 1].astype(jnp.float32)
            s_sum[...] = total

        @pl.when((t >= 5) & (t < chunks + 5))
        def update():
            index = t - 5
            total = z_own[index]
            for k in range(1, side_z):
                z_copy(index, k).wait_recv()
                total = total + z_got[index, k - 1].astype(jnp.float32)
            squares = s_sum[...]
            coarse = squares.astype(jnp.bfloat16)
            fine = (squares - coarse.astype(jnp.float32)).astype(jnp.bfloat16)
            pair = jnp.dot(
                jnp.concatenate([coarse, fine], axis=0),
                pick[index],
                preferred_element_type=jnp.float32,
            )
            energy = pair[:share] + pair[share:]
            damping = 0.5 * squares[:, radii - 1 : radii] + 1.0
            scale = 1.0 / damping
            start = anchor[:, columns(index)].astype(jnp.float32)
            first = (start - (start * energy - total) * scale).astype(jnp.bfloat16)
            table[index, 0:share] = first
            for k in range(1, side_z):
                table_z_copy(index, k).start()
            again = first.astype(jnp.float32)
            refined[:, columns(index)] = (again - (again * energy - total) * scale).astype(
                jnp.bfloat16
            )

        @pl.when((t >= 7) & (t < chunks + 7))
        def spread():
            index = t - 7
            for k in range(1, side_z):
                table_z_copy(index, k).wait_recv()
            table_y_copy(index).start()

        @pl.when(t < chunks)
        def contrasts():
            for block in range(2):
                span = pl.ds(2 * block * LANES, 2 * LANES)
                con[t, span] = jnp.dot(
                    crad[t % FAMILIES, span], pick[t], preferred_element_type=jnp.float32
                ).astype(jnp.bfloat16)

        @pl.when(t >= 9)
        def residuals():
            index = t - 9
            table_y_copy(index).wait_recv()
            for block in range(4):
                span = block_rows(block)
                tiles = jnp.dot(
                    hot_t[index % FAMILIES, span], table[index], preferred_element_type=jnp.float32
                )
                total = acc[index % FAMILIES, span]
                for part in range(width // LANES):
                    lanes = slice(part * LANES, (part + 1) * LANES)
                    rest = con[index, span, lanes].astype(jnp.float32) * tiles[:, lanes]
                    rest = rest - img[index, span, lanes].astype(jnp.float32)
                    total = total + rest * rest
                acc[index % FAMILIES, span] = total

        @pl.when(t < chunks)
        def forward():
            share_copy(t).wait_recv()
            forward_copy(t).start()

        @pl.when(t < chunks - WINDOW)
        def start_images():
            share_copy(t + WINDOW).start()
            core_copy(t + WINDOW).start()

        @pl.when((t >= 1) & (t < chunks + 1))
        def partial_sums():
            index = t - 1
            own_copy(index).wait()
            core_copy(index).wait_recv()
            forward_copy(index).wait_recv()
            total = jnp.dot(
                hot[index % FAMILIES], con[index] * img[index], preferred_element_type=jnp.float32
            )
            b_own[index] = total[:half]
            b_send[index] = total[half:].astype(jnp.bfloat16)
            y_copy(index).start()

        @pl.when(t == 1)
        def counts_start():
            partial = jnp.dot(hot[0], sq[...], preferred_element_type=jnp.float32)
            s_own[...] = partial[:half]
            s_send[...] = partial[half:].astype(jnp.bfloat16)
            s_y_copy.start()

        return carry

    lax.fori_loop(0, chunks + 9, tick, 0)

    def row_of(family, block):
        part = acc[family, block * LANES : (block + 1) * LANES]
        row = jnp.sum(jnp.transpose(part), axis=0, keepdims=True)
        return jnp.where(owned[family, block], row * (1.0 / float(chunks * width)), 0.0)

    rows_out = [row_of(0, 1), row_of(0, 2), row_of(0, 3)]
    if FAMILIES == 2:
        rows_out[0] = rows_out[0] + row_of(1, 1)
        rows_out = rows_out + [row_of(1, 2), row_of(1, 3)]
    for k, row in enumerate(rows_out):
        mis[k] = jnp.broadcast_to(row, mis.shape[1:])
        misfit_copy(k).start()

    @pl.loop(0, chunks)
    def drain(index):
        core_copy(index).wait_send()
        share_copy(index).wait_send()
        forward_copy(index).wait_send()
        y_copy(index).wait_send()
        for k in range(1, side_z):
            z_copy(index, k).wait_send()
            table_z_copy(index, k).wait_send()
        table_y_copy(index).wait_send()

    s_y_copy.wait_send()
    for k in range(1, side_z):
        s_z_copy(k).wait_send()
    total = row_of(0, 0)
    if FAMILIES == 2:
        total = total + row_of(1, 0)
    for k in range(friends):
        meta_copy(k).wait_send()
        misfit_copy(k).wait()
        total = total + mis_got[k, 0:1]
    misfit[...] = total


def shards_close(side_y, side_z, images, defocus, classes, rotations, references):
    count_dp = lax.axis_size("dp")
    rows, pixels = images.shape
    share = references.shape[1] // count_dp
    chunks = CHUNKS
    width = pixels // chunks
    half = side_z * share
    cells = side_y * half
    tables, place = radius_tables(SIDE)
    radii = tables.shape[1]
    constants = np.zeros((8 + chunks, max(radii, width)), np.float32)
    constants[:8, :radii] = tables
    constants[8:, :width] = place.reshape(chunks, width)
    bf16, f32 = jnp.bfloat16, jnp.float32
    kinds = 3 + 2 * side_z
    vmem = pl.BlockSpec(memory_space=pltpu.VMEM)
    anywhere = pl.BlockSpec(memory_space=pltpu.HBM)
    refined, misfit = pl.pallas_call(
        functools.partial(refine_kernel, (chunks, width, share, side_y, side_z)),
        out_shape=(
            jax.ShapeDtypeStruct((share, pixels), bf16),
            jax.ShapeDtypeStruct((1, rows), f32),
        ),
        in_specs=[anywhere, vmem, vmem, vmem, vmem, anywhere],
        out_specs=(vmem, vmem),
        scratch_shapes=[
            pltpu.VMEM((chunks, 4 * rows, width), bf16),
            pltpu.VMEM((8, rows), f32),
            pltpu.VMEM((1 + 2 * FAMILIES, 8, rows), f32),
            pltpu.VMEM((FAMILIES, 4 * rows, radii), bf16),
            pltpu.VMEM((4 * rows, radii), bf16),
            pltpu.VMEM((chunks, 4 * rows, width), bf16),
            pltpu.VMEM((chunks, radii, width), bf16),
            pltpu.VMEM((FAMILIES, cells, 4 * rows), bf16),
            pltpu.VMEM((FAMILIES, 4 * rows, cells), bf16),
            pltpu.VMEM((chunks, half, width), f32),
            pltpu.VMEM((chunks, half, width), bf16),
            pltpu.VMEM((chunks, half, width), bf16),
            pltpu.VMEM((chunks, share, width), f32),
            pltpu.VMEM((chunks, side_z - 1, share, width), bf16),
            pltpu.VMEM((chunks, side_z - 1, share, width), bf16),
            pltpu.VMEM((chunks, cells, width), bf16),
            pltpu.VMEM((half, radii), f32),
            pltpu.VMEM((half, radii), bf16),
            pltpu.VMEM((half, radii), bf16),
            pltpu.VMEM((share, radii), f32),
            pltpu.VMEM((side_z - 1, share, radii), bf16),
            pltpu.VMEM((side_z - 1, share, radii), bf16),
            pltpu.VMEM((share, radii), f32),
            pltpu.VMEM((share, pixels), bf16),
            pltpu.VMEM((FAMILIES, 4 * rows, LANES), f32),
            pltpu.VMEM((1 + 2 * FAMILIES, 8, rows), f32),
            pltpu.VMEM((1 + 2 * FAMILIES, 8, rows), f32),
            pltpu.SemaphoreType.DMA((kinds, chunks)),
            pltpu.SemaphoreType.DMA((kinds, chunks)),
            pltpu.SemaphoreType.DMA((10 + side_z,)),
            pltpu.SemaphoreType.DMA((10 + side_z,)),
            pltpu.SemaphoreType.DMA((chunks + 1,)),
        ],
        compiler_params=pltpu.CompilerParams(
            collective_id=0, has_side_effects=True, vmem_limit_bytes=63 * 1024 * 1024
        ),
    )(
        images,
        classes.reshape(1, rows),
        rotations.reshape(1, rows),
        defocus.reshape(1, rows),
        jnp.asarray(constants),
        references,
    )
    return refined.reshape(1, share, pixels), misfit.reshape(rows)


def solution(mesh):
    in_specs = (
        P(("cls", "dp"), None),
        P(("cls", "dp")),
        P(("cls", "dp"), None),
        P(("cls", "dp")),
        P("cls", None, None),
    )
    out_specs = (P("cls", "dp", None), P(("cls", "dp")))
    per_device = shards
    if mesh.shape["cls"] == 8 and mesh.shape["dp"] == 4:
        per_device = functools.partial(shards_close, 2, 4)
    return jax.shard_map(
        per_device, mesh=mesh, in_specs=in_specs, out_specs=out_specs, check_vma=False
    )
```

```python
import functools
import jax
import jax.numpy as jnp
import numpy as np
from jax import lax
from jax.experimental import pallas as pl
from jax.experimental.pallas import tpu as pltpu
from jax.sharding import PartitionSpec as P

SIDE = 64
MESH = pl.DeviceIdType.MESH
CHUNKS = 8
WINDOW = 2
FAMILIES = 1
SINE = (
    6.283182792843448,
    -41.341419333015786,
    81.59613740878902,
    -76.57967400034848,
    41.203682075135006,
    -12.268761447374176,
)
LANES = 128


def wave_table(side_count):
    pixel_index = jnp.arange(side_count * side_count, dtype=jnp.int32)
    half_side = side_count // 2
    row_freq = (pixel_index // side_count + half_side) % side_count - half_side
    col_freq = (pixel_index % side_count + half_side) % side_count - half_side
    return (row_freq * row_freq + col_freq * col_freq).astype(jnp.float32) / float(
        half_side * half_side
    )


def contrast(defocus_rows, radius):
    phase = 20.0 * defocus_rows.astype(jnp.float32)[:, None] * radius[None, :] + 0.1
    return -jnp.sin(phase) * jnp.exp(-0.5 * radius)[None, :]


def sweep_rows(table, image_rows, rotation_rows, defocus_rows, radius):
    row_total = image_rows.shape[0]
    block_rows = min(64, row_total)
    block_count = row_total // block_rows
    rotation_count = table.shape[0]
    labels = jnp.arange(rotation_count, dtype=jnp.int32)

    def advance(gradient, block_index):
        row_start = block_index * block_rows
        image_block = lax.dynamic_slice_in_dim(image_rows, row_start, block_rows, 0)
        rotation_block = lax.dynamic_slice_in_dim(rotation_rows, row_start, block_rows, 0)
        defocus_block = lax.dynamic_slice_in_dim(defocus_rows, row_start, block_rows, 0)
        selector = (rotation_block[:, None] == labels[None, :]).astype(jnp.bfloat16)
        tiles = jnp.dot(selector, table, preferred_element_type=jnp.float32)
        contrast_rows = contrast(defocus_block, radius)
        residual = contrast_rows * tiles - image_block.astype(jnp.float32)
        misfit_rows = jnp.mean(residual * residual, axis=1)
        weighted = (contrast_rows * residual).astype(jnp.bfloat16)
        gradient = gradient + lax.dot_general(
            selector, weighted, (((0,), (0,)), ((), ())), preferred_element_type=jnp.float32
        )
        return (gradient, misfit_rows)

    start_grad = jnp.zeros((rotation_count, image_rows.shape[1]), jnp.float32)
    gradient, misfit_blocks = lax.scan(
        advance, start_grad, jnp.arange(block_count, dtype=jnp.int32)
    )
    return (gradient, misfit_blocks.reshape(row_total))


def build_slots(
    images, defocus, rotations, class_rows, class_rank, rank_first, slot_width, count_cls
):
    particle_ids = jnp.arange(images.shape[0], dtype=jnp.int32)
    inside = (class_rank >= rank_first) & (class_rank < rank_first + slot_width)
    slot_of = jnp.where(inside, class_rows * slot_width + class_rank - rank_first, -1)
    slot_ids = jnp.arange(count_cls * slot_width, dtype=jnp.int32)
    slot_match = slot_ids[:, None] == slot_of[None, :]
    slot_live = jnp.any(slot_match, axis=1)
    slot_source = jnp.sum(jnp.where(slot_match, particle_ids[None, :], 0), axis=1)
    send_images = jnp.where(
        slot_live[:, None], jnp.take(images, slot_source, axis=0), jnp.zeros((), jnp.bfloat16)
    )
    send_rotation = jnp.where(slot_live, jnp.take(rotations, slot_source), -1)
    send_defocus = jnp.where(
        slot_live, jnp.take(defocus, slot_source).astype(jnp.float32), 0.0
    ).astype(jnp.bfloat16)
    return (send_images, send_rotation, send_defocus)


def shards(images, defocus, classes, rotations, references):
    count_cls = lax.axis_size("cls")
    count_dp = lax.axis_size("dp")
    particle_count = images.shape[0]
    pixel_count = images.shape[1]
    rotation_count = references.shape[1]
    capacity = max(2, 2 * particle_count // count_cls)
    slot_count = count_cls * capacity
    radius = wave_table(SIDE)
    class_rows = classes[:, 0]
    particle_ids = jnp.arange(particle_count, dtype=jnp.int32)
    earlier_same = (class_rows[:, None] == class_rows[None, :]) & (
        particle_ids[None, :] < particle_ids[:, None]
    )
    class_rank = jnp.sum(earlier_same.astype(jnp.int32), axis=1)
    slot_of = class_rows * capacity + class_rank
    slot_ids = jnp.arange(slot_count, dtype=jnp.int32)
    slot_match = slot_ids[:, None] == slot_of[None, :]
    send_images, send_rotation, send_defocus = build_slots(
        images, defocus, rotations, class_rows, class_rank, 0, capacity, count_cls
    )
    recv_images, recv_rotation, recv_defocus = (
        lax.all_to_all(
            send_images.reshape(count_cls, capacity, pixel_count),
            "cls",
            split_axis=0,
            concat_axis=0,
            tiled=True,
        ),
        lax.all_to_all(
            send_rotation.astype(jnp.bfloat16).reshape(count_cls, capacity),
            "cls",
            split_axis=0,
            concat_axis=0,
            tiled=True,
        ),
        lax.all_to_all(
            send_defocus.reshape(count_cls, capacity),
            "cls",
            split_axis=0,
            concat_axis=0,
            tiled=True,
        ),
    )
    image_slots = recv_images.reshape(slot_count, pixel_count)
    rotation_slots = recv_rotation.reshape(slot_count).astype(jnp.int32)
    defocus_slots = recv_defocus.reshape(slot_count)
    labels = jnp.arange(rotation_count, dtype=jnp.int32)
    local_counts = jnp.sum((rotation_slots[:, None] == labels[None, :]).astype(jnp.float32), axis=0)
    counts = lax.psum(local_counts, "dp")
    damping = 0.5 * counts + 1.0
    table = references[0]
    grad_first, unused_first = sweep_rows(table, image_slots, rotation_slots, defocus_slots, radius)
    share_rows = rotation_count // count_dp
    share_start = lax.axis_index("dp") * share_rows
    damping_share = lax.dynamic_slice_in_dim(damping, share_start, share_rows, 0)
    grad_share = lax.psum_scatter(
        grad_first.astype(jnp.bfloat16), "dp", scatter_dimension=0, tiled=True
    ).astype(jnp.float32)
    anchor = lax.dynamic_slice_in_dim(table, share_start, share_rows, 0).astype(jnp.float32)
    fresh_share = (anchor - grad_share / damping_share[:, None]).astype(jnp.bfloat16)
    table_next = lax.all_gather(fresh_share, "dp", axis=0, tiled=True)
    grad_second, misfit_slots = sweep_rows(
        table_next, image_slots, rotation_slots, defocus_slots, radius
    )
    second_share = lax.psum_scatter(
        grad_second.astype(jnp.bfloat16), "dp", scatter_dimension=0, tiled=True
    ).astype(jnp.float32)
    anchor_next = lax.dynamic_slice_in_dim(table_next, share_start, share_rows, 0).astype(
        jnp.float32
    )
    refined = (anchor_next - second_share / damping_share[:, None]).astype(jnp.bfloat16)
    returned = lax.all_to_all(
        misfit_slots.reshape(count_cls, capacity), "cls", split_axis=0, concat_axis=0, tiled=True
    )
    returned_slots = returned.reshape(slot_count)
    misfit = jnp.sum(jnp.where(slot_match, returned_slots[:, None], 0.0), axis=0)
    return (refined.reshape(1, share_rows, pixel_count), misfit)


def radius_tables(side_count):
    half_side = side_count // 2
    freq = (np.arange(side_count) + half_side) % side_count - half_side
    square = (freq[:, None] ** 2 + freq[None, :] ** 2).reshape(-1)
    values, place = np.unique(square, return_inverse=True)
    width = -(-(len(values) + 1) // LANES) * LANES
    rows = np.zeros((8, width), np.float32)
    rows[0, : len(values)] = values.astype(np.float32) / np.float32(half_side * half_side)
    rows[1, : len(values)] = -np.exp(-0.5 * rows[0, : len(values)])
    rows[0] = (rows[0].astype(np.float64) * (10.0 / np.pi)).astype(np.float32)
    rows[2, width - 1] = 1.0
    return rows, place.reshape(1, -1).astype(np.float32)


def sine_of_turns(turns):
    rest = turns - jnp.floor(turns + 0.5)
    square = rest * rest
    poly = np.float32(SINE[-1])
    for term in SINE[-2::-1]:
        poly = poly * square + np.float32(term)
    return rest * poly


def refine_kernel(
    sizes,
    images,
    class_in,
    rotation_in,
    defocus_in,
    tables,
    references,
    refined,
    misfit,
    img,
    meta,
    metas,
    crad,
    sq,
    con,
    pick,
    hot,
    hot_t,
    b_own,
    b_send,
    y_got,
    z_own,
    z_send,
    z_got,
    table,
    s_own,
    s_send,
    sy_got,
    sz_own,
    sz_send,
    sz_got,
    s_sum,
    anchor,
    acc,
    mis,
    mis_got,
    send,
    recv,
    send_small,
    recv_small,
    local,
):
    chunks, width, share, side_y, side_z = sizes
    cls = lax.axis_index("cls")
    dp = lax.axis_index("dp")
    z = cls // side_y
    y = cls % side_y
    radii = crad.shape[2]
    half = side_z * share
    cells = side_y * half

    core = dp % 2
    x = dp // 2
    other_core = dp + 1 - 2 * core
    other_x = dp + 2 - 4 * x
    other_y = cls + 1 - 2 * y
    core_mate = (cls, other_core)
    x_mate = (cls, other_x)
    y_mate = (other_y, dp)
    mates = (
        core_mate,
        x_mate,
        (cls, other_x + 1 - 2 * core),
        y_mate,
        (other_y, other_core),
    )
    z_mates = [(((z + k) % side_z) * side_y + y, dp) for k in range(1, side_z)]

    barrier = pltpu.get_barrier_semaphore()
    friends = 1 + 2 * FAMILIES
    everyone = list(mates[:friends]) + z_mates
    if FAMILIES == 1:
        everyone.append(y_mate)
    for other in everyone:
        pl.semaphore_signal(barrier, inc=1, device_id=other, device_id_type=MESH)

    def remote(source, target, kind, index, device):
        return pltpu.make_async_remote_copy(
            src_ref=source,
            dst_ref=target,
            send_sem=send.at[kind, index],
            recv_sem=recv.at[kind, index],
            device_id=device,
            device_id_type=MESH,
        )

    def small(source, target, index, device):
        return pltpu.make_async_remote_copy(
            src_ref=source,
            dst_ref=target,
            send_sem=send_small.at[index],
            recv_sem=recv_small.at[index],
            device_id=device,
            device_id_type=MESH,
        )

    def share_mate(index):
        family = index % FAMILIES
        return (cls + family * (1 - 2 * y), dp + (1 - family) * (2 - 4 * x))

    def sum_mate(index):
        family = index % FAMILIES
        return (cls + (1 - family) * (1 - 2 * y), dp + family * (2 - 4 * x))

    def block_rows(block):
        return pl.ds(block * LANES, LANES)

    def columns(index):
        return pl.ds(pl.multiple_of(index * width, width), width)

    def own_copy(index):
        return pltpu.make_async_copy(
            images.at[:, columns(index)], img.at[index, block_rows(0)], local.at[index]
        )

    def core_copy(index):
        return remote(
            images.at[:, columns(index)], img.at[index, block_rows(1)], 0, index, core_mate
        )

    def share_copy(index):
        return remote(
            images.at[:, columns(index)],
            img.at[index, block_rows(2)],
            1,
            index,
            share_mate(index),
        )

    def forward_copy(index):
        return remote(
            img.at[index, block_rows(2)], img.at[index, block_rows(3)], 2, index, core_mate
        )

    def y_copy(index):
        return remote(b_send.at[index], y_got.at[index], 3, index, sum_mate(index))

    def z_copy(index, k):
        return remote(
            z_send.at[index, k - 1], z_got.at[index, k - 1], 3 + k, index, z_mates[k - 1]
        )

    def table_z_copy(index, k):
        rows = pl.ds((side_z - k) * share, share)
        return remote(
            table.at[index, pl.ds(0, share)],
            table.at[index, rows],
            2 + side_z + k,
            index,
            z_mates[k - 1],
        )

    def table_y_copy(index):
        return remote(
            table.at[index, pl.ds(0, half)],
            table.at[index, pl.ds(half, half)],
            2 + 2 * side_z,
            index,
            sum_mate(index),
        )

    def meta_copy(k):
        return small(meta, metas.at[k], k, mates[k])

    def misfit_copy(k):
        return small(mis.at[k], mis_got.at[k], 5 + k, mates[k])

    s_y_copy = small(s_send, sy_got, 10, y_mate)

    def s_z_copy(k):
        return small(sz_send.at[k - 1], sz_got.at[k - 1], 10 + k, z_mates[k - 1])

    anchor_copy = pltpu.make_async_copy(
        references.at[0, pl.ds(pl.multiple_of(dp * share, share), share)],
        anchor,
        local.at[chunks],
    )
    anchor_copy.start()

    @pl.loop(0, chunks)
    def start_local(index):
        own_copy(index).start()

    meta[0:1] = class_in[...].astype(jnp.float32)
    meta[1:2] = rotation_in[...].astype(jnp.float32)
    meta[2:3] = defocus_in[...].astype(jnp.float32)
    meta[3:8] = jnp.zeros((5, LANES), jnp.float32)
    pl.semaphore_wait(barrier, len(everyone))
    for k in range(friends):
        meta_copy(k).start()
    for index in range(WINDOW):
        share_copy(index).start()
        core_copy(index).start()

    index_rows = lax.broadcasted_iota(jnp.int32, (LANES, LANES), 0).astype(jnp.float32)

    @pl.loop(0, chunks)
    def pick_radii(index):
        row = tables[pl.ds(8 + index, 1), :width]
        for part in range(width // LANES):
            lanes = slice(part * LANES, (part + 1) * LANES)
            target = jnp.broadcast_to(row[:, lanes], (LANES, LANES))
            for block in range(radii // LANES):
                match = index_rows == target - float(block * LANES)
                pick[index, block * LANES : (block + 1) * LANES, lanes] = jnp.where(
                    match, 1.0, 0.0
                ).astype(jnp.bfloat16)

    z_first = z.astype(jnp.float32)
    y_first = y.astype(jnp.float32)
    x_first = x.astype(jnp.float32)
    core_first = core.astype(jnp.float32)
    cell_rows = lax.broadcasted_iota(jnp.int32, (cells, LANES), 0).astype(jnp.float32)
    cell_lanes = lax.broadcasted_iota(jnp.int32, (LANES, cells), 1).astype(jnp.float32)
    owned = {}
    groups = (((0, 0), (1, 0)), ((0, 1), (1, 1)), ((0, 2),), ((0, 3),), ((1, 2),), ((1, 3),))
    for source in range(friends + 1):
        places = [place for place in groups[source] if place[0] < FAMILIES]
        if source > 0:
            meta_copy(source - 1).wait_recv()
            rows = metas[source - 1]
        else:
            rows = meta[...]
        class_z = jnp.floor(rows[0:1] / float(side_y))
        class_y = rows[0:1] - float(side_y) * class_z
        turn_dp = jnp.floor(rows[1:2] / float(share))
        turn_r = rows[1:2] - float(share) * turn_dp
        turn_x = jnp.floor(turn_dp * 0.5)
        rel_z = class_z - z_first
        rel_z = jnp.where(rel_z < 0.0, rel_z + float(side_z), rel_z)
        off_x = jnp.abs(turn_x - x_first)
        off_y = jnp.abs(class_y - y_first)
        off_core = jnp.abs(turn_dp - 2.0 * turn_x - core_first)
        focus = jnp.transpose(jnp.broadcast_to(rows[2:3], (LANES, LANES)))
        for family, block in places:
            off_share, off_sum = (off_x, off_y) if family == 0 else (off_y, off_x)
            mine = (off_share + off_core) < 0.5
            cell = jnp.where(mine, off_sum * float(half) + rel_z * float(share) + turn_r, -1.0)
            owned[family, block] = mine
            span = slice(block * LANES, (block + 1) * LANES)
            hot[family, :, span] = jnp.where(cell_rows == cell, 1.0, 0.0).astype(jnp.bfloat16)
            cell_t = jnp.transpose(jnp.broadcast_to(cell, (LANES, LANES)))
            hot_t[family, span] = jnp.where(cell_lanes == cell_t, 1.0, 0.0).astype(jnp.bfloat16)
        for part in range(radii // LANES):
            lanes = slice(part * LANES, (part + 1) * LANES)
            turns = focus * tables[0:1, lanes] + np.float32(0.1 / (2.0 * np.pi))
            wave = sine_of_turns(turns) * tables[1:2, lanes]
            for family, block in places:
                span = slice(block * LANES, (block + 1) * LANES)
                crad[family, span, lanes] = wave.astype(jnp.bfloat16)
                if family == 0:
                    sq[span, lanes] = (wave * wave + tables[2:3, lanes]).astype(jnp.bfloat16)
    acc[...] = jnp.zeros_like(acc)

    def tick(t, carry):
        @pl.when(t == 4)
        def counts_out():
            s_y_copy.wait_recv()
            total = s_own[...] + sy_got[...].astype(jnp.float32)
            sz_own[...] = total[:share]
            for k in range(1, side_z):
                sz_send[k - 1] = total[k * share : (k + 1) * share].astype(jnp.bfloat16)
                s_z_copy(k).start()

        @pl.when((t >= 4) & (t < chunks + 4))
        def sum_y():
            index = t - 4
            y_copy(index).wait_recv()
            total = b_own[index] + y_got[index].astype(jnp.float32)
            z_own[index] = total[:share]
            for k in range(1, side_z):
                z_send[index, k - 1] = total[k * share : (k + 1) * share].astype(jnp.bfloat16)
                z_copy(index, k).start()

        @pl.when(t == 7)
        def counts_in():
            anchor_copy.wait()
            total = sz_own[...]
            for k in range(1, side_z):
                s_z_copy(k).wait_recv()
                total = total + sz_got[k - 1].astype(jnp.float32)
            s_sum[...] = total

        @pl.when((t >= 7) & (t < chunks + 7))
        def update():
            index = t - 7
            total = z_own[index]
            for k in range(1, side_z):
                z_copy(index, k).wait_recv()
                total = total + z_got[index, k - 1].astype(jnp.float32)
            squares = s_sum[...]
            coarse = squares.astype(jnp.bfloat16)
            fine = (squares - coarse.astype(jnp.float32)).astype(jnp.bfloat16)
            pair = jnp.dot(
                jnp.concatenate([coarse, fine], axis=0),
                pick[index],
                preferred_element_type=jnp.float32,
            )
            energy = pair[:share] + pair[share:]
            damping = 0.5 * squares[:, radii - 1 : radii] + 1.0
            scale = 1.0 / damping
            start = anchor[:, columns(index)].astype(jnp.float32)
            first = (start - (start * energy - total) * scale).astype(jnp.bfloat16)
            table[index, 0:share] = first
            for k in range(1, side_z):
                table_z_copy(index, k).start()
            again = first.astype(jnp.float32)
            refined[:, columns(index)] = (again - (again * energy - total) * scale).astype(
                jnp.bfloat16
            )

        @pl.when((t >= 10) & (t < chunks + 10))
        def spread():
            index = t - 10
            for k in range(1, side_z):
                table_z_copy(index, k).wait_recv()
            table_y_copy(index).start()

        @pl.when(t < chunks)
        def contrasts():
            for block in range(2):
                span = pl.ds(2 * block * LANES, 2 * LANES)
                con[t, span] = jnp.dot(
                    crad[t % FAMILIES, span], pick[t], preferred_element_type=jnp.float32
                ).astype(jnp.bfloat16)

        @pl.when(t >= 13)
        def residuals():
            index = t - 13
            table_y_copy(index).wait_recv()
            for block in range(4):
                span = block_rows(block)
                tiles = jnp.dot(
                    hot_t[index % FAMILIES, span], table[index], preferred_element_type=jnp.float32
                )
                total = acc[index % FAMILIES, span]
                for part in range(width // LANES):
                    lanes = slice(part * LANES, (part + 1) * LANES)
                    rest = con[index, span, lanes].astype(jnp.float32) * tiles[:, lanes]
                    rest = rest - img[index, span, lanes].astype(jnp.float32)
                    total = total + rest * rest
                acc[index % FAMILIES, span] = total

        @pl.when(t < chunks)
        def forward():
            share_copy(t).wait_recv()
            forward_copy(t).start()

        @pl.when(t < chunks - WINDOW)
        def start_images():
            share_copy(t + WINDOW).start()
            core_copy(t + WINDOW).start()

        @pl.when((t >= 1) & (t < chunks + 1))
        def partial_sums():
            index = t - 1
            own_copy(index).wait()
            core_copy(index).wait_recv()
            forward_copy(index).wait_recv()
            total = jnp.dot(
                hot[index % FAMILIES], con[index] * img[index], preferred_element_type=jnp.float32
            )
            b_own[index] = total[:half]
            b_send[index] = total[half:].astype(jnp.bfloat16)
            y_copy(index).start()

        @pl.when(t == 1)
        def counts_start():
            partial = jnp.dot(hot[0], sq[...], preferred_element_type=jnp.float32)
            s_own[...] = partial[:half]
            s_send[...] = partial[half:].astype(jnp.bfloat16)
            s_y_copy.start()

        return carry

    lax.fori_loop(0, chunks + 13, tick, 0)

    def row_of(family, block):
        part = acc[family, block * LANES : (block + 1) * LANES]
        row = jnp.sum(jnp.transpose(part), axis=0, keepdims=True)
        return jnp.where(owned[family, block], row * (1.0 / float(chunks * width)), 0.0)

    rows_out = [row_of(0, 1), row_of(0, 2), row_of(0, 3)]
    if FAMILIES == 2:
        rows_out[0] = rows_out[0] + row_of(1, 1)
        rows_out = rows_out + [row_of(1, 2), row_of(1, 3)]
    for k, row in enumerate(rows_out):
        mis[k] = jnp.broadcast_to(row, mis.shape[1:])
        misfit_copy(k).start()

    @pl.loop(0, chunks)
    def drain(index):
        core_copy(index).wait_send()
        share_copy(index).wait_send()
        forward_copy(index).wait_send()
        y_copy(index).wait_send()
        for k in range(1, side_z):
            z_copy(index, k).wait_send()
            table_z_copy(index, k).wait_send()
        table_y_copy(index).wait_send()

    s_y_copy.wait_send()
    for k in range(1, side_z):
        s_z_copy(k).wait_send()
    total = row_of(0, 0)
    if FAMILIES == 2:
        total = total + row_of(1, 0)
    for k in range(friends):
        meta_copy(k).wait_send()
        misfit_copy(k).wait()
        total = total + mis_got[k, 0:1]
    misfit[...] = total


def shards_close(side_y, side_z, images, defocus, classes, rotations, references):
    count_dp = lax.axis_size("dp")
    rows, pixels = images.shape
    share = references.shape[1] // count_dp
    chunks = CHUNKS
    width = pixels // chunks
    half = side_z * share
    cells = side_y * half
    tables, place = radius_tables(SIDE)
    radii = tables.shape[1]
    constants = np.zeros((8 + chunks, max(radii, width)), np.float32)
    constants[:8, :radii] = tables
    constants[8:, :width] = place.reshape(chunks, width)
    bf16, f32 = jnp.bfloat16, jnp.float32
    kinds = 3 + 2 * side_z
    vmem = pl.BlockSpec(memory_space=pltpu.VMEM)
    anywhere = pl.BlockSpec(memory_space=pltpu.HBM)
    refined, misfit = pl.pallas_call(
        functools.partial(refine_kernel, (chunks, width, share, side_y, side_z)),
        out_shape=(
            jax.ShapeDtypeStruct((share, pixels), bf16),
            jax.ShapeDtypeStruct((1, rows), f32),
        ),
        in_specs=[anywhere, vmem, vmem, vmem, vmem, anywhere],
        out_specs=(vmem, vmem),
        scratch_shapes=[
            pltpu.VMEM((chunks, 4 * rows, width), bf16),
            pltpu.VMEM((8, rows), f32),
            pltpu.VMEM((1 + 2 * FAMILIES, 8, rows), f32),
            pltpu.VMEM((FAMILIES, 4 * rows, radii), bf16),
            pltpu.VMEM((4 * rows, radii), bf16),
            pltpu.VMEM((chunks, 4 * rows, width), bf16),
            pltpu.VMEM((chunks, radii, width), bf16),
            pltpu.VMEM((FAMILIES, cells, 4 * rows), bf16),
            pltpu.VMEM((FAMILIES, 4 * rows, cells), bf16),
            pltpu.VMEM((chunks, half, width), f32),
            pltpu.VMEM((chunks, half, width), bf16),
            pltpu.VMEM((chunks, half, width), bf16),
            pltpu.VMEM((chunks, share, width), f32),
            pltpu.VMEM((chunks, side_z - 1, share, width), bf16),
            pltpu.VMEM((chunks, side_z - 1, share, width), bf16),
            pltpu.VMEM((chunks, cells, width), bf16),
            pltpu.VMEM((half, radii), f32),
            pltpu.VMEM((half, radii), bf16),
            pltpu.VMEM((half, radii), bf16),
            pltpu.VMEM((share, radii), f32),
            pltpu.VMEM((side_z - 1, share, radii), bf16),
            pltpu.VMEM((side_z - 1, share, radii), bf16),
            pltpu.VMEM((share, radii), f32),
            pltpu.VMEM((share, pixels), bf16),
            pltpu.VMEM((FAMILIES, 4 * rows, LANES), f32),
            pltpu.VMEM((1 + 2 * FAMILIES, 8, rows), f32),
            pltpu.VMEM((1 + 2 * FAMILIES, 8, rows), f32),
            pltpu.SemaphoreType.DMA((kinds, chunks)),
            pltpu.SemaphoreType.DMA((kinds, chunks)),
            pltpu.SemaphoreType.DMA((10 + side_z,)),
            pltpu.SemaphoreType.DMA((10 + side_z,)),
            pltpu.SemaphoreType.DMA((chunks + 1,)),
        ],
        compiler_params=pltpu.CompilerParams(
            collective_id=0, has_side_effects=True, vmem_limit_bytes=63 * 1024 * 1024
        ),
    )(
        images,
        classes.reshape(1, rows),
        rotations.reshape(1, rows),
        defocus.reshape(1, rows),
        jnp.asarray(constants),
        references,
    )
    return refined.reshape(1, share, pixels), misfit.reshape(rows)


def solution(mesh):
    in_specs = (
        P(("cls", "dp"), None),
        P(("cls", "dp")),
        P(("cls", "dp"), None),
        P(("cls", "dp")),
        P("cls", None, None),
    )
    out_specs = (P("cls", "dp", None), P(("cls", "dp")))
    per_device = shards
    if mesh.shape["cls"] == 8 and mesh.shape["dp"] == 4:
        per_device = functools.partial(shards_close, 2, 4)
    return jax.shard_map(
        per_device, mesh=mesh, in_specs=in_specs, out_specs=out_specs, check_vma=False
    )
```
